32 devices in a mesh: section: 2 (over x), tensor: 2 (over y), batch: 8 (over z, core).
Axes of the slice: x: 2, y: 2, z: 4, core: 2. Of those that a mesh axis runs over, the one named last changes fastest.
Arguments:
- tokens: bfloat16 [2, 8, 512, 768], P(None, 'batch', 'tensor'), may hold values from -6 to 6
- block_place: int32 [2, 8], P(None, 'batch'), may hold values from 0 to 3, as said below
- cotangent: bfloat16 [2, 8, 512, 768], P(None, 'batch', 'tensor'), may hold values from -6 to 6
- norm_gains: float32 [2, 2, 768], P('section'), may hold values from 0.5 to 1.5
- norm_biases: float32 [2, 2, 768], P('section'), may hold values from -1.2 to 1.2
- query_key: bfloat16 [2, 768, 2, 768], P('section', None, None, 'tensor'), may hold values from -0.21875 to 0.21875
- query_bias: float32 [2, 768], P('section', 'tensor'), may hold values from -1.8 to 1.8
- value_own: bfloat16 [2, 768, 384], P('section', None, 'tensor'), may hold values from -0.21875 to 0.21875
- value_bias: float32 [2, 384], P('section', 'tensor'), may hold values from -0.3 to 0.3
- value_extra: bfloat16 [768, 384], P(None, 'tensor'), may hold values from -0.21875 to 0.21875
- out_weight: bfloat16 [2, 768, 768], P('section', 'tensor'), may hold values from -1.75 to 1.75
- out_bias: float32 [2, 768], P('section'), may hold values from -1.8 to 1.8
- up_weight: bfloat16 [2, 768, 3072], P('section', None, 'tensor'), may hold values from -0.21875 to 0.21875
- up_bias: float32 [2, 3072], P('section', 'tensor'), may hold values from -1.8 to 1.8
- down_weight: bfloat16 [2, 3072, 768], P('section', 'tensor'), may hold values from -0.109375 to 0.109375
- down_bias: float32 [2, 768], P('section'), may hold values from -1.8 to 1.8
Outputs:
- layer_outputs: bfloat16 [2, 2, 8, 512, 768], P('section', None, 'batch', 'tensor')
- input_grads: float32 [2, 2, 8, 512, 768], P('section', None, 'batch', 'tensor')
- norm_gains_grad: float32 [2, 2, 768], P('section')
- norm_biases_grad: float32 [2, 2, 768], P('section')
- query_key_grad: float32 [2, 768, 2, 768], P('section', None, None, 'tensor')
- query_bias_grad: float32 [2, 768], P('section', 'tensor')
- value_own_grad: float32 [2, 768, 384], P('section', None, 'tensor')
- value_bias_grad: float32 [2, 384], P('section', 'tensor')
- value_extra_grad: float32 [768, 384], P('section', 'tensor')
- out_weight_grad: float32 [2, 768, 768], P('section', 'tensor')
- out_bias_grad: float32 [2, 768], P('section')
- up_weight_grad: float32 [2, 768, 3072], P('section', None, 'tensor')
- up_bias_grad: float32 [2, 3072], P('section', 'tensor')
- down_weight_grad: float32 [2, 3072, 768], P('section', 'tensor')
- down_bias_grad: float32 [2, 768], P('section')
The draws below stay inside these ranges and needn't reach their ends.
Inputs may be any that keep to these rules, and one draw needn't show every extreme that they name: `block_place`: in each micro-batch, sequences of 2 or 4 blocks lie one after another along the 8 blocks: block 0 has value 0, and a block with value p > 0 continues the sequence of the block before it, whose value is p - 1. A third of each micro-batch's sequences hold 4 blocks, the others 2.
All inputs are finite; a program needn't handle non-finite values.
Results may differ from the reference program's by a relative error of at most 0.028.
Values may be sent and summed in bfloat16 or wider, within the bound.
No kernel may reach another device: no remote copies, remote signals or barrier semaphores. Data moves between devices by JAX's collectives and lax.ppermute only.
A program may use at most 256 MiB of HBM per device.

```python
import jax
import jax.numpy as jnp
from jax import lax

D = 768
HEADS = 12
HEAD = 64
FF = 3072
GROUP = 6
BLOCK = 512
MICRO = 2
BLOCKS = 8


def draw_block_place(key, part):
    key = jax.random.fold_in(key, 11)
    long_count = BLOCKS // 8
    short_count = (BLOCKS - 4 * long_count) // 2
    lengths = jnp.concatenate([jnp.full((long_count,), 4, jnp.int32), jnp.full((short_count,), 2, jnp.int32)])

    def one_micro(subkey):
        ordering = jax.random.permutation(subkey, long_count + short_count)
        spans = lengths[ordering]
        starts = (jnp.cumsum(spans) - spans).astype(jnp.int32)
        owners = jnp.repeat(starts, spans, total_repeat_length=BLOCKS)
        return (jnp.arange(BLOCKS, dtype=jnp.int32) - owners).astype(jnp.int32)
    return jax.vmap(one_micro)(jax.random.split(key, MICRO))


def steps_of(rng, extent, cuts, smallest, largest):
    gain = 1.0
    for axis_at, blocks in cuts:
        steps = jax.random.uniform(jax.random.fold_in(jax.random.fold_in(rng, 6), axis_at), (blocks,), jnp.float32, smallest / len(cuts), largest / len(cuts))
        gain = gain * jnp.repeat(jnp.exp(steps), extent[axis_at] // blocks).reshape((-1,) + (1,) * (len(extent) - 1 - axis_at))
    return gain


def scatter_about(own_key, dims, width, limit, shards=(), kind=jnp.bfloat16):
    factor_of = steps_of(own_key, dims, shards, -0.22, 0.18) if shards else 1.0
    drawn = jax.random.normal(own_key, dims, jnp.float32) * width * factor_of
    return jnp.minimum(jnp.maximum(drawn, -limit), limit).astype(kind)


def setup_inputs(seed: int = 0) -> dict:
    seeds = jax.random.split(jax.random.key(seed), 17)
    return {
        "tokens": scatter_about(seeds[0], (MICRO, BLOCKS, BLOCK, D), 1.0, 6.0, ((1, 8), (2, 2))),
        "block_place": draw_block_place(jax.random.fold_in(seeds[16], 71), 0),
        "cotangent": scatter_about(seeds[2], (MICRO, BLOCKS, BLOCK, D), 1.0, 6.0, ((1, 8), (2, 2))),
        "norm_gains": jnp.clip(1.0 + 0.1 * jax.random.normal(seeds[3], (2, 2, D), jnp.float32), 0.5, 1.5),
        "norm_biases": scatter_about(seeds[4], (2, 2, D), 0.2, 1.2, ((0, 2),), jnp.float32),
        "query_key": scatter_about(seeds[5], (2, D, 2, D), D ** -0.5, 0.21875, ((0, 2), (3, 2))),
        "query_bias": scatter_about(seeds[6], (2, D), 0.3, 1.8, ((0, 2), (1, 2)), jnp.float32),
        "value_own": scatter_about(seeds[7], (2, D, D // 2), D ** -0.5, 0.21875, ((0, 2), (2, 2))),
        "value_bias": scatter_about(seeds[8], (2, D // 2), 0.05, 0.3, ((0, 2), (1, 2)), jnp.float32),
        "value_extra": scatter_about(seeds[9], (D, D // 2), D ** -0.5, 0.21875, ((1, 2),)),
        "out_weight": scatter_about(seeds[10], (2, D, D), (D // 64) ** -0.5, 1.75, ((0, 2), (1, 2))),
        "out_bias": scatter_about(seeds[11], (2, D), 0.3, 1.8, ((0, 2),), jnp.float32),
        "up_weight": scatter_about(seeds[12], (2, D, FF), D ** -0.5, 0.21875, ((0, 2), (2, 2))),
        "up_bias": scatter_about(seeds[13], (2, FF), 0.3, 1.8, ((0, 2), (1, 2)), jnp.float32),
        "down_weight": scatter_about(seeds[14], (2, FF, D), FF ** -0.5, 0.109375, ((0, 2), (1, 2))),
        "down_bias": scatter_about(seeds[15], (2, D), 0.3, 1.8, ((0, 2),), jnp.float32),
    }


@jax.custom_vjp
def low(v):
    return lax.optimization_barrier(v.astype(jnp.bfloat16)).astype(jnp.float32)

@jax.custom_vjp
def low_back(v):
    return v

def low_keep(v):
    return (low(v), None)

def low_pass(kept, grad):
    return (grad,)

def back_keep(v):
    return (v, None)

def back_low(kept, grad):
    return (low(grad),)
low.defvjp(low_keep, low_pass)
low_back.defvjp(back_keep, back_low)
HIGHEST = lax.Precision.HIGHEST

def matrix_product(left_side, right_side):
    return jnp.dot(left_side, right_side, precision=HIGHEST)

def round_both(values):
    return low_back(low(values))

def norm_rows(values, scales, shifts):
    centred = values - lax.optimization_barrier(jnp.mean(values, axis=-1, keepdims=True))
    spread = lax.optimization_barrier(jnp.mean(centred * centred, axis=-1, keepdims=True))
    return centred * lax.rsqrt(spread + 1e-05) * scales + shifts

def value_heads(first_part, second_part, row_count):
    groups = HEADS // GROUP
    half_group = GROUP // 2
    first_part = first_part.reshape(row_count, groups, half_group, HEAD)
    second_part = second_part.reshape(row_count, groups, half_group, HEAD)
    return jnp.concatenate([first_part, second_part], axis=2).reshape(row_count, HEADS * HEAD)

def attend_all(queries, key_matrix, values, places):
    factor = HEAD ** (-0.5)
    padding = jnp.zeros((3, BLOCK, HEADS, HEAD), jnp.float32)
    padded_keys = jnp.concatenate([padding, key_matrix], axis=0)
    padded_values = jnp.concatenate([padding, values], axis=0)
    row_index = lax.broadcasted_iota(jnp.int32, (BLOCK, 4 * BLOCK), 0)
    column_index = lax.broadcasted_iota(jnp.int32, (BLOCK, 4 * BLOCK), 1)
    offset = 3 - column_index // BLOCK

    def one_block(position):
        window_keys = lax.dynamic_slice_in_dim(padded_keys, position, 4, 0).reshape(4 * BLOCK, HEADS, HEAD)
        window_values = lax.dynamic_slice_in_dim(padded_values, position, 4, 0).reshape(4 * BLOCK, HEADS, HEAD)
        scores = low_back(jnp.einsum('qhd,khd->hqk', queries[position], window_keys, precision=HIGHEST) * factor)
        allowed = (offset <= places[position]) & ((offset > 0) | (column_index % BLOCK <= row_index))
        scores = jnp.where(allowed[None], scores, -1e+30)
        row_top = lax.optimization_barrier(jnp.max(scores, axis=-1, keepdims=True))
        weights = jnp.exp(scores - row_top)
        attention = low(weights / lax.optimization_barrier(jnp.sum(weights, axis=-1, keepdims=True)))
        return jnp.einsum('hqk,khd->qhd', attention, window_values, precision=HIGHEST)
    return lax.map(jax.checkpoint(one_block), jnp.arange(BLOCKS, dtype=jnp.int32))

def layer(inputs, places, shared, params, layer_index):
    norm_gains, norm_biases, query_key, query_bias, value_own, value_bias, value_extra, out_weight, out_bias, up_weight, up_bias, down_weight, down_bias = params
    row_count = BLOCKS * BLOCK
    normed = low(norm_rows(inputs, norm_gains[layer_index, 0], norm_biases[layer_index, 0])).reshape(row_count, D)
    queries = round_both(matrix_product(normed, query_key[layer_index, :, 0]) + query_bias[layer_index])
    key_matrix = round_both(matrix_product(normed, query_key[layer_index, :, 1]))
    own_values = round_both(matrix_product(normed, value_own[layer_index]) + value_bias[layer_index])
    if shared is None:
        other_values = round_both(matrix_product(normed, value_extra))
    else:
        other_values = shared
    values = value_heads(own_values, other_values, row_count)
    layout = (BLOCKS, BLOCK, HEADS, HEAD)
    attended = round_both(attend_all(queries.reshape(layout), key_matrix.reshape(layout), values.reshape(layout), places))
    branch = low_back(matrix_product(attended.reshape(row_count, D), out_weight[layer_index]))
    hidden = inputs + branch.reshape(BLOCKS, BLOCK, D) + out_bias[layer_index]

    def one_block(block_rows):
        mlp_in = low(norm_rows(block_rows, norm_gains[layer_index, 1], norm_biases[layer_index, 1]))
        up_values = low_back(matrix_product(mlp_in, up_weight[layer_index]) + up_bias[layer_index])
        active = low(jax.nn.gelu(up_values, approximate=True))
        down_branch = low_back(matrix_product(active, down_weight[layer_index]))
        return block_rows + down_branch + down_bias[layer_index]
    return (lax.map(jax.checkpoint(one_block), hidden), own_values)

def reference(tokens, block_place, cotangent, norm_gains, norm_biases, query_key, query_bias, value_own, value_bias, value_extra, out_weight, out_bias, up_weight, up_bias, down_weight, down_bias):
    weights_in = tuple((weight.astype(jnp.float32) for weight in (norm_gains, norm_biases, query_key, query_bias, value_own, value_bias, value_extra, out_weight, out_bias, up_weight, up_bias, down_weight, down_bias)))
    tokens_wide = tokens.astype(jnp.float32)
    probe_zero = jnp.zeros(tokens.shape, jnp.float32)

    def forward(tokens_in, probe_in, *params):

        def one_micro(carried, inputs):
            block_tokens, block_probe, places = inputs
            first_out, shared = layer(block_tokens, places, None, params, 0)
            first_out = round_both(first_out) + block_probe
            second_out, ignored = layer(first_out, places, shared, params, 1)
            return (carried, (first_out, second_out))
        ignored, outputs = lax.scan(jax.checkpoint(one_micro), jnp.zeros((), jnp.float32), (tokens_in, probe_in, block_place))
        return outputs
    outputs, pullback = jax.vjp(forward, tokens_wide, probe_zero, *weights_in)
    gradients = pullback((jnp.zeros(tokens.shape, jnp.float32), cotangent.astype(jnp.float32)))
    layer_outputs = jnp.stack([outputs[0], outputs[1]]).astype(jnp.bfloat16)
    input_grads = jnp.stack([gradients[0], gradients[1]])
    return (layer_outputs, input_grads, gradients[2], gradients[3], gradients[4], gradients[5], gradients[6], gradients[7], gradients[8], gradients[9], gradients[10], gradients[11], gradients[12], gradients[13], gradients[14])
```

```python
import jax
import jax.numpy as jnp
from jax import lax
from jax.experimental import pallas as pl
from jax.experimental.pallas import tpu as pltpu
from jax.sharding import PartitionSpec as P

F32 = jnp.float32
BF = jnp.bfloat16
NEG=-1e30
def dot_nt(a,b): return lax.dot_general(a,b,(((1,),(1,)),((),())),preferred_element_type=F32)
def dot_nn(a,b): return lax.dot_general(a,b,(((1,),(0,)),((),())),preferred_element_type=F32)
def dot_tn(a,b): return lax.dot_general(a,b,(((0,),(0,)),((),())),preferred_element_type=F32)

def lane_low(shape):
    return lax.broadcasted_iota(jnp.int32, shape, 1) < 64

def head_of(pair, sub, fill):
    low = lane_low(pair.shape)
    keep = low if sub==0 else ~low
    return jnp.where(keep, pair, jnp.full_like(pair, fill))

def fwd_local_kernel(flag_ref, q_ref, k_ref, v_ref, pk_ref, pv_ref, o_ref, l_ref, m_ref):
    pairs = q_ref.shape[1]//128
    n = q_ref.shape[0]; half = n//2
    def run(with_partner):
        for c in range(2):
            rows = pl.ds(c*half, half)
            nk = (c+1)*half
            row = lax.broadcasted_iota(jnp.int32,(half,nk),0)+c*half
            col = lax.broadcasted_iota(jnp.int32,(half,nk),1)
            ok = col<=row
            for p in range(pairs):
                ls = slice(p*128,(p+1)*128)
                qp = q_ref[rows, ls]
                kp = k_ref[0:nk, ls]; vp = v_ref[0:nk, ls]
                outs=[]
                for sub in range(2):
                    s = dot_nt(qp, head_of(kp, sub, 0))
                    s = jnp.where(ok, s, NEG)
                    m = jnp.max(s,axis=1,keepdims=True)
                    if with_partner:
                        s2 = dot_nt(qp, head_of(pk_ref[:, ls], sub, 0))
                        m = jnp.maximum(m, jnp.max(s2,axis=1,keepdims=True))
                    e = jnp.exp(s-m).astype(BF)
                    o = dot_nn(e, head_of(vp, sub, 1))
                    if with_partner:
                        e2 = jnp.exp(s2-m).astype(BF)
                        o = o + dot_nn(e2, head_of(pv_ref[:, ls], sub, 1))
                    outs.append(o)
                    m_ref[rows, 2*p+sub:2*p+sub+1] = m
                low = lane_low(outs[0].shape)
                o_ref[rows, ls] = jnp.where(low, outs[0], outs[1])
                l_ref[rows, ls] = pltpu.roll(jnp.where(low, outs[1], outs[0]), 64, 1)
    @pl.when(flag_ref[0]==1)
    def _(): run(True)
    @pl.when(flag_ref[0]==0)
    def _(): run(False)

def fwd_cross_kernel(flag_ref, q_ref, k_ref, v_ref, o_ref, l_ref, m_ref, out_ref, lse_ref, scr):
    pairs = q_ref.shape[1]//128
    n = q_ref.shape[0]; half=n//2
    @pl.when(flag_ref[1]==0)
    def _():
        out_ref[...] = (o_ref[...]/l_ref[...]).astype(BF)
        for p in range(pairs):
            for sub in range(2):
                h=2*p+sub
                scr[:,h:h+1] = m_ref[:,h:h+1] + jnp.log(l_ref[:,h*64:h*64+1])
    @pl.when(flag_ref[1]==1)
    def _():
        for c in range(2):
            rows = pl.ds(c*half, half)
            for p in range(pairs):
                ls = slice(p*128,(p+1)*128)
                qp = q_ref[rows, ls]
                outs=[]; als=[]; ms=[]
                for sub in range(2):
                    h=2*p+sub
                    s = dot_nt(qp, head_of(k_ref[:, ls], sub, 0))
                    m0 = m_ref[rows,h:h+1]
                    m = jnp.maximum(m0, jnp.max(s,axis=1,keepdims=True))
                    e = jnp.exp(s-m).astype(BF)
                    outs.append(dot_nn(e, head_of(v_ref[:, ls], sub, 1)))
                    als.append(jnp.exp(m0-m)); ms.append(m)
                low = lane_low(outs[0].shape)
                al = jnp.where(low, als[0], als[1])
                o = o_ref[rows, ls]*al + jnp.where(low, outs[0], outs[1])
                l = l_ref[rows, ls]*al + pltpu.roll(jnp.where(low, outs[1], outs[0]), 64, 1)
                out_ref[rows, ls] = (o/l).astype(BF)
                lg = jnp.log(l)
                scr[rows, 2*p:2*p+1] = ms[0] + lg[:,0:1]
                scr[rows, 2*p+1:2*p+2] = ms[1] + lg[:,64:65]
    lse_ref[...] = jnp.transpose(scr[...])[0:8,:]

VM = pl.BlockSpec(memory_space=pltpu.VMEM)
SM = pl.BlockSpec(memory_space=pltpu.SMEM)
PAR = pltpu.CompilerParams(vmem_limit_bytes=48*1024*1024)
def S(shape,d): return jax.ShapeDtypeStruct(shape,d)
def attend_local(flags,q,k,v,pk,pv):
    n,w=q.shape
    return pl.pallas_call(fwd_local_kernel,out_shape=[S((n,w),F32),S((n,w),F32),S((n,128),F32)],in_specs=[SM]+[VM]*5,out_specs=[VM]*3,compiler_params=PAR)(flags,q,k,v,pk,pv)
def attend_cross(flags,q,k,v,o,l,m):
    n,w=q.shape
    return pl.pallas_call(fwd_cross_kernel,out_shape=[S((n,w),BF),S((8,n),F32)],in_specs=[SM]+[VM]*6,out_specs=[VM]*2,scratch_shapes=[pltpu.VMEM((n,128),F32)],compiler_params=PAR)(flags,q,k,v,o,l,m)

def bwd_tile(qp, kh, vh, dop, lse_row, del_row, ok):
    st = dot_nt(kh, qp)
    pt = jnp.exp(st - lse_row)
    if ok is not None: pt = jnp.where(ok, pt, 0.0)
    dpt = dot_nt(vh, dop)
    dst = (pt*(dpt-del_row)).astype(BF)
    return pt.astype(BF), dst

def deltas(do_ref, at_ref, scr, del_ref):
    pairs = do_ref.shape[1]//128
    for p in range(pairs):
        ls = slice(p*128,(p+1)*128)
        pr = do_ref[:,ls].astype(F32)*at_ref[:,ls].astype(F32)
        low = lane_low(pr.shape)
        scr[:,2*p:2*p+1] = jnp.sum(jnp.where(low,pr,0.0),axis=1,keepdims=True)
        scr[:,2*p+1:2*p+2] = jnp.sum(jnp.where(low,0.0,pr),axis=1,keepdims=True)
    del_ref[...] = jnp.transpose(scr[...])[0:8,:]

def bwd_cross_kernel(flag_ref, q_ref, do_ref, at_ref, lse_ref, k_ref, v_ref, dq_ref, dk_ref, dv_ref, del_ref, scr):
    deltas(do_ref, at_ref, scr, del_ref)
    pairs = q_ref.shape[1]//128
    nk = k_ref.shape[0]; kc=256
    @pl.when(flag_ref[1]==0)
    def _():
        dq_ref[...]=jnp.zeros_like(dq_ref); dk_ref[...]=jnp.zeros_like(dk_ref); dv_ref[...]=jnp.zeros_like(dv_ref)
    @pl.when(flag_ref[1]==1)
    def _():
        for p in range(pairs):
            ls = slice(p*128,(p+1)*128)
            qp=q_ref[:,ls]; dop=do_ref[:,ls]
            dqs=[None,None]
            low = lane_low((kc,128))
            for j in range(nk//kc):
                ks=pl.ds(j*kc,kc)
                kp=k_ref[ks,ls]; vp=v_ref[ks,ls]
                r=[]
                for sub in range(2):
                    h=2*p+sub
                    kh=head_of(kp,sub,0); vh=head_of(vp,sub,0)
                    pt,dst=bwd_tile(qp,kh,vh,dop,lse_ref[h:h+1,:],del_ref[h:h+1,:],None)
                    r.append((dot_nn(pt,dop), dot_nn(dst,qp)))
                    d=dot_tn(dst,kh)
                    dqs[sub]= d if dqs[sub] is None else dqs[sub]+d
                dv_ref[ks,ls]=jnp.where(low,r[0][0],r[1][0]).astype(BF)
                dk_ref[ks,ls]=jnp.where(low,r[0][1],r[1][1]).astype(BF)
            dq_ref[:,ls]=dqs[0]+dqs[1]

def bwd_local_kernel(flag_ref, q_ref, do_ref, lse_ref, del_ref, k_ref, v_ref, pk_ref, pv_ref, dqc_ref, dq_ref, dk_ref, dv_ref, dpk_ref, dpv_ref):
    pairs = q_ref.shape[1]//128
    n=q_ref.shape[0]; half=n//2; kc=half
    def tile_pair(p, ks, kr, vr, qoff, ok):
        ls = slice(p*128,(p+1)*128)
        qp=q_ref[qoff:,ls]; dop=do_ref[qoff:,ls]
        kp=kr[ks,ls]; vp=vr[ks,ls]
        low = lane_low((kc,128)); r=[]; dq=None
        for sub in range(2):
            h=2*p+sub
            kh=head_of(kp,sub,0); vh=head_of(vp,sub,0)
            pt,dst=bwd_tile(qp,kh,vh,dop,lse_ref[h:h+1,qoff:],del_ref[h:h+1,qoff:],ok)
            r.append((dot_nn(pt,dop), dot_nn(dst,qp)))
            d=dot_tn(dst,kh)
            dq = d if dq is None else dq+d
        return dq, jnp.where(low,r[0][1],r[1][1]), jnp.where(low,r[0][0],r[1][0])
    def mask(j):
        key=lax.broadcasted_iota(jnp.int32,(kc,n-j*kc),0); qq=lax.broadcasted_iota(jnp.int32,(kc,n-j*kc),1)
        return key<=qq
    for p in range(pairs):
        ls = slice(p*128,(p+1)*128)
        for j in range(2):
            ks=pl.ds(j*kc,kc)
            dq,dk,dv=tile_pair(p,ks,k_ref,v_ref,j*kc,mask(j))
            dk_ref[ks,ls]=dk; dv_ref[ks,ls]=dv
            if j==0: dq_ref[:,ls]=dqc_ref[:,ls]+dq
            else: dq_ref[kc:,ls]=dq_ref[kc:,ls]+dq
    @pl.when(flag_ref[0]==1)
    def _():
        for p in range(pairs):
            ls = slice(p*128,(p+1)*128)
            acc=dq_ref[:,ls]
            for j in range(2):
                ks=pl.ds(j*kc,kc)
                dq,dk,dv=tile_pair(p,ks,pk_ref,pv_ref,0,None)
                dpk_ref[ks,ls]=dk.astype(BF); dpv_ref[ks,ls]=dv.astype(BF)
                acc=acc+dq
            dq_ref[:,ls]=acc
    @pl.when(flag_ref[0]==0)
    def _():
        dpk_ref[...]=jnp.zeros_like(dpk_ref); dpv_ref[...]=jnp.zeros_like(dpv_ref)

def attend_cross_back(flags,q,do,at,lse,k,v):
    n,w=q.shape; nk=k.shape[0]
    return pl.pallas_call(bwd_cross_kernel,out_shape=[S((n,w),F32),S((nk,w),BF),S((nk,w),BF),S((8,n),F32)],in_specs=[SM]+[VM]*6,out_specs=[VM]*4,scratch_shapes=[pltpu.VMEM((n,128),F32)],compiler_params=PAR)(flags,q,do,at,lse,k,v)
def attend_local_back(flags,q,do,lse,dl,k,v,pk,pv,dqc):
    n,w=q.shape
    return pl.pallas_call(bwd_local_kernel,out_shape=[S((n,w),F32),S((n,w),F32),S((n,w),F32),S((n,w),BF),S((n,w),BF)],in_specs=[SM]+[VM]*9,out_specs=[VM]*5,compiler_params=PAR)(flags,q,do,lse,dl,k,v,pk,pv,dqc)


def swap(value, axis, bit=0):
    count = lax.axis_size(axis)
    return lax.ppermute(value, axis, [(i, i ^ (1 << bit)) for i in range(count)])


def shift(value, steps):
    count = lax.axis_size("batch")
    first, last = max(0, -steps), min(count, count - steps)
    return lax.ppermute(value, "batch", [(i, i + steps) for i in range(first, last)])


def after(value, *earlier):
    return lax.optimization_barrier((value,) + earlier)[0]


def matmul(left, right):
    return jnp.dot(left, right, preferred_element_type=F32)


def matmul_nt(left, right):
    return lax.dot_general(left, right, (((1,), (1,)), ((), ())), preferred_element_type=F32)


def matmul_tn(left, right):
    return lax.dot_general(left, right, (((0,), (0,)), ((), ())), preferred_element_type=F32)


def norm_rows(values, scales, shifts):
    centred = values - jnp.mean(values, axis=-1, keepdims=True)
    spread = jnp.mean(centred * centred, axis=-1, keepdims=True)
    return centred * lax.rsqrt(spread + 1e-05) * scales + shifts


def norm_back(values, scales, grad):
    centred = values - jnp.mean(values, axis=-1, keepdims=True)
    spread = jnp.mean(centred * centred, axis=-1, keepdims=True)
    rate = lax.rsqrt(spread + 1e-05)
    unit = centred * rate
    scaled = grad * scales
    inner = jnp.mean(scaled * unit, axis=-1, keepdims=True)
    result = rate * (scaled - jnp.mean(scaled, axis=-1, keepdims=True) - unit * inner)
    return result, jnp.sum(grad * unit, axis=0), jnp.sum(grad, axis=0)


def gelu_both(u):
    factor = 0.7978845608028654
    square = u * u
    t = jnp.tanh(factor * u * (1.0 + 0.044715 * square))
    value = 0.5 * u * (1.0 + t)
    slope = 0.5 * (1.0 + t) + 0.5 * u * (1.0 - t * t) * factor * (1.0 + 3 * 0.044715 * square)
    return value, slope


def tensor_sum(make_part, count, rows):
    size = rows // count
    sums = []
    for i in range(count):
        part = make_part(i * size, size).astype(BF)
        sums.append(part.astype(F32) + swap(part, "tensor").astype(F32))
    return jnp.concatenate(sums, axis=0)


CHUNKS = 2


def forward_layer(x, layer, flags, carried_values):
    rows = x.shape[0]
    normed = norm_rows(x, layer["gains"][0], layer["biases"][0]).astype(BF)
    queries = ((matmul(normed, layer["wq"]) + layer["bq"]).astype(BF) * 0.125).astype(BF)
    keys = matmul(normed, layer["wk"]).astype(BF)
    own = (matmul(normed, layer["wvo"]) + layer["bv"]).astype(BF)
    if carried_values is None:
        values = jnp.concatenate([own, matmul(normed, layer["wvx"]).astype(BF)], axis=1)
        sent = values
    else:
        sent = own
    prior_k = shift(keys, 2)
    prior_v = shift(sent, 2)
    part_k, part_v = swap(keys, "batch"), swap(sent, "batch")
    prior_k = jnp.concatenate([prior_k, swap(prior_k, "batch")], axis=0)
    prior_v = jnp.concatenate([prior_v, swap(prior_v, "batch")], axis=0)
    if carried_values is not None:
        width = own.shape[1]
        values, part_v, prior_v = [
            jnp.concatenate([a, b[:, :width]], axis=1)
            for a, b in zip((own, part_v, prior_v), carried_values)
        ]
    out, total, top = attend_local(flags, queries, keys, values, part_k, part_v)
    attended, lse = attend_cross(flags, queries, prior_k, prior_v, out, total, top)

    hidden = x + layer["bo"] + tensor_sum(
        lambda start, size: matmul(attended[start : start + size], layer["wo"]), CHUNKS, rows
    )
    mlp_in = norm_rows(hidden, layer["gains"][1], layer["biases"][1]).astype(BF)
    pieces = []

    def down(start, size):
        active, slope = gelu_both(matmul(mlp_in[start : start + size], layer["wup"]) + layer["bup"])
        active = active.astype(BF)
        pieces.append((active, slope.astype(BF)))
        return matmul(active, layer["wdown"])

    y = hidden + layer["bdown"] + tensor_sum(down, CHUNKS, rows)
    active = jnp.concatenate([p[0] for p in pieces], axis=0)
    slope = jnp.concatenate([p[1] for p in pieces], axis=0)
    stored = dict(
        x=x, normed=normed, queries=queries, keys=keys, values=values, part_k=part_k, part_v=part_v,
        prior_k=prior_k, prior_v=prior_v, attended=attended, lse=lse, hidden=hidden, mlp_in=mlp_in,
        active=active, slope=slope,
    )
    return y, (values, part_v, prior_v), stored


def backward_layer(dy, layer, kept, flags, returned):
    rows = dy.shape[0]
    dy_low = dy.astype(BF)
    pieces = []

    def up_back(start, size):
        d_active = matmul_nt(dy_low[start : start + size], layer["wdown"])
        d_up = (d_active * kept["slope"][start : start + size].astype(F32)).astype(BF)
        pieces.append(d_up)
        return matmul_nt(d_up, layer["wup"])

    d_mlp_in = tensor_sum(up_back, CHUNKS, rows)
    d_up = jnp.concatenate(pieces, axis=0)
    back, d_gain1, d_bias1 = norm_back(kept["hidden"], layer["gains"][1], d_mlp_in)
    dh = dy + back
    dh_low = dh.astype(BF)
    d_attended = matmul_nt(dh_low, layer["wo"]).astype(BF)
    width = layer["wvo"].shape[1]
    dq_cross, d_prior_k, d_prior_v, delta = attend_cross_back(
        flags, kept["queries"], d_attended, kept["attended"], kept["lse"], kept["prior_k"], kept["prior_v"]
    )
    if returned is None:
        send_v = d_prior_v[:, :width]
    else:
        send_v = jnp.concatenate(
            [
                (d_prior_v[:, :width].astype(F32) + returned[2].astype(F32)).astype(BF),
                d_prior_v[:, width:],
            ],
            axis=1,
        )

    def home(grads):
        return shift(
            (grads[:rows].astype(F32) + swap(grads[rows:], "batch").astype(F32)).astype(BF), -2
        ).astype(F32)

    far_k, far_v = home(d_prior_k), home(send_v)
    dq, dk, dv, d_part_k, d_part_v = attend_local_back(
        flags, kept["queries"], d_attended, kept["lse"], delta, kept["keys"], kept["values"],
        kept["part_k"], kept["part_v"], dq_cross,
    )
    dk = dk + swap(d_part_k, "batch").astype(F32) + far_k
    dv_own, dv_other = dv[:, :width], dv[:, width:]
    if returned is None:
        back_values = (dv_other, d_part_v[:, width:], d_prior_v[:, width:])
        dv_low = (
            dv_own + swap(d_part_v[:, :width], "batch").astype(F32) + far_v
        ).astype(BF)
    else:
        back_values = None
        near = jnp.concatenate(
            [
                (d_part_v[:, :width].astype(F32) + returned[1].astype(F32)).astype(BF),
                d_part_v[:, width:],
            ],
            axis=1,
        )
        arrived = swap(near, "batch").astype(F32) + far_v
        dv_low = jnp.concatenate(
            [dv_own + returned[0] + arrived[:, :width], dv_other + arrived[:, width:]], axis=1
        ).astype(BF)
    dq_low = (dq * 0.125).astype(BF)
    dk_low = dk.astype(BF)

    def input_part(start, size):
        cut = slice(start, start + size)
        part = matmul_nt(dq_low[cut], layer["wq"]) + matmul_nt(dk_low[cut], layer["wk"])
        part = part + matmul_nt(dv_low[cut, :width], layer["wvo"])
        if returned is not None:
            part = part + matmul_nt(dv_low[cut, width:], layer["wvx"])
        return part

    d_normed = tensor_sum(input_part, CHUNKS, rows)
    back, d_gain0, d_bias0 = norm_back(kept["x"], layer["gains"][0], d_normed)
    dx = dh + back

    half = layer["wdown"].shape[1]
    up_cols = d_up.shape[1]
    d_down = matmul_tn(kept["active"], dy_low).astype(BF)
    d_ups = [
        matmul_tn(kept["mlp_in"], d_up[:, i : i + half]).astype(BF) for i in range(0, up_cols, half)
    ]
    d_out = matmul_tn(kept["attended"], dh_low).astype(BF)
    d_qk = matmul_tn(kept["normed"], jnp.concatenate([dq_low, dk_low], axis=1)).astype(BF)
    d_v = matmul_tn(kept["normed"], dv_low).astype(BF)
    if returned is None:
        d_v = jnp.concatenate([d_v, jnp.zeros_like(d_v)], axis=1)
    small = jnp.concatenate(
        [
            d_gain0, d_gain1, d_bias0, d_bias1, jnp.sum(dh, axis=0), jnp.sum(dy, axis=0),
            jnp.sum(dq_low.astype(F32), axis=0), jnp.sum(dv_low[:, :width].astype(F32), axis=0),
            jnp.sum(d_up.astype(F32), axis=0),
        ]
    )
    mlp = jnp.concatenate(
        [d.reshape(2, 2, -1, half) for d in [d_down] + d_ups], axis=2
    )
    features = half
    v_rows = features // 4
    v_packed = jnp.concatenate(
        [d_v.reshape(2, 2, 2, v_rows // 2, 2 * width)[:, :, i] for i in range(2)], axis=3
    )
    pad = 4 * SMALL_ROWS * features - small.shape[0]
    small_packed = jnp.pad(small, (0, pad)).astype(BF).reshape(2, 2, SMALL_ROWS, features)
    attn = jnp.concatenate(
        [d_qk.reshape(2, 2, -1, features), d_out.reshape(2, 2, -1, features), v_packed, small_packed],
        axis=2,
    )
    return dx, back_values, mlp, attn


SMALL_ROWS = 32


def scatter_sum(parts):
    core = lax.axis_index("batch") % 2
    section = lax.axis_index("section")
    take = lambda a, i, axis: lax.dynamic_index_in_dim(a, i, axis, keepdims=False)
    near = take(parts, core, 1).astype(F32) + swap(take(parts, 1 - core, 1), "batch").astype(F32)
    near = near.astype(BF)
    mine = take(near, section, 0).astype(F32) + swap(take(near, 1 - section, 0), "section").astype(F32)
    return all_sum(mine.astype(BF))


def all_sum(part):
    bits = (lax.axis_size("batch") // 2).bit_length() - 1
    index = lax.axis_index("batch")
    for bit in range(1, bits + 1):
        side = (index >> bit) & 1
        halves = part.reshape((2, part.shape[0] // 2) + part.shape[1:])
        keep = lax.dynamic_index_in_dim(halves, side, 0, keepdims=False)
        send = lax.dynamic_index_in_dim(halves, 1 - side, 0, keepdims=False)
        part = (keep.astype(F32) + swap(send, "batch", bit).astype(F32)).astype(BF)
    for bit in range(bits, 0, -1):
        side = (index >> bit) & 1
        part = paired(part, swap(part, "batch", bit), side).reshape((2 * part.shape[0],) + part.shape[1:])
    return part


def paired(mine, other, side):
    first = jnp.where(side == 0, mine, other)
    second = jnp.where(side == 0, other, mine)
    return jnp.stack([first, second])


def fetch_weights(values):
    core = lax.axis_index("batch") % 2
    halves = [v.reshape((2, v.shape[0] // 2) + v.shape[1:]) for v in values]
    sent = [lax.dynamic_index_in_dim(h, core, 0, keepdims=False) for h in halves]
    got = swap(sent, "section")
    other = swap(got, "batch")
    return [
        paired(a, b, core).reshape(v.shape) for a, b, v in zip(got, other, values)
    ]


def local(
    tokens, block_place, cotangent, norm_gains, norm_biases, query_key, query_bias, value_own, value_bias,
    value_extra, out_weight, out_bias, up_weight, up_bias, down_weight, down_bias,
):
    section = lax.axis_index("section")
    tensor = lax.axis_index("tensor")
    core = lax.axis_index("batch") % 2
    features = tokens.shape[3]
    half_rows = tokens.shape[2]
    head_width = query_bias.shape[1]
    width = value_own.shape[2]
    micros = tokens.shape[0]
    assert micros == 2 and lax.axis_size("section") == 2 and lax.axis_size("tensor") == 2

    def micro(array):
        return lax.dynamic_index_in_dim(array, section, 0, keepdims=False)[0]

    my_tokens = micro(tokens)
    my_cotangent = micro(cotangent)
    place = micro(block_place)
    flags = jnp.stack([place & 1, place >> 1]).astype(jnp.int32)

    small_sizes = [2 * features, 2 * features, head_width, width, features, up_bias.shape[1], features]
    small = jnp.concatenate(
        [a.reshape(-1) for a in (norm_gains, norm_biases, query_bias, value_bias, out_bias, up_bias, down_bias)]
    )
    wqk = query_key[0].reshape(features, 2 * head_width)
    first_own = [wqk, value_own[0]]
    x_rows = paired(my_tokens, swap(my_tokens, "tensor"), tensor).reshape(2 * half_rows, features)
    small_other = swap(small, "section")
    first_other = fetch_weights(first_own)
    second_own = [out_weight[0], up_weight[0]]
    held = lax.optimization_barrier(tuple(second_own) + tuple(first_other))
    second_other = fetch_weights(list(held[:2]))
    first_other = list(held[2:])
    held = lax.optimization_barrier((down_weight[0],) + tuple(second_other))
    third_other = fetch_weights([held[0]])
    second_other = list(held[1:])
    owns = first_own + second_own + [down_weight[0]]
    others = first_other + second_other + third_other

    layers = []
    for number in range(2):
        mine = section == number
        picked = [jnp.where(mine, a, b) for a, b in zip(owns, others)]
        numbers = jnp.where(mine, small, small_other)
        cuts = []
        start = 0
        for size in small_sizes:
            cuts.append(numbers[start : start + size])
            start += size
        layers.append(
            dict(
                gains=cuts[0].reshape(2, features), biases=cuts[1].reshape(2, features), bq=cuts[2], bv=cuts[3],
                bo=cuts[4], bup=cuts[5], bdown=cuts[6], wq=picked[0][:, :head_width], wk=picked[0][:, head_width:],
                wvo=picked[1], wvx=value_extra, wo=picked[2], wup=picked[3], wdown=picked[4],
            )
        )

    y0, carried, kept0 = forward_layer(x_rows.astype(F32), layers[0], flags, None)
    y0_low = y0.astype(BF)
    y1, ignored, kept1 = forward_layer(y0_low.astype(F32), layers[1], flags, carried)
    y1_low = y1.astype(BF)

    def my_half(rows):
        return lax.dynamic_slice_in_dim(rows, tensor * half_rows, half_rows, 0)

    def by_section(first, second, low):
        mine = jnp.where(section == 0, first, second)
        other = swap(jnp.where(section == 0, second, first).astype(low), "section").astype(mine.dtype)
        return paired(mine, other, section)

    outputs = by_section(my_half(y0_low), my_half(y1_low), BF)

    dy1 = paired(my_cotangent, swap(my_cotangent, "tensor"), tensor).reshape(2 * half_rows, features)
    dx1, back_values, mlp1, attn1 = backward_layer(dy1.astype(F32), layers[1], kept1, flags, None)
    mlp1, attn1 = scatter_sum(mlp1), scatter_sum(attn1)
    dx0, ignored, mlp0, attn0 = backward_layer(
        dx1.astype(BF).astype(F32), layers[0], kept0, flags, back_values
    )
    mlp0, attn0 = scatter_sum(mlp0), scatter_sum(attn0)
    input_grads = by_section(my_half(dx0), my_half(dx1), BF)

    def gathered(first, second):
        mine = jnp.where(section == 0, first, second)
        other = swap(jnp.where(section == 0, second, first), "section")
        both = paired(mine, other, section)
        return jnp.moveaxis(paired(both, swap(both, "batch"), core), 0, 1)

    mlp = gathered(mlp0, mlp1)
    attn = gathered(attn0, attn1)
    v_rows = features // 4

    def v_unpacked(packed):
        return jnp.stack([packed[..., : 2 * width], packed[..., 2 * width :]], axis=-3)

    qk_rows, out_rows = features // 4, head_width // 4
    v_start = qk_rows + out_rows
    v_end = v_start + v_rows // 2
    extra_mine = attn0[v_start:v_end]
    extra_mine = v_unpacked(extra_mine).reshape(v_rows, 2 * width)[:, width:]
    extra = paired(extra_mine, swap(extra_mine, "batch"), core).reshape(2 * v_rows, width).astype(F32)

    d_qk = attn[:, :, :qk_rows].reshape(features, 2, head_width).astype(F32)
    d_out = attn[:, :, qk_rows:v_start].reshape(head_width, features).astype(F32)
    d_v = v_unpacked(attn[:, :, v_start:v_end]).reshape(features, 2 * width)[:, :width].astype(F32)
    numbers = attn[:, :, v_end:].reshape(-1).astype(F32)
    d_down = mlp[:, :, : down_weight.shape[1] // 4].reshape(-1, features).astype(F32)
    pieces = []
    start = down_weight.shape[1] // 4
    for i in range(up_weight.shape[2] // features):
        pieces.append(mlp[:, :, start : start + features // 4].reshape(features, features))
        start += features // 4
    d_up = jnp.concatenate(pieces, axis=1).astype(F32)
    cuts = []
    start = 0
    for size in [features] * 6 + [head_width, width, up_bias.shape[1]]:
        cuts.append(numbers[start : start + size])
        start += size
    return (
        outputs.reshape(1, micros, 1, half_rows, features),
        input_grads.reshape(1, micros, 1, half_rows, features),
        jnp.stack(cuts[0:2])[None],
        jnp.stack(cuts[2:4])[None],
        d_qk[None],
        cuts[6][None],
        d_v[None],
        cuts[7][None],
        extra,
        d_out[None],
        cuts[4][None],
        d_up[None],
        cuts[8][None],
        d_down[None],
        cuts[5][None],
    )


def solution(mesh):
    return jax.shard_map(
        local,
        mesh=mesh,
        in_specs=(
            P(None, "batch", "tensor", None),
            P(None, "batch"),
            P(None, "batch", "tensor", None),
            P("section", None, None),
            P("section", None, None),
            P("section", None, None, "tensor"),
            P("section", "tensor"),
            P("section", None, "tensor"),
            P("section", "tensor"),
            P(None, "tensor"),
            P("section", "tensor", None),
            P("section", None),
            P("section", None, "tensor"),
            P("section", "tensor"),
            P("section", "tensor", None),
            P("section", None),
        ),
        out_specs=(
            P("section", None, "batch", "tensor", None),
            P("section", None, "batch", "tensor", None),
            P("section", None, None),
            P("section", None, None),
            P("section", None, None, "tensor"),
            P("section", "tensor"),
            P("section", None, "tensor"),
            P("section", "tensor"),
            P("section", "tensor"),
            P("section", "tensor", None),
            P("section", None),
            P("section", None, "tensor"),
            P("section", "tensor"),
            P("section", "tensor", None),
            P("section", None),
        ),
        check_vma=False,
    )
```

```python
import jax
import jax.numpy as jnp
from jax import lax
from jax.experimental import pallas as pl
from jax.experimental.pallas import tpu as pltpu
from jax.sharding import PartitionSpec as P

F32 = jnp.float32
BF = jnp.bfloat16
LOW = -1e30
HEAD = 64
CHUNKS = 2

GAIN0, GAIN1, BIAS0, BIAS1, BO, BDOWN, BQ, BKV, BUP = range(9)
TABLE = 16

WHOLE = pl.BlockSpec(memory_space=pltpu.VMEM)
SCALARS = pl.BlockSpec(memory_space=pltpu.SMEM)
FAR_OFF = pl.BlockSpec(memory_space=pltpu.HBM)


def dot_nn(a, b):
    return lax.dot_general(a, b, (((1,), (0,)), ((), ())), preferred_element_type=F32)


def dot_nt(a, b):
    return lax.dot_general(a, b, (((1,), (1,)), ((), ())), preferred_element_type=F32)


def dot_tn(a, b):
    return lax.dot_general(a, b, (((0,), (0,)), ((), ())), preferred_element_type=F32)


class Late:
    def __init__(self, array):
        self.array = array


def call(inner_body, outs, scalars, blocks, remote=(), scratch=(), us=1.0, limit=16):
    shapes = [jax.ShapeDtypeStruct(shape, kind) for shape, kind in outs]
    late = [i for i, b in enumerate(blocks) if isinstance(b, Late)]
    blocks = [b.array if isinstance(b, Late) else b for b in blocks]
    n_in, n_out = 1 + len(blocks) + len(remote), len(outs)
    staged = [pltpu.VMEM(blocks[i].shape, blocks[i].dtype) for i in late]
    sems = [pltpu.SemaphoreType.DMA((len(late),))] if late else []

    def body(*refs):
        refs = list(refs)
        if not late:
            return inner_body(*refs)
        first = n_in + n_out
        stage, sem, own = refs[first : first + len(late)], refs[first + len(late)], refs[first + len(late) + 1 :]
        copies = [pltpu.make_async_copy(refs[1 + i], v, sem.at[k]) for k, (i, v) in enumerate(zip(late, stage))]
        for copy in copies:
            copy.start()
        for copy in copies:
            copy.wait()
        for i, v in zip(late, stage):
            refs[1 + i] = v
        return inner_body(*refs[:first], *own)

    return pl.pallas_call(
        body,
        out_shape=shapes,
        in_specs=[SCALARS] + [FAR_OFF if i in late else WHOLE for i in range(len(blocks))] + [FAR_OFF] * len(remote),
        out_specs=[WHOLE] * len(outs),
        scratch_shapes=staged + sems + list(scratch),
        compiler_params=pltpu.CompilerParams(vmem_limit_bytes=limit * 1024 * 1024),
        cost_estimate=pl.CostEstimate(flops=int(us * 2.3e9), bytes_accessed=int(us * 4e6), transcendentals=0),
    )(scalars, *blocks, *remote)


def fetch_start(scalars, layer, own, got, other, held, sem):
    half = held.shape[0] // 2

    @pl.when(scalars[2] == layer)
    def _():
        pltpu.make_async_copy(own, held, sem).start()

    @pl.when(scalars[2] != layer)
    def _():
        mine = pl.multiple_of(scalars[3] * half, half)
        rest = pl.multiple_of((1 - scalars[3]) * half, half)
        pltpu.make_async_copy(got, held.at[pl.ds(mine, half)], sem).start()
        pltpu.make_async_copy(other, held.at[pl.ds(rest, half)], sem).start()


def fetch_wait(own, held, sem):
    pltpu.make_async_copy(own, held, sem).wait()


def held_like(*weights):
    return [pltpu.VMEM(w[0].shape, BF) for w in weights] + [pltpu.SemaphoreType.DMA] * len(weights)


def norm_parts(v):
    centred = v - jnp.mean(v, axis=-1, keepdims=True)
    rate = lax.rsqrt(jnp.mean(centred * centred, axis=-1, keepdims=True) + 1e-05)
    return centred * rate, rate


def norm_grad(v, gain, grad):
    unit, rate = norm_parts(v)
    scaled = grad * gain
    inner = jnp.mean(scaled * unit, axis=-1, keepdims=True)
    result = rate * (scaled - jnp.mean(scaled, axis=-1, keepdims=True) - unit * inner)
    return result, jnp.sum(grad * unit, axis=0, keepdims=True), jnp.sum(grad, axis=0, keepdims=True)


def gelu_both(u):
    factor = 0.7978845608028654
    square = u * u
    t = jnp.tanh(factor * u * (1.0 + 0.044715 * square))
    half = 0.5 * (1.0 + t)
    slope = half + (0.5 * factor) * u * (1.0 - t * t) * (1.0 + (3 * 0.044715) * square)
    return u * half, slope


def project(scalars, layer, weights, table, x=None, ahead=None, carried=None):
    if ahead is None:
        rows, features = x[0].shape
        blocks = [table, *x]
    else:
        rows, features = ahead[0][1].shape
        blocks = [table, ahead[0][0], Late(carried)]
        for chunk in ahead:
            blocks.extend(chunk[1:])
    width = weights[0].shape[1] // 3

    def body(scal, tab, *refs):
        given = refs[: len(blocks) - 1]
        own, got, other = refs[len(blocks) - 1 : len(blocks) + 2]
        outs = refs[len(blocks) + 2 : -2]
        held, sem = refs[-2:]
        fetch_start(scal, layer, own, got, other, held, sem)
        for c in range(CHUNKS):
            at = slice(c * rows, (c + 1) * rows)
            if ahead is None:
                v = given[c][...].astype(F32)
            else:
                before, carry = given[:2]
                hid, mine, came = given[2 + 3 * c : 5 + 3 * c]
                y = hid[...] + before[BDOWN : BDOWN + 1] + mine[...].astype(F32) + came[...].astype(F32)
                low = y.astype(BF)
                outs[5 + c][...] = low
                v = low.astype(F32)
            unit, _ = norm_parts(v)
            normed = (unit * tab[GAIN0 : GAIN0 + 1] + tab[BIAS0 : BIAS0 + 1]).astype(BF)
            outs[c][...] = normed
            if c == 0:
                fetch_wait(own, held, sem)
            q = dot_nn(normed, held[:, :width]) + tab[BQ : BQ + 1, :width]
            outs[2 + c][...] = (q.astype(BF).astype(F32) * 0.125).astype(BF)
            kv = dot_nn(normed, held[:, width:]) + tab[BKV : BKV + 1]
            if ahead is not None:
                rolled = pltpu.roll(carry[at, :].astype(F32), width // 2, 1)
                lane = lax.broadcasted_iota(jnp.int32, kv.shape, 1)
                kv = jnp.where(lane >= width + width // 2, rolled, kv)
            outs[4][at, :] = kv.astype(BF)

    outs = [((rows, features), BF)] * 2 + [((rows, width), BF)] * 2 + [((2 * rows, 2 * width), BF)]
    if ahead is not None:
        outs += [((rows, features), BF)] * 2
    r = call(body, outs, scalars, blocks, weights, held_like(weights), us=2.5)
    return list(x) if ahead is None else r[5:], r[:2], r[2:4], r[4]


def low_lanes(shape):
    return lax.broadcasted_iota(jnp.int32, shape, 1) < HEAD


def head_of(pair, sub, fill):
    keep = low_lanes(pair.shape)
    return jnp.where(keep if sub == 0 else ~keep, pair, jnp.full_like(pair, fill))


def halves_of(ref, size):
    return tuple(ref.at[i * size : (i + 1) * size] for i in range(ref.shape[0] // size))


def spans(p, width):
    return slice(p * 128, (p + 1) * 128), slice(width + p * 128, width + (p + 1) * 128)


def scored(q, tiles, p, width, masks):
    ks, vs = spans(p, width)
    tops, outs = [], []
    for sub in range(2):
        scores = [dot_nt(q, head_of(t[:, ks], sub, 0)) for t in tiles]
        scores = [s if m is None else jnp.where(m, s, LOW) for s, m in zip(scores, masks)]
        top = scores[0].max(axis=1, keepdims=True)
        for s in scores[1:]:
            top = jnp.maximum(top, s.max(axis=1, keepdims=True))
        total = None
        for s, t in zip(scores, tiles):
            part = dot_nn(jnp.exp(s - top).astype(BF), head_of(t[:, vs], sub, 1))
            total = part if total is None else total + part
        tops.append(top)
        outs.append(total)
    low = low_lanes(outs[0].shape)
    value = jnp.where(low, outs[0], outs[1])
    amount = pltpu.roll(jnp.where(low, outs[1], outs[0]), HEAD, 1)
    return tops, value, amount


def attend_local(scalars, q, kv, near):
    size, width = q[0].shape
    rows = size * CHUNKS

    def body(scal, q0, q1, k_all, n_all, out, amount, tops):
        own = halves_of(k_all, size)
        row = lax.broadcasted_iota(jnp.int32, (size, size), 0)
        col = lax.broadcasted_iota(jnp.int32, (size, size), 1)
        causal = col <= row

        def run(extra):
            for c, q_ref in enumerate((q0, q1)):
                at = slice(c * size, (c + 1) * size)
                tiles = list(extra) + [own[i] for i in range(c + 1)]
                masks = [None] * (len(tiles) - 1) + [causal]
                for p in range(width // 128):
                    span = slice(p * 128, (p + 1) * 128)
                    top, value, total = scored(q_ref[:, span], tiles, p, width, masks)
                    out[at, span] = value
                    amount[at, span] = total
                    tops[at, 2 * p : 2 * p + 1] = top[0]
                    tops[at, 2 * p + 1 : 2 * p + 2] = top[1]

        @pl.when(scal[0] == 1)
        def _():
            run(halves_of(n_all, size))

        @pl.when(scal[0] == 0)
        def _():
            run(())

    outs = [((rows, width), F32), ((rows, width), F32), ((rows, 128), F32)]
    return call(body, outs, scalars, [*q, kv, near], us=5)


def attend_far(scalars, layer, c, q, far, out, amount, tops, weights):
    size, width = q.shape
    features = weights[0].shape[1]

    def body(scal, q_ref, fa, fb, out_ref, amount_ref, tops_ref, own, got, other, att, lse, part, stats, held, sem):
        fetch_start(scal, layer, own, got, other, held, sem)
        at = slice(c * size, (c + 1) * size)
        stats[...] = jnp.zeros_like(stats)

        def finish(p, value, total, top0, top1):
            span = slice(p * 128, (p + 1) * 128)
            att[:, span] = (value / total).astype(BF)
            logs = jnp.log(total)
            stats[:, 2 * p : 2 * p + 1] = top0 + logs[:, 0:1]
            stats[:, 2 * p + 1 : 2 * p + 2] = top1 + logs[:, HEAD : HEAD + 1]

        @pl.when(scal[1] == 0)
        def _():
            for p in range(width // 128):
                span = slice(p * 128, (p + 1) * 128)
                finish(p, out_ref[at, span], amount_ref[at, span], tops_ref[at, 2 * p : 2 * p + 1], tops_ref[at, 2 * p + 1 : 2 * p + 2])

        @pl.when(scal[1] == 1)
        def _():
            for p in range(width // 128):
                span = slice(p * 128, (p + 1) * 128)
                new, value, total = scored(q_ref[:, span], halves_of(fa, size) + halves_of(fb, size), p, width, [None] * 4)
                tops_all, olds, news = [], [], []
                for sub in range(2):
                    before = tops_ref[at, 2 * p + sub : 2 * p + sub + 1]
                    top = jnp.maximum(before, new[sub])
                    tops_all.append(top)
                    olds.append(jnp.exp(before - top))
                    news.append(jnp.exp(new[sub] - top))
                low = low_lanes(value.shape)
                keep = jnp.where(low, olds[0], olds[1])
                take = jnp.where(low, news[0], news[1])
                finish(p, out_ref[at, span] * keep + value * take, amount_ref[at, span] * keep + total * take, *tops_all)

        lse[...] = jnp.transpose(stats[...])[0:8, :]
        fetch_wait(own, held, sem)
        part[...] = dot_nn(att[...], held[...]).astype(BF)

    outs = [((size, width), BF), ((8, size), F32), ((size, features), BF)]
    scratch = [pltpu.VMEM((size, 128), F32)] + held_like(weights)
    return call(body, outs, scalars, [q, *far, out, amount, tops], weights, scratch, us=4.5)


def back_tile(p, width, q, do, lse, delta, kv, mask):
    ks, vs = spans(p, width)
    dq, dks, dvs = None, [], []
    for sub in range(2):
        h = 2 * p + sub
        key = head_of(kv[:, ks], sub, 0)
        scores = dot_nt(key, q)
        weight = jnp.exp(scores - lse[h : h + 1, :])
        if mask is not None:
            weight = jnp.where(mask, weight, 0.0)
        d_weight = dot_nt(head_of(kv[:, vs], sub, 0), do)
        d_score = (weight * (d_weight - delta[h : h + 1, :])).astype(BF)
        dvs.append(dot_nn(weight.astype(BF), do))
        dks.append(dot_nn(d_score, q))
        d = dot_tn(d_score, key)
        dq = d if dq is None else dq + d
    low = low_lanes(dks[0].shape)
    return dq, jnp.where(low, dks[0], dks[1]), jnp.where(low, dvs[0], dvs[1])


def attend_others_back(scalars, q, do, lse, delta, far, near):
    size, width = q[0].shape
    rows = size * CHUNKS

    def body(scal, q0, q1, o0, o1, l0, l1, d0, d1, fa, fb, n_all, dq_out, mine, crossing):
        queries, grads, lses, deltas = (q0, q1), (o0, o1), (l0, l1), (d0, d1)
        dq_out[...] = jnp.zeros_like(dq_out)

        def run(sources):
            for p in range(width // 128):
                ks, vs = spans(p, width)
                total = [dq_out[c * size : (c + 1) * size, ks] for c in range(CHUNKS)]
                for source, ref, start in sources:
                    for i in range(CHUNKS):
                        tile = source.at[i * size : (i + 1) * size]
                        at = slice(start + i * size, start + (i + 1) * size)
                        dk = dv = None
                        for c in range(CHUNKS):
                            dq, k, v = back_tile(p, width, queries[c][:, ks], grads[c][:, ks], lses[c], deltas[c], tile, None)
                            total[c] = total[c] + dq
                            dk, dv = (k, v) if dk is None else (dk + k, dv + v)
                        ref[at, ks] = dk.astype(BF)
                        ref[at, vs] = dv.astype(BF)
                for c in range(CHUNKS):
                    dq_out[c * size : (c + 1) * size, ks] = total[c]

        @pl.when(scal[0] == 1)
        def _():
            run([(n_all, crossing, rows)])

        @pl.when(scal[0] == 0)
        def _():
            crossing[rows:, :] = jnp.zeros((rows, 2 * width), BF)

        @pl.when(scal[1] == 1)
        def _():
            run([(fb, crossing, 0), (fa, mine, 0)])

        @pl.when(scal[1] == 0)
        def _():
            mine[...] = jnp.zeros_like(mine)
            crossing[:rows, :] = jnp.zeros((rows, 2 * width), BF)

    outs = [((rows, width), F32), ((rows, 2 * width), BF), ((2 * rows, 2 * width), BF)]
    blocks = [*map(Late, q), *do, *map(Late, lse), *delta, *map(Late, far), Late(near)]
    return call(body, outs, scalars, blocks, us=16)


def attend_own_back(scalars, q, do, lse, delta, kv, dq_before):
    size, width = q[0].shape

    def body(scal, q0, q1, o0, o1, l0, l1, d0, d1, k_all, before, dq0, dq1, dk0, dk1):
        queries, grads, lses, deltas = (q0, q1), (o0, o1), (l0, l1), (d0, d1)
        key = lax.broadcasted_iota(jnp.int32, (size, size), 0)
        query = lax.broadcasted_iota(jnp.int32, (size, size), 1)
        causal = key <= query
        for p in range(width // 128):
            ks, vs = spans(p, width)
            total = [before[c * size : (c + 1) * size, ks] for c in range(CHUNKS)]
            for j, (source, ref) in enumerate(zip(halves_of(k_all, size), (dk0, dk1))):
                dk = dv = None
                for c in range(j, CHUNKS):
                    mask = causal if c == j else None
                    dq, k, v = back_tile(p, width, queries[c][:, ks], grads[c][:, ks], lses[c], deltas[c], source, mask)
                    total[c] = total[c] + dq
                    dk, dv = (k, v) if dk is None else (dk + k, dv + v)
                ref[:, ks] = dk
                ref[:, vs] = dv
            for c, ref in enumerate((dq0, dq1)):
                ref[:, ks] = (total[c] * 0.125).astype(BF)

    outs = [((size, width), BF)] * 2 + [((size, 2 * width), F32)] * 2
    blocks = [*map(Late, q), *do, *map(Late, lse), *delta, Late(kv), dq_before]
    return call(body, outs, scalars, blocks, us=6)


def feed_forward(scalars, layer, table, x, mine, came, up, down):
    rows, features = x.shape
    inner = up[0].shape[1]

    def body(scal, tab, x_ref, mine_ref, came_ref, u_own, u_got, u_other, d_own, d_got, d_other,
             hidden, mlp_in, active, slope, part, up_held, down_held, up_sem, down_sem):
        fetch_start(scal, layer, u_own, u_got, u_other, up_held, up_sem)
        fetch_start(scal, layer, d_own, d_got, d_other, down_held, down_sem)
        h = x_ref[...].astype(F32) + (mine_ref[...].astype(F32) + came_ref[...].astype(F32)) + tab[BO : BO + 1]
        hidden[...] = h
        unit, _ = norm_parts(h)
        low = (unit * tab[GAIN1 : GAIN1 + 1] + tab[BIAS1 : BIAS1 + 1]).astype(BF)
        mlp_in[...] = low
        fetch_wait(u_own, up_held, up_sem)
        for j in range(inner // features):
            cols = slice(j * features, (j + 1) * features)
            value, grad = gelu_both(dot_nn(low, up_held[:, cols]) + tab[BUP + j : BUP + j + 1])
            active[:, cols] = value.astype(BF)
            slope[:, cols] = grad.astype(BF)
        fetch_wait(d_own, down_held, down_sem)
        part[...] = dot_nn(active[...], down_held[...]).astype(BF)

    outs = [((rows, features), F32), ((rows, features), BF), ((rows, inner), BF), ((rows, inner), BF), ((rows, features), BF)]
    return call(body, outs, scalars, [table, Late(x), mine, came], [*up, *down], held_like(up, down), us=4, limit=24)


def feed_back(scalars, layer, dy, slope, up, down):
    rows, features = dy.shape
    inner = up[0].shape[1]

    def body(scal, dy_ref, slope_ref, u_own, u_got, u_other, d_own, d_got, d_other,
             d_up, part, sums, up_held, down_held, up_sem, down_sem):
        fetch_start(scal, layer, d_own, d_got, d_other, down_held, down_sem)
        fetch_start(scal, layer, u_own, u_got, u_other, up_held, up_sem)
        sums[...] = jnp.zeros_like(sums)
        fetch_wait(d_own, down_held, down_sem)
        for j in range(inner // features):
            cols = slice(j * features, (j + 1) * features)
            grad = (dot_nt(dy_ref[...], down_held[cols, :]) * slope_ref[:, cols].astype(F32)).astype(BF)
            d_up[:, cols] = grad
            sums[j : j + 1, :] = jnp.sum(grad.astype(F32), axis=0, keepdims=True)
        fetch_wait(u_own, up_held, up_sem)
        part[...] = dot_nt(d_up[...], up_held[...]).astype(BF)

    outs = [((rows, inner), BF), ((rows, features), BF), ((8, features), F32)]
    return call(body, outs, scalars, [dy, Late(slope)], [*up, *down], held_like(up, down), us=4.5, limit=24)


def middle_back(scalars, layer, table, hidden, mine, came, dy, attended, weights):
    rows, features = hidden.shape
    width = attended.shape[1]

    def body(scal, tab, hid, mine_ref, came_ref, dy_ref, att, own, got, other, dh_ref, low_ref, da_ref, delta, sums, stats, held, sem):
        fetch_start(scal, layer, own, got, other, held, sem)
        grad = mine_ref[...].astype(F32) + came_ref[...].astype(F32)
        back, d_gain, d_bias = norm_grad(hid[...], tab[GAIN1 : GAIN1 + 1], grad)
        up = dy_ref[...].astype(F32)
        dh = up + back
        dh_ref[...] = dh
        low = dh.astype(BF)
        low_ref[...] = low
        sums[...] = jnp.zeros_like(sums)
        sums[0:1, :] = d_gain
        sums[1:2, :] = d_bias
        sums[2:3, :] = jnp.sum(dh, axis=0, keepdims=True)
        sums[3:4, :] = jnp.sum(up, axis=0, keepdims=True)
        stats[...] = jnp.zeros_like(stats)
        fetch_wait(own, held, sem)
        da = dot_nt(low, held[...]).astype(BF)
        da_ref[...] = da
        for p in range(width // 128):
            span = slice(p * 128, (p + 1) * 128)
            product = da[:, span].astype(F32) * att[:, span].astype(F32)
            first = low_lanes(product.shape)
            stats[:, 2 * p : 2 * p + 1] = jnp.sum(jnp.where(first, product, 0.0), axis=1, keepdims=True)
            stats[:, 2 * p + 1 : 2 * p + 2] = jnp.sum(jnp.where(first, 0.0, product), axis=1, keepdims=True)
        delta[...] = jnp.transpose(stats[...])[0:8, :]

    outs = [((rows, features), F32), ((rows, features), BF), ((rows, width), BF), ((8, rows), F32), ((8, features), F32)]
    scratch = [pltpu.VMEM((rows, 128), F32)] + held_like(weights)
    return call(body, outs, scalars, [table, Late(hidden), mine, came, dy, Late(attended)], weights, scratch, us=2.8)


def project_back(scalars, layer, c, dq, dkv, near, far, returned, weights):
    rows, width = dq.shape
    features = weights[0].shape[0]

    def body(scal, dq_ref, dkv_ref, near_ref, far_ref, *rest):
        back_ref = rest[0] if returned is not None else None
        own, got, other = rest[-9:-6] if returned is None else rest[-8:-5]
        outs = rest[-6:-2] if returned is None else rest[-5:-2]
        held, sem = rest[-2:]
        fetch_start(scal, layer, own, got, other, held, sem)
        at = slice(c * rows, (c + 1) * rows)
        total = dkv_ref[...] + near_ref[at, :].astype(F32) + far_ref[at, :].astype(F32)
        if returned is None:
            outs[3][...] = total
        else:
            rolled = pltpu.roll(back_ref[...], 2 * width - width // 2, 1)
            lane = lax.broadcasted_iota(jnp.int32, total.shape, 1)
            total = total + jnp.where((lane >= width) & (lane < width + width // 2), rolled, 0.0)
        low = total.astype(BF)
        outs[0][...] = low
        sums = outs[2]
        sums[...] = jnp.zeros_like(sums)
        sums[0:1, :width] = jnp.sum(dq_ref[...].astype(F32), axis=0, keepdims=True)
        sums[1:2, :] = jnp.sum(low.astype(F32), axis=0, keepdims=True)
        fetch_wait(own, held, sem)
        outs[1][...] = (dot_nt(dq_ref[...], held[:, :width]) + dot_nt(low, held[:, width:])).astype(BF)

    outs = [((rows, 2 * width), BF), ((rows, features), BF), ((8, features), F32)]
    blocks = [dq, dkv, near, far]
    if returned is None:
        outs.append(((rows, 2 * width), F32))
    else:
        blocks.append(returned)
    return call(body, outs, scalars, blocks, weights, held_like(weights), us=2.7)


def last_back(scalars, table, x, mine, came, dh):
    rows, features = x.shape

    def body(scal, tab, x_ref, mine_ref, came_ref, dh_ref, dx_ref, low_ref, sums):
        grad = mine_ref[...].astype(F32) + came_ref[...].astype(F32)
        back, d_gain, d_bias = norm_grad(x_ref[...].astype(F32), tab[GAIN0 : GAIN0 + 1], grad)
        dx = dh_ref[...] + back
        dx_ref[...] = dx
        low_ref[...] = dx.astype(BF)
        sums[...] = jnp.zeros_like(sums)
        sums[0:1, :] = d_gain
        sums[1:2, :] = d_bias

    outs = [((rows, features), F32), ((rows, features), BF), ((8, features), F32)]
    return call(body, outs, scalars, [table, Late(x), mine, came, Late(dh)], us=1.5)


def both_chunks(left, left_span, right, right_span):
    total = None
    for a, b in zip(left, right):
        d = dot_tn(a[:, left_span], b[:, right_span])
        total = d if total is None else total + d
    return total


def wide_grads(scalars, active, dy, mlp_in, d_up):
    features = dy[0].shape[1]
    inner = active[0].shape[1]
    a, half = inner // 4, features // 2
    size = a + half

    def body(scal, a0, a1, y0, y1, m0, m1, u0, u1, packed):
        for k in range(4):
            span = slice(k * a, (k + 1) * a)
            packed[k, :a, :] = both_chunks((a0, a1), span, (y0, y1), slice(None)).astype(BF)
            for i in range(2):
                part = both_chunks((m0, m1), slice(i * half, (i + 1) * half), (u0, u1), span)
                packed[k, a:, i * a : (i + 1) * a] = part.astype(BF)

    blocks = [*map(Late, active), *dy, *map(Late, mlp_in), *d_up]
    return call(body, [((4, size, features), BF)], scalars, blocks, us=3.7)[0]


def narrow_grads(scalars, normed, dq, dkv, attended, dh_low):
    features = normed[0].shape[1]
    width = dq[0].shape[1]
    rows = features // 4
    half, c = rows // 2, width // 4
    size = rows + half + c

    def body(scal, n0, n1, q0, q1, k0, k1, t0, t1, h0, h1, packed):
        every = slice(None)
        for x in range(2):
            span = slice(2 * x * rows, 2 * (x + 1) * rows)
            first = both_chunks((n0, n1), span, (q0, q1), every).astype(BF)
            second = both_chunks((n0, n1), span, (k0, k1), every).astype(BF)
            for core in range(2):
                k, at = 2 * core + x, core * rows
                packed[k, :rows, :width] = first[at : at + rows, :]
                packed[k, :rows, width:] = second[at : at + rows, :width]
                packed[k, rows : rows + half, :width] = second[at : at + half, width:]
                packed[k, rows : rows + half, width:] = second[at + half : at + rows, width:]
        out = both_chunks((t0, t1), every, (h0, h1), every).astype(BF)
        for k in range(4):
            packed[k, rows + half :, :] = out[k * c : (k + 1) * c, :]

    blocks = [*map(Late, normed), *dq, *dkv, *map(Late, attended), *map(Late, dh_low)]
    return call(body, [((4, size, features), BF)], scalars, blocks, us=2.1)[0]


def collect(scal, refs, held, sem):
    copies = []
    for i, ref in enumerate(refs):
        core = scal[3] if i < 2 else 1 - scal[3]
        section = scal[2] if i % 2 == 0 else 1 - scal[2]
        copies.append(pltpu.make_async_copy(ref, held.at[2 * core + section], sem.at[i]))
    for copy in copies:
        copy.start()
    for copy in copies:
        copy.wait()


def wide_unpack(scalars, parts, inner):
    size, features = parts[0].shape
    a, half = inner // 4, features // 2

    def body(scal, p0, p1, p2, p3, down, up, held, sem):
        collect(scal, (p0, p1, p2, p3), held, sem)
        for k in range(4):
            down[k * a : (k + 1) * a, :] = held[k, :a, :].astype(F32)
            for i in range(2):
                up[i * half : (i + 1) * half, k * a : (k + 1) * a] = held[k, a:, i * a : (i + 1) * a].astype(F32)

    outs = [((inner, features), F32), ((features, inner), F32)]
    scratch = [pltpu.VMEM((4, size, features), BF), pltpu.SemaphoreType.DMA((4,))]
    return call(body, outs, scalars, [], parts, scratch, us=5)


def narrow_unpack(scalars, parts, extras, width):
    size, features = parts[0].shape
    rows = features // 4
    half, c, own = rows // 2, width // 4, width // 2

    def body(scal, p0, p1, p2, p3, e0, e1, query, key, value, extra, out, held, pair, sem, pair_sem):
        last = [pltpu.make_async_copy(e, pair.at[i if i == 0 else 1], pair_sem.at[i]) for i, e in enumerate((e0, e1))]
        for copy in last:
            copy.start()
        collect(scal, (p0, p1, p2, p3), held, sem)
        for copy in last:
            copy.wait()
        for x in range(2):
            for core in range(2):
                k, at = 2 * core + x, (2 * x + core) * rows
                query[at : at + rows, :] = held[k, :rows, :width].astype(F32)
                key[at : at + rows, :] = held[k, :rows, width:].astype(F32)
                value[at : at + half, :] = held[k, rows : rows + half, :own].astype(F32)
                value[at + half : at + rows, :] = held[k, rows : rows + half, width : width + own].astype(F32)
        for k in range(4):
            out[k * c : (k + 1) * c, :] = held[k, rows + half :, :].astype(F32)
        for i in range(2):
            core = scal[3] if i == 0 else 1 - scal[3]
            at = pl.multiple_of(core * rows, rows)
            cut = pair[i].astype(F32)
            left = pltpu.roll(cut[:, :width], own, 1)
            right = pltpu.roll(cut[:, width:], own, 1)
            extra[pl.ds(at, half), :] = left[:, :own]
            extra[pl.ds(pl.multiple_of(at + half, 8), half), :] = right[:, :own]

    outs = [((features, width), F32)] * 2 + [((features, own), F32), ((2 * rows, own), F32), ((width, features), F32)]
    scratch = [
        pltpu.VMEM((4, size, features), BF), pltpu.VMEM((2, half, features), BF),
        pltpu.SemaphoreType.DMA((4,)), pltpu.SemaphoreType.DMA((2,)),
    ]
    return call(body, outs, scalars, [], list(parts) + list(extras), scratch, us=3)


def swap(value, axis, bits=1):
    count = lax.axis_size(axis)
    return lax.ppermute(value, axis, [(i, i ^ bits) for i in range(count)])


def shift(value, steps):
    count = lax.axis_size("batch")
    first, last = max(0, -steps), min(count, count - steps)
    return lax.ppermute(value, "batch", [(i, i + steps) for i in range(first, last)])


def after(value, *earlier):
    return lax.optimization_barrier((value,) + earlier)[0]


def take(array, index, axis=0):
    return lax.dynamic_index_in_dim(array, index, axis, keepdims=False)


def paired(mine, other, side):
    return jnp.where(side == 0, mine, other), jnp.where(side == 0, other, mine)


class Reduction:
    def __init__(self, parts):
        self.core = lax.axis_index("batch") % 2
        self.section = lax.axis_index("section")
        self.parts = parts.reshape((2, 2) + parts.shape[1:])

    def over_cores(self):
        self.near = swap(take(self.parts, 1 - self.core), "batch")
        return self.near

    def prepare(self):
        mine = take(self.parts, self.core)
        other = 1 - self.section
        self.sent = (take(mine, other).astype(F32) + take(self.near, other).astype(F32)).astype(BF)
        self.kept = (take(mine, self.section).astype(F32) + take(self.near, self.section).astype(F32)).astype(BF)

    def over_sections(self):
        self.came = swap(self.sent, "section")

    def scatter(self):
        self.bits = list(range(1, lax.axis_size("batch").bit_length() - 1))
        index = lax.axis_index("batch")
        part = (self.kept.astype(F32) + self.came.astype(F32)).astype(BF)
        for bit in self.bits[:-1]:
            side = (index >> bit) & 1
            cut = part.reshape((2, part.shape[0] // 2) + part.shape[1:])
            if bit > 1:
                cut = lax.optimization_barrier(cut)
            got = swap(take(cut, 1 - side), "batch", 1 << bit)
            part = (take(cut, side), got)
            if bit != self.bits[-2]:
                part = (part[0].astype(F32) + part[1].astype(F32)).astype(BF)
        self.part = part
        return part

    def exchange(self):
        part = self.part
        self.part = (part[0].astype(F32) + part[1].astype(F32)).astype(BF)
        self.over = swap(self.part, "batch", 1 << self.bits[-1])

    def gather(self):
        part = (self.part.astype(F32) + self.over.astype(F32)).astype(BF)
        index = lax.axis_index("batch")
        for bit in reversed(self.bits[:-1]):
            got = swap(part, "batch", 1 << bit)
            self.pair = (part, got, (index >> bit) & 1)
            part = jnp.concatenate(paired(*self.pair), axis=0)
        return part

    def finish(self):
        self.quarter = jnp.concatenate(paired(*self.pair), axis=0)


def tie(value, *others):
    return lax.optimization_barrier((value,) + others)


def forward_layer(scalars, layer, table, w, x=None, ahead=None, carried=None, hooks=None):
    hooks = hooks or {}
    nothing = lambda value: value
    x, normed, q, kv = project(scalars, layer, w["qkv"], table, x=x, ahead=ahead, carried=carried)
    if "projected" in hooks:
        kv = hooks["projected"](kv, q)
    far = shift(kv, 2)
    near = swap(kv, "batch")
    out, amount, tops = attend_local(scalars, q, kv, near)
    far = hooks.get("arrived", nothing)(after(far, out))
    far = [far, swap(far, "batch")]
    att, lse, parts, came = [], [], [], []
    for c in range(CHUNKS):
        a, l, part = attend_far(scalars, layer, c, q[c], far, out, amount, tops, w["out"])
        att.append(a)
        lse.append(l)
        parts.append(part)
        came.append(swap(part, "tensor"))
    came[0] = hooks.get("far", lambda came, part: came)(came[0], parts[-1])
    hidden, mlp_in, active, slope, results = [], [], [], [], []
    for c in range(CHUNKS):
        h, m, a, s, part = feed_forward(scalars, layer, table, x[c], parts[c], came[c], w["up"], w["down"])
        hidden.append(h)
        mlp_in.append(m)
        active.append(a)
        slope.append(s)
        results.append((table, h, part))
    kept = dict(x=x, normed=normed, q=q, kv=kv, near=near, far=far, att=att, lse=lse, hidden=hidden,
                mlp_in=mlp_in, active=active, slope=slope)
    return results, kept


def backward_layer(scalars, layer, table, w, kept, dy, returned, steps):
    rows = CHUNKS * dy[0].shape[0]
    dy = steps("start", dy)
    d_up, parts, up_sums = [], [], []
    for c in range(CHUNKS):
        grad, part, sums = feed_back(scalars, layer, dy[c], kept["slope"][c], w["up"], w["down"])
        d_up.append(grad)
        up_sums.append(sums)
        parts.append((part, swap(part, "tensor")))
    wide = Reduction(wide_grads(scalars, kept["active"], dy, kept["mlp_in"], d_up))
    parts = steps("fed", parts, wide)
    dh, dh_low, d_att, delta, mid_sums = [], [], [], [], []
    for c in range(CHUNKS):
        r = middle_back(scalars, layer, table, kept["hidden"][c], *parts[c], dy[c], kept["att"][c], w["out"])
        for held, value in zip((dh, dh_low, d_att, delta, mid_sums), r):
            held.append(value)
    d_att = steps("mid", d_att, wide)
    dq, mine, crossing = attend_others_back(
        scalars, kept["q"], d_att, kept["lse"], delta, kept["far"], kept["near"]
    )
    came = swap(crossing, "batch")
    total, near = (mine.astype(F32) + came[:rows].astype(F32)).astype(BF), came[rows:]
    total, dq = steps("far", (total, dq), wide)
    home = shift(total, -2)
    dq0, dq1, dk0, dk1 = attend_own_back(scalars, kept["q"], d_att, kept["lse"], delta, kept["kv"], dq)
    dq, dkv = [dq0, dq1], [dk0, dk1]
    home, dq = steps("near", (home, dq), wide)
    dkv_low, parts, in_sums, back = [], [], [], []
    for c in range(CHUNKS):
        again = None if returned is None else returned[c]
        r = project_back(scalars, layer, c, dq[c], dkv[c], near, home, again, w["qkv"])
        dkv_low.append(r[0])
        parts.append((r[1], swap(r[1], "tensor")))
        in_sums.append(r[2])
        back.extend(r[3:])
    narrow = Reduction(narrow_grads(scalars, kept["normed"], dq, dkv_low, kept["att"], dh_low))
    parts = steps("proj", parts, wide, narrow)
    dx, dx_low, last_sums = [], [], []
    for c in range(CHUNKS):
        r = last_back(scalars, table, kept["x"][c], *parts[c], dh[c])
        dx.append(r[0])
        dx_low.append(r[1])
        last_sums.append(r[2])
    up, mid, last, inn = [a + b for a, b in (up_sums, mid_sums, last_sums, in_sums)]
    blank = jnp.zeros((TABLE - BUP - 2, up.shape[1]), F32)
    small = jnp.concatenate(
        [last[0:1], mid[0:1], last[1:2], mid[1:2], mid[2:4], inn[0:2], up[0:2], blank], axis=0
    )
    return dx, dx_low, back, wide, narrow, small


def local(
    tokens, block_place, cotangent, norm_gains, norm_biases, query_key, query_bias, value_own, value_bias,
    value_extra, out_weight, out_bias, up_weight, up_bias, down_weight, down_bias,
):
    section = lax.axis_index("section")
    tensor = lax.axis_index("tensor")
    core = lax.axis_index("batch") % 2
    micros, _, half_rows, features = tokens.shape
    width = query_bias.shape[1]
    own_width = value_own.shape[2]
    inner = up_weight.shape[2]
    assert micros == 2 and lax.axis_size("section") == 2 and lax.axis_size("tensor") == 2
    assert 2 * own_width == width and 2 * width == features and inner == 2 * features

    place = take(block_place, section)[0]
    scalars = jnp.stack([place & 1, place >> 1, section, core]).astype(jnp.int32)

    my_tokens = take(tokens, section)[0]
    x = paired(my_tokens, swap(my_tokens, "tensor"), tensor)

    def row(*pieces):
        flat = jnp.concatenate([p.reshape(-1) for p in pieces])
        return jnp.pad(flat, (0, features - flat.shape[0]))[None]

    blank = jnp.zeros((width,), F32)
    own_table = jnp.concatenate(
        [norm_gains[0], norm_biases[0], out_bias, down_bias, row(query_bias[0]), row(blank, value_bias[0]),
         up_bias[0].reshape(2, features), jnp.zeros((TABLE - BUP - 2, features), F32)], axis=0
    )
    extra = jnp.where(section == 0, value_extra, jnp.zeros_like(value_extra))
    pieces = [query_key[0].reshape(features, 2 * width), value_own[0], extra]

    def half_of(weight):
        return take(weight.reshape((2, weight.shape[0] // 2) + weight.shape[1:]), core)

    qkv_half = jnp.concatenate([half_of(p) for p in pieces], axis=1)
    qkv = jnp.concatenate(pieces, axis=1)
    other_table = swap(own_table, "section")
    qkv_got = swap(qkv_half, "section")
    out_got = swap(half_of(out_weight[0]), "section")
    tables = paired(own_table, other_table, section)
    qkv_got, out_got, qkv, scalars, *rest = tie(qkv_got, out_got, qkv, scalars, *tables, *x)
    tables, x = rest[:2], rest[2:]
    qkv_other = swap(qkv_got, "batch")
    w = dict(qkv=(qkv, qkv_got, qkv_other))
    late = {}

    def on_projected(kv, q):
        up, down, mine, kv = tie(half_of(up_weight[0]), half_of(down_weight[0]), take(cotangent, section)[0], kv)
        late["up"], late["down"] = swap(up, "section"), swap(down, "section")
        late["dy"] = mine, swap(mine, "tensor")
        w["out"] = (out_weight[0], out_got, swap(after(out_got, kv), "batch"))
        return kv

    def on_arrived(far):
        mine, other = late["dy"]
        far, got, other = tie(far, late["up"], other)
        late["dy"] = paired(mine, other, tensor)
        w["up"] = (up_weight[0], got, swap(got, "batch"))
        return far

    def on_far(came, part):
        came, got = tie(came, late["down"], part)[:2]
        w["down"] = (down_weight[0], got, swap(got, "batch"))
        return came

    first, kept0 = forward_layer(
        scalars, 0, tables[0], w, x=x, hooks=dict(projected=on_projected, arrived=on_arrived, far=on_far)
    )
    first = [r + (swap(r[2], "tensor"),) for r in first]
    second, kept1 = forward_layer(scalars, 1, tables[1], w, ahead=first, carried=kept0["kv"])
    y0 = kept1["x"]

    def my_half(chunks):
        return jnp.where(tensor == 0, chunks[0], chunks[1])

    def by_section(mine0, mine1, kind):
        mine = jnp.where(section == 0, mine0, mine1)
        other = swap(jnp.where(section == 0, mine1, mine0).astype(kind), "section")
        return mine, other

    def steps1(number, values, wide=None, narrow=None):
        leaves, tree = jax.tree.flatten(values)
        if number == "fed":
            *leaves, wide.parts = tie(*leaves, wide.parts)
            wide.over_cores()
        if number == "mid":
            *leaves, wide.near = tie(*leaves, wide.near)
            wide.prepare()
            *leaves, wide.sent = tie(*leaves, wide.sent)
            wide.over_sections()
        if number == "near":
            *leaves, wide.came = tie(*leaves, wide.came)
            wide.scatter()
        if number == "proj":
            *leaves, narrow.parts = tie(*leaves, narrow.parts)
            narrow.over_cores()
        return jax.tree.unflatten(tree, leaves)

    dx1, dx1_low, back, wide1, narrow1, small1 = backward_layer(scalars, 1, tables[1], w, kept1, late["dy"], None, steps1)

    def steps0(number, values, wide=None, narrow=None):
        leaves, tree = jax.tree.flatten(values)
        if number == "start":
            kept, got = wide1.part
            *leaves, got, narrow1.near = tie(*leaves, got, narrow1.near)
            wide1.part = kept, got
            wide1.exchange()
            narrow1.prepare()
            narrow1.over_sections()
        if number == "fed":
            *leaves, wide.parts, narrow1.came = tie(*leaves, wide.parts, narrow1.came)
            wide.over_cores()
            narrow1.scatter()
        if number == "mid":
            *leaves, wide.near, wide1.over = tie(*leaves, wide.near, wide1.over)
            wide1.gather()
            wide.prepare()
            *leaves, wide.sent = tie(*leaves, wide.sent)
            wide.over_sections()
        if number == "far":
            mine, got, side = wide1.pair
            kept, came = narrow1.part
            *leaves, got, came = tie(*leaves, got, came)
            wide1.pair = mine, got, side
            narrow1.part = kept, came
        if number == "near":
            *leaves, wide.came = tie(*leaves, wide.came)
            wide.scatter()
            narrow1.exchange()
        if number == "proj":
            kept, got = wide.part
            *leaves, narrow.parts, got = tie(*leaves, narrow.parts, got)
            wide.part = kept, got
            narrow.over_cores()
            wide.exchange()
            narrow.prepare()
            narrow.over_sections()
        return jax.tree.unflatten(tree, leaves)

    dx0, dx0_low, _, wide0, narrow0, small0 = backward_layer(scalars, 0, tables[0], w, kept0, dx1_low, back, steps0)
    came = [swap(after(r[2], dx0_low[0]), "tensor") for r in second]
    y1 = my_half(
        [(r[1] + r[0][BDOWN : BDOWN + 1] + r[2].astype(F32) + c.astype(F32)).astype(BF) for r, c in zip(second, came)]
    )
    outputs = jnp.stack(paired(*by_section(my_half(y0), y1, BF), section))
    narrow1.gather()
    narrow0.scatter()
    wide0.gather()
    narrow0.exchange()
    narrow0.gather()
    for work in (wide0, wide1, narrow0, narrow1):
        work.finish()
    input_grads = paired(*[a.astype(F32) for a in by_section(my_half(dx0), my_half(dx1), BF)], section)
    input_grads = jnp.stack(input_grads)

    sums = jnp.stack([small0, small1])
    sums = sums + swap(sums, "batch")
    table = take(sums, section) + swap(take(sums, 1 - section), "section")
    for bit in range(1, lax.axis_size("batch").bit_length() - 1):
        table = table + swap(table, "batch", 1 << bit)

    def gathered(first, second):
        mine = jnp.where(section == 0, first, second)
        other = swap(jnp.where(section == 0, second, first), "section")
        return mine, other, swap(mine, "batch"), swap(other, "batch")

    d_down, d_up = wide_unpack(scalars, gathered(wide0.quarter, wide1.quarter), inner)
    rows = features // 4
    extra = narrow0.quarter[rows : rows + rows // 2]
    extras = (extra, swap(extra, "batch"))
    d_q, d_k, d_v, d_extra, d_out = narrow_unpack(
        scalars, gathered(narrow0.quarter, narrow1.quarter), extras, width
    )
    d_qk = jnp.stack([d_q, d_k], axis=1)
    return (
        outputs.reshape(1, micros, 1, half_rows, features),
        input_grads.reshape(1, micros, 1, half_rows, features),
        table[GAIN0 : GAIN1 + 1][None],
        table[BIAS0 : BIAS1 + 1][None],
        d_qk.reshape(1, features, 2, width),
        table[BQ : BQ + 1, :width],
        d_v[None],
        table[BKV : BKV + 1, width : width + own_width],
        d_extra,
        d_out[None],
        table[BO : BO + 1],
        d_up[None],
        table[BUP : BUP + 2].reshape(1, inner),
        d_down[None],
        table[BDOWN : BDOWN + 1],
    )


def solution(mesh):
    return jax.shard_map(
        local,
        mesh=mesh,
        in_specs=(
            P(None, "batch", "tensor", None),
            P(None, "batch"),
            P(None, "batch", "tensor", None),
            P("section", None, None),
            P("section", None, None),
            P("section", None, None, "tensor"),
            P("section", "tensor"),
            P("section", None, "tensor"),
            P("section", "tensor"),
            P(None, "tensor"),
            P("section", "tensor", None),
            P("section", None),
            P("section", None, "tensor"),
            P("section", "tensor"),
            P("section", "tensor", None),
            P("section", None),
        ),
        out_specs=(
            P("section", None, "batch", "tensor", None),
            P("section", None, "batch", "tensor", None),
            P("section", None, None),
            P("section", None, None),
            P("section", None, None, "tensor"),
            P("section", "tensor"),
            P("section", None, "tensor"),
            P("section", "tensor"),
            P("section", "tensor"),
            P("section", "tensor", None),
            P("section", None),
            P("section", None, "tensor"),
            P("section", "tensor"),
            P("section", "tensor", None),
            P("section", None),
        ),
        check_vma=False,
    )
```

```python
import jax
import jax.numpy as jnp
from jax import lax
from jax.experimental import pallas as pl
from jax.experimental.pallas import tpu as pltpu
from jax.sharding import PartitionSpec as P

F32 = jnp.float32
BF = jnp.bfloat16
LOW = -1e30
HEAD = 64
CHUNKS = 2

GAIN0, GAIN1, BIAS0, BIAS1, BO, BDOWN, BQ, BKV, BUP = range(9)
TABLE = 16

WHOLE = pl.BlockSpec(memory_space=pltpu.VMEM)
SCALARS = pl.BlockSpec(memory_space=pltpu.SMEM)
FAR_OFF = pl.BlockSpec(memory_space=pltpu.HBM)


def dot_nn(a, b):
    return lax.dot_general(a, b, (((1,), (0,)), ((), ())), preferred_element_type=F32)


def dot_nt(a, b):
    return lax.dot_general(a, b, (((1,), (1,)), ((), ())), preferred_element_type=F32)


def dot_tn(a, b):
    return lax.dot_general(a, b, (((0,), (0,)), ((), ())), preferred_element_type=F32)


class Late:
    def __init__(self, array):
        self.array = array


def call(inner_body, outs, scalars, blocks, remote=(), scratch=(), us=1.0, limit=16):
    shapes = [jax.ShapeDtypeStruct(shape, kind) for shape, kind in outs]
    late = [i for i, b in enumerate(blocks) if isinstance(b, Late)]
    blocks = [b.array if isinstance(b, Late) else b for b in blocks]
    n_in, n_out = 1 + len(blocks) + len(remote), len(outs)
    staged = [pltpu.VMEM(blocks[i].shape, blocks[i].dtype) for i in late]
    sems = [pltpu.SemaphoreType.DMA((len(late),))] if late else []

    def body(*refs):
        refs = list(refs)
        if not late:
            return inner_body(*refs)
        first = n_in + n_out
        stage, sem, own = refs[first : first + len(late)], refs[first + len(late)], refs[first + len(late) + 1 :]
        copies = [pltpu.make_async_copy(refs[1 + i], v, sem.at[k]) for k, (i, v) in enumerate(zip(late, stage))]
        for copy in copies:
            copy.start()
        for copy in copies:
            copy.wait()
        for i, v in zip(late, stage):
            refs[1 + i] = v
        return inner_body(*refs[:first], *own)

    return pl.pallas_call(
        body,
        out_shape=shapes,
        in_specs=[SCALARS] + [FAR_OFF if i in late else WHOLE for i in range(len(blocks))] + [FAR_OFF] * len(remote),
        out_specs=[WHOLE] * len(outs),
        scratch_shapes=staged + sems + list(scratch),
        compiler_params=pltpu.CompilerParams(vmem_limit_bytes=limit * 1024 * 1024),
        cost_estimate=pl.CostEstimate(flops=int(us * 2.3e9), bytes_accessed=int(us * 4e6), transcendentals=0),
    )(scalars, *blocks, *remote)


def fetch_start(scalars, layer, own, got, other, held, sem):
    half = held.shape[0] // 2

    @pl.when(scalars[2] == layer)
    def _():
        pltpu.make_async_copy(own, held, sem).start()

    @pl.when(scalars[2] != layer)
    def _():
        mine = pl.multiple_of(scalars[3] * half, half)
        rest = pl.multiple_of((1 - scalars[3]) * half, half)
        pltpu.make_async_copy(got, held.at[pl.ds(mine, half)], sem).start()
        pltpu.make_async_copy(other, held.at[pl.ds(rest, half)], sem).start()


def fetch_wait(own, held, sem):
    pltpu.make_async_copy(own, held, sem).wait()


def held_like(*weights):
    return [pltpu.VMEM(w[0].shape, BF) for w in weights] + [pltpu.SemaphoreType.DMA] * len(weights)


def norm_parts(v):
    centred = v - jnp.mean(v, axis=-1, keepdims=True)
    rate = lax.rsqrt(jnp.mean(centred * centred, axis=-1, keepdims=True) + 1e-05)
    return centred * rate, rate


def norm_grad(v, gain, grad):
    unit, rate = norm_parts(v)
    scaled = grad * gain
    inner = jnp.mean(scaled * unit, axis=-1, keepdims=True)
    result = rate * (scaled - jnp.mean(scaled, axis=-1, keepdims=True) - unit * inner)
    return result, jnp.sum(grad * unit, axis=0, keepdims=True), jnp.sum(grad, axis=0, keepdims=True)


def gelu_both(u):
    factor = 0.7978845608028654
    square = u * u
    t = jnp.tanh(factor * u * (1.0 + 0.044715 * square))
    half = 0.5 * (1.0 + t)
    slope = half + (0.5 * factor) * u * (1.0 - t * t) * (1.0 + (3 * 0.044715) * square)
    return u * half, slope


def project(scalars, layer, weights, table, x=None, ahead=None, carried=None):
    if ahead is None:
        rows, features = x[0].shape
        blocks = [table, *x]
    else:
        rows, features = ahead[0][1].shape
        blocks = [table, ahead[0][0], Late(carried)]
        for chunk in ahead:
            blocks.extend(chunk[1:])
    width = weights[0].shape[1] // 3

    def body(scal, tab, *refs):
        given = refs[: len(blocks) - 1]
        own, got, other = refs[len(blocks) - 1 : len(blocks) + 2]
        outs = refs[len(blocks) + 2 : -2]
        held, sem = refs[-2:]
        fetch_start(scal, layer, own, got, other, held, sem)
        for c in range(CHUNKS):
            at = slice(c * rows, (c + 1) * rows)
            if ahead is None:
                v = given[c][...].astype(F32)
            else:
                before, carry = given[:2]
                hid, mine, came = given[2 + 3 * c : 5 + 3 * c]
                y = hid[...] + before[BDOWN : BDOWN + 1] + mine[...].astype(F32) + came[...].astype(F32)
                low = y.astype(BF)
                outs[5 + c][...] = low
                v = low.astype(F32)
            unit, _ = norm_parts(v)
            normed = (unit * tab[GAIN0 : GAIN0 + 1] + tab[BIAS0 : BIAS0 + 1]).astype(BF)
            outs[c][...] = normed
            if c == 0:
                fetch_wait(own, held, sem)
            q = dot_nn(normed, held[:, :width]) + tab[BQ : BQ + 1, :width]
            outs[2 + c][...] = (q.astype(BF).astype(F32) * 0.125).astype(BF)
            kv = dot_nn(normed, held[:, width:]) + tab[BKV : BKV + 1]
            if ahead is not None:
                rolled = pltpu.roll(carry[at, :].astype(F32), width // 2, 1)
                lane = lax.broadcasted_iota(jnp.int32, kv.shape, 1)
                kv = jnp.where(lane >= width + width // 2, rolled, kv)
            outs[4][at, :] = kv.astype(BF)

    outs = [((rows, features), BF)] * 2 + [((rows, width), BF)] * 2 + [((2 * rows, 2 * width), BF)]
    if ahead is not None:
        outs += [((rows, features), BF)] * 2
    r = call(body, outs, scalars, blocks, weights, held_like(weights), us=2.5)
    return list(x) if ahead is None else r[5:], r[:2], r[2:4], r[4]


def low_lanes(shape):
    return lax.broadcasted_iota(jnp.int32, shape, 1) < HEAD


def head_of(pair, sub, fill):
    keep = low_lanes(pair.shape)
    return jnp.where(keep if sub == 0 else ~keep, pair, jnp.full_like(pair, fill))


def halves_of(ref, size):
    return tuple(ref.at[i * size : (i + 1) * size] for i in range(ref.shape[0] // size))


def spans(p, width):
    return slice(p * 128, (p + 1) * 128), slice(width + p * 128, width + (p + 1) * 128)


def scored(q, tiles, p, width, masks):
    ks, vs = spans(p, width)
    tops, outs = [], []
    for sub in range(2):
        scores = [dot_nt(q, head_of(t[:, ks], sub, 0)) for t in tiles]
        scores = [s if m is None else jnp.where(m, s, LOW) for s, m in zip(scores, masks)]
        top = scores[0].max(axis=1, keepdims=True)
        for s in scores[1:]:
            top = jnp.maximum(top, s.max(axis=1, keepdims=True))
        total = None
        for s, t in zip(scores, tiles):
            part = dot_nn(jnp.exp(s - top).astype(BF), head_of(t[:, vs], sub, 1))
            total = part if total is None else total + part
        tops.append(top)
        outs.append(total)
    low = low_lanes(outs[0].shape)
    value = jnp.where(low, outs[0], outs[1])
    amount = pltpu.roll(jnp.where(low, outs[1], outs[0]), HEAD, 1)
    return tops, value, amount


def attend_local(scalars, q, kv, near):
    size, width = q[0].shape
    rows = size * CHUNKS

    def body(scal, q0, q1, k_all, n_all, out, amount, tops):
        own = halves_of(k_all, size)
        row = lax.broadcasted_iota(jnp.int32, (size, size), 0)
        col = lax.broadcasted_iota(jnp.int32, (size, size), 1)
        causal = col <= row

        def run(extra):
            for c, q_ref in enumerate((q0, q1)):
                at = slice(c * size, (c + 1) * size)
                tiles = list(extra) + [own[i] for i in range(c + 1)]
                masks = [None] * (len(tiles) - 1) + [causal]
                for p in range(width // 128):
                    span = slice(p * 128, (p + 1) * 128)
                    top, value, total = scored(q_ref[:, span], tiles, p, width, masks)
                    out[at, span] = value
                    amount[at, span] = total
                    tops[at, 2 * p : 2 * p + 1] = top[0]
                    tops[at, 2 * p + 1 : 2 * p + 2] = top[1]

        @pl.when(scal[0] == 1)
        def _():
            run(halves_of(n_all, size))

        @pl.when(scal[0] == 0)
        def _():
            run(())

    outs = [((rows, width), F32), ((rows, width), F32), ((rows, 128), F32)]
    return call(body, outs, scalars, [*q, kv, near], us=5)


def attend_far(scalars, layer, c, q, far, out, amount, tops, weights):
    size, width = q.shape
    features = weights[0].shape[1]

    def body(scal, q_ref, fa, fb, out_ref, amount_ref, tops_ref, own, got, other, att, lse, part, stats, held, sem):
        fetch_start(scal, layer, own, got, other, held, sem)
        at = slice(c * size, (c + 1) * size)
        stats[...] = jnp.zeros_like(stats)

        def finish(p, value, total, top0, top1):
            span = slice(p * 128, (p + 1) * 128)
            att[:, span] = (value / total).astype(BF)
            logs = jnp.log(total)
            stats[:, 2 * p : 2 * p + 1] = top0 + logs[:, 0:1]
            stats[:, 2 * p + 1 : 2 * p + 2] = top1 + logs[:, HEAD : HEAD + 1]

        @pl.when(scal[1] == 0)
        def _():
            for p in range(width // 128):
                span = slice(p * 128, (p + 1) * 128)
                finish(p, out_ref[at, span], amount_ref[at, span], tops_ref[at, 2 * p : 2 * p + 1], tops_ref[at, 2 * p + 1 : 2 * p + 2])

        @pl.when(scal[1] == 1)
        def _():
            for p in range(width // 128):
                span = slice(p * 128, (p + 1) * 128)
                new, value, total = scored(q_ref[:, span], halves_of(fa, size) + halves_of(fb, size), p, width, [None] * 4)
                tops_all, olds, news = [], [], []
                for sub in range(2):
                    before = tops_ref[at, 2 * p + sub : 2 * p + sub + 1]
                    top = jnp.maximum(before, new[sub])
                    tops_all.append(top)
                    olds.append(jnp.exp(before - top))
                    news.append(jnp.exp(new[sub] - top))
                low = low_lanes(value.shape)
                keep = jnp.where(low, olds[0], olds[1])
                take = jnp.where(low, news[0], news[1])
                finish(p, out_ref[at, span] * keep + value * take, amount_ref[at, span] * keep + total * take, *tops_all)

        lse[...] = jnp.transpose(stats[...])[0:8, :]
        fetch_wait(own, held, sem)
        part[...] = dot_nn(att[...], held[...]).astype(BF)

    outs = [((size, width), BF), ((8, size), F32), ((size, features), BF)]
    scratch = [pltpu.VMEM((size, 128), F32)] + held_like(weights)
    return call(body, outs, scalars, [q, *far, out, amount, tops], weights, scratch, us=4.5)


def back_tile(p, width, q, do, lse, delta, kv, mask):
    ks, vs = spans(p, width)
    dq, dks, dvs = None, [], []
    for sub in range(2):
        h = 2 * p + sub
        key = head_of(kv[:, ks], sub, 0)
        scores = dot_nt(key, q)
        weight = jnp.exp(scores - lse[h : h + 1, :])
        if mask is not None:
            weight = jnp.where(mask, weight, 0.0)
        d_weight = dot_nt(head_of(kv[:, vs], sub, 0), do)
        d_score = (weight * (d_weight - delta[h : h + 1, :])).astype(BF)
        dvs.append(dot_nn(weight.astype(BF), do))
        dks.append(dot_nn(d_score, q))
        d = dot_tn(d_score, key)
        dq = d if dq is None else dq + d
    low = low_lanes(dks[0].shape)
    return dq, jnp.where(low, dks[0], dks[1]), jnp.where(low, dvs[0], dvs[1])


def staged(size, width):
    rows = size * CHUNKS
    return [pltpu.VMEM((rows, width), BF), pltpu.VMEM((rows, width), BF), pltpu.VMEM((8, rows), F32), pltpu.VMEM((8, rows), F32)]


def stage(size, given, held):
    for k, ref in enumerate(held):
        for c in range(CHUNKS):
            at = slice(c * size, (c + 1) * size)
            if k < 2:
                ref[at, :] = given[2 * k + c][...]
            else:
                ref[:, at] = given[2 * k + c][...]


def back_over(held, width, size, sources, dq_ref):
    q, do, lse, delta = held
    for p in range(width // 128):
        ks, vs = spans(p, width)
        total = dq_ref[:, ks]
        for source, ref, start in sources:
            for i in range(CHUNKS):
                at = slice(start + i * size, start + (i + 1) * size)
                tile = source.at[i * size : (i + 1) * size]
                dq, dk, dv = back_tile(p, width, q[:, ks], do[:, ks], lse, delta, tile, None)
                total = total + dq
                ref[at, ks] = dk.astype(BF)
                ref[at, vs] = dv.astype(BF)
        dq_ref[:, ks] = total


def attend_far_back(scalars, q, do, lse, delta, far):
    size, width = q[0].shape
    rows = size * CHUNKS

    def body(scal, q0, q1, o0, o1, l0, l1, d0, d1, fa, fb, dq_out, mine, others, *held):
        dq_out[...] = jnp.zeros_like(dq_out)

        @pl.when(scal[1] == 1)
        def _():
            stage(size, (q0, q1, o0, o1, l0, l1, d0, d1), held)
            back_over(held, width, size, [(fb, others, 0), (fa, mine, 0)], dq_out)

        @pl.when(scal[1] == 0)
        def _():
            mine[...] = jnp.zeros_like(mine)
            others[...] = jnp.zeros_like(others)

    outs = [((rows, width), F32), ((rows, 2 * width), BF), ((rows, 2 * width), BF)]
    blocks = [*map(Late, q), *do, *map(Late, lse), *delta, *map(Late, far)]
    return call(body, outs, scalars, blocks, (), staged(size, width), us=12)


def attend_near_back(scalars, q, do, lse, delta, near, dq_before, others):
    size, width = q[0].shape
    rows = size * CHUNKS

    def body(scal, q0, q1, o0, o1, l0, l1, d0, d1, n_all, before, passed, dq_out, crossing, *held):
        dq_out[...] = before[...]
        crossing[:rows, :] = passed[...]

        @pl.when(scal[0] == 1)
        def _():
            stage(size, (q0, q1, o0, o1, l0, l1, d0, d1), held)
            back_over(held, width, size, [(n_all, crossing, rows)], dq_out)

        @pl.when(scal[0] == 0)
        def _():
            crossing[rows:, :] = jnp.zeros((rows, 2 * width), BF)

    outs = [((rows, width), F32), ((2 * rows, 2 * width), BF)]
    blocks = [*map(Late, q), *do, *map(Late, lse), *delta, Late(near), dq_before, others]
    return call(body, outs, scalars, blocks, (), staged(size, width), us=6)


def attend_own_back(scalars, q, do, lse, delta, kv, dq_before):
    size, width = q[0].shape
    rows = size * CHUNKS

    def body(scal, q0, q1, o0, o1, l0, l1, d0, d1, k_all, before, dq0, dq1, dk0, dk1, *held):
        stage(size, (q0, q1, o0, o1, l0, l1, d0, d1), held)
        qs, dos, lses, deltas = held
        key = lax.broadcasted_iota(jnp.int32, (size, rows), 0)
        query = lax.broadcasted_iota(jnp.int32, (size, rows), 1)
        causal = key <= query
        for p in range(width // 128):
            ks, vs = spans(p, width)
            k0, k1 = halves_of(k_all, size)
            first, dk, dv = back_tile(p, width, qs[:, ks], dos[:, ks], lses, deltas, k0, causal)
            dk0[:, ks] = dk
            dk0[:, vs] = dv
            late = [ref.at[:, size:rows] for ref in (lses, deltas)]
            second, dk, dv = back_tile(p, width, qs[size:, ks], dos[size:, ks], *late, k1, causal[:, :size])
            dk1[:, ks] = dk
            dk1[:, vs] = dv
            dq0[:, ks] = ((before[:size, ks] + first[:size]) * 0.125).astype(BF)
            dq1[:, ks] = ((before[size:, ks] + first[size:] + second) * 0.125).astype(BF)

    outs = [((size, width), BF)] * 2 + [((size, 2 * width), F32)] * 2
    blocks = [*map(Late, q), *do, *map(Late, lse), *delta, Late(kv), dq_before]
    return call(body, outs, scalars, blocks, (), staged(size, width), us=6)


def feed_forward(scalars, layer, table, x, mine, came, up, down):
    rows, features = x.shape
    inner = up[0].shape[1]

    def body(scal, tab, x_ref, mine_ref, came_ref, u_own, u_got, u_other, d_own, d_got, d_other,
             hidden, mlp_in, active, slope, part, up_held, down_held, up_sem, down_sem):
        fetch_start(scal, layer, u_own, u_got, u_other, up_held, up_sem)
        fetch_start(scal, layer, d_own, d_got, d_other, down_held, down_sem)
        h = x_ref[...].astype(F32) + (mine_ref[...].astype(F32) + came_ref[...].astype(F32)) + tab[BO : BO + 1]
        hidden[...] = h
        unit, _ = norm_parts(h)
        low = (unit * tab[GAIN1 : GAIN1 + 1] + tab[BIAS1 : BIAS1 + 1]).astype(BF)
        mlp_in[...] = low
        fetch_wait(u_own, up_held, up_sem)
        for j in range(inner // features):
            cols = slice(j * features, (j + 1) * features)
            value, grad = gelu_both(dot_nn(low, up_held[:, cols]) + tab[BUP + j : BUP + j + 1])
            active[:, cols] = value.astype(BF)
            slope[:, cols] = grad.astype(BF)
        fetch_wait(d_own, down_held, down_sem)
        part[...] = dot_nn(active[...], down_held[...]).astype(BF)

    outs = [((rows, features), F32), ((rows, features), BF), ((rows, inner), BF), ((rows, inner), BF), ((rows, features), BF)]
    return call(body, outs, scalars, [table, Late(x), mine, came], [*up, *down], held_like(up, down), us=4, limit=24)


def feed_back(scalars, layer, dy, slope, up, down):
    rows, features = dy.shape
    inner = up[0].shape[1]

    def body(scal, dy_ref, slope_ref, u_own, u_got, u_other, d_own, d_got, d_other,
             d_up, part, sums, up_held, down_held, up_sem, down_sem):
        fetch_start(scal, layer, d_own, d_got, d_other, down_held, down_sem)
        fetch_start(scal, layer, u_own, u_got, u_other, up_held, up_sem)
        sums[...] = jnp.zeros_like(sums)
        fetch_wait(d_own, down_held, down_sem)
        for j in range(inner // features):
            cols = slice(j * features, (j + 1) * features)
            grad = (dot_nt(dy_ref[...], down_held[cols, :]) * slope_ref[:, cols].astype(F32)).astype(BF)
            d_up[:, cols] = grad
            sums[j : j + 1, :] = jnp.sum(grad.astype(F32), axis=0, keepdims=True)
        fetch_wait(u_own, up_held, up_sem)
        part[...] = dot_nt(d_up[...], up_held[...]).astype(BF)

    outs = [((rows, inner), BF), ((rows, features), BF), ((8, features), F32)]
    return call(body, outs, scalars, [dy, Late(slope)], [*up, *down], held_like(up, down), us=4.5, limit=24)


def middle_back(scalars, layer, table, hidden, mine, came, dy, attended, weights):
    rows, features = hidden.shape
    width = attended.shape[1]

    def body(scal, tab, hid, mine_ref, came_ref, dy_ref, att, own, got, other, dh_ref, low_ref, da_ref, delta, sums, stats, held, sem):
        fetch_start(scal, layer, own, got, other, held, sem)
        grad = mine_ref[...].astype(F32) + came_ref[...].astype(F32)
        back, d_gain, d_bias = norm_grad(hid[...], tab[GAIN1 : GAIN1 + 1], grad)
        up = dy_ref[...].astype(F32)
        dh = up + back
        dh_ref[...] = dh
        low = dh.astype(BF)
        low_ref[...] = low
        sums[...] = jnp.zeros_like(sums)
        sums[0:1, :] = d_gain
        sums[1:2, :] = d_bias
        sums[2:3, :] = jnp.sum(dh, axis=0, keepdims=True)
        sums[3:4, :] = jnp.sum(up, axis=0, keepdims=True)
        stats[...] = jnp.zeros_like(stats)
        fetch_wait(own, held, sem)
        da = dot_nt(low, held[...]).astype(BF)
        da_ref[...] = da
        for p in range(width // 128):
            span = slice(p * 128, (p + 1) * 128)
            product = da[:, span].astype(F32) * att[:, span].astype(F32)
            first = low_lanes(product.shape)
            stats[:, 2 * p : 2 * p + 1] = jnp.sum(jnp.where(first, product, 0.0), axis=1, keepdims=True)
            stats[:, 2 * p + 1 : 2 * p + 2] = jnp.sum(jnp.where(first, 0.0, product), axis=1, keepdims=True)
        delta[...] = jnp.transpose(stats[...])[0:8, :]

    outs = [((rows, features), F32), ((rows, features), BF), ((rows, width), BF), ((8, rows), F32), ((8, features), F32)]
    scratch = [pltpu.VMEM((rows, 128), F32)] + held_like(weights)
    return call(body, outs, scalars, [table, Late(hidden), mine, came, dy, Late(attended)], weights, scratch, us=2.8)


def project_back(scalars, layer, c, dq, dkv, near, far, returned, weights):
    rows, width = dq.shape
    features = weights[0].shape[0]

    def body(scal, dq_ref, dkv_ref, near_ref, far_ref, *rest):
        back_ref = rest[0] if returned is not None else None
        own, got, other = rest[-9:-6] if returned is None else rest[-8:-5]
        outs = rest[-6:-2] if returned is None else rest[-5:-2]
        held, sem = rest[-2:]
        fetch_start(scal, layer, own, got, other, held, sem)
        at = slice(c * rows, (c + 1) * rows)
        total = dkv_ref[...] + near_ref[at, :].astype(F32) + far_ref[at, :].astype(F32)
        if returned is None:
            outs[3][...] = total
        else:
            rolled = pltpu.roll(back_ref[...], 2 * width - width // 2, 1)
            lane = lax.broadcasted_iota(jnp.int32, total.shape, 1)
            total = total + jnp.where((lane >= width) & (lane < width + width // 2), rolled, 0.0)
        low = total.astype(BF)
        outs[0][...] = low
        sums = outs[2]
        sums[...] = jnp.zeros_like(sums)
        sums[0:1, :width] = jnp.sum(dq_ref[...].astype(F32), axis=0, keepdims=True)
        sums[1:2, :] = jnp.sum(low.astype(F32), axis=0, keepdims=True)
        fetch_wait(own, held, sem)
        outs[1][...] = (dot_nt(dq_ref[...], held[:, :width]) + dot_nt(low, held[:, width:])).astype(BF)

    outs = [((rows, 2 * width), BF), ((rows, features), BF), ((8, features), F32)]
    blocks = [dq, dkv, near, far]
    if returned is None:
        outs.append(((rows, 2 * width), F32))
    else:
        blocks.append(returned)
    return call(body, outs, scalars, blocks, weights, held_like(weights), us=2.7)


def last_back(scalars, table, x, mine, came, dh):
    rows, features = x.shape

    def body(scal, tab, x_ref, mine_ref, came_ref, dh_ref, dx_ref, low_ref, sums):
        grad = mine_ref[...].astype(F32) + came_ref[...].astype(F32)
        back, d_gain, d_bias = norm_grad(x_ref[...].astype(F32), tab[GAIN0 : GAIN0 + 1], grad)
        dx = dh_ref[...] + back
        dx_ref[...] = dx
        low_ref[...] = dx.astype(BF)
        sums[...] = jnp.zeros_like(sums)
        sums[0:1, :] = d_gain
        sums[1:2, :] = d_bias

    outs = [((rows, features), F32), ((rows, features), BF), ((8, features), F32)]
    return call(body, outs, scalars, [table, Late(x), mine, came, Late(dh)], us=1.5)


def both_chunks(left, left_span, right, right_span):
    total = None
    for a, b in zip(left, right):
        d = dot_tn(a[:, left_span], b[:, right_span])
        total = d if total is None else total + d
    return total


def wide_grads(scalars, active, dy, mlp_in, d_up):
    features = dy[0].shape[1]
    inner = active[0].shape[1]
    a, half = inner // 4, features // 2
    size = a + half

    def body(scal, a0, a1, y0, y1, m0, m1, u0, u1, packed):
        for k in range(4):
            span = slice(k * a, (k + 1) * a)
            packed[k, :a, :] = both_chunks((a0, a1), span, (y0, y1), slice(None)).astype(BF)
            for i in range(2):
                part = both_chunks((m0, m1), slice(i * half, (i + 1) * half), (u0, u1), span)
                packed[k, a:, i * a : (i + 1) * a] = part.astype(BF)

    blocks = [*map(Late, active), *dy, *map(Late, mlp_in), *d_up]
    return call(body, [((4, size, features), BF)], scalars, blocks, us=3.7)[0]


def narrow_grads(scalars, normed, dq, dkv, attended, dh_low):
    features = normed[0].shape[1]
    width = dq[0].shape[1]
    rows = features // 4
    half, c = rows // 2, width // 4
    size = rows + half + c

    def body(scal, n0, n1, q0, q1, k0, k1, t0, t1, h0, h1, packed):
        every = slice(None)
        for x in range(2):
            span = slice(2 * x * rows, 2 * (x + 1) * rows)
            first = both_chunks((n0, n1), span, (q0, q1), every).astype(BF)
            second = both_chunks((n0, n1), span, (k0, k1), every).astype(BF)
            for core in range(2):
                k, at = 2 * core + x, core * rows
                packed[k, :rows, :width] = first[at : at + rows, :]
                packed[k, :rows, width:] = second[at : at + rows, :width]
                packed[k, rows : rows + half, :width] = second[at : at + half, width:]
                packed[k, rows : rows + half, width:] = second[at + half : at + rows, width:]
        out = both_chunks((t0, t1), every, (h0, h1), every).astype(BF)
        for k in range(4):
            packed[k, rows + half :, :] = out[k * c : (k + 1) * c, :]

    blocks = [*map(Late, normed), *dq, *dkv, *map(Late, attended), *map(Late, dh_low)]
    return call(body, [((4, size, features), BF)], scalars, blocks, us=2.1)[0]


def collect(scal, refs, held, sem):
    copies = []
    for i, ref in enumerate(refs):
        core = scal[3] if i < 2 else 1 - scal[3]
        section = scal[2] if i % 2 == 0 else 1 - scal[2]
        copies.append(pltpu.make_async_copy(ref, held.at[2 * core + section], sem.at[i]))
    for copy in copies:
        copy.start()
    for copy in copies:
        copy.wait()


def wide_unpack(scalars, parts, inner):
    size, features = parts[0].shape
    a, half = inner // 4, features // 2

    def body(scal, p0, p1, p2, p3, down, up, held, sem):
        collect(scal, (p0, p1, p2, p3), held, sem)
        for k in range(4):
            down[k * a : (k + 1) * a, :] = held[k, :a, :].astype(F32)
            for i in range(2):
                up[i * half : (i + 1) * half, k * a : (k + 1) * a] = held[k, a:, i * a : (i + 1) * a].astype(F32)

    outs = [((inner, features), F32), ((features, inner), F32)]
    scratch = [pltpu.VMEM((4, size, features), BF), pltpu.SemaphoreType.DMA((4,))]
    return call(body, outs, scalars, [], parts, scratch, us=5)


def narrow_unpack(scalars, parts, extras, width):
    size, features = parts[0].shape
    rows = features // 4
    half, c, own = rows // 2, width // 4, width // 2

    def body(scal, p0, p1, p2, p3, e0, e1, query, key, value, extra, out, held, pair, sem, pair_sem):
        last = [pltpu.make_async_copy(e, pair.at[i if i == 0 else 1], pair_sem.at[i]) for i, e in enumerate((e0, e1))]
        for copy in last:
            copy.start()
        collect(scal, (p0, p1, p2, p3), held, sem)
        for copy in last:
            copy.wait()
        for x in range(2):
            for core in range(2):
                k, at = 2 * core + x, (2 * x + core) * rows
                query[at : at + rows, :] = held[k, :rows, :width].astype(F32)
                key[at : at + rows, :] = held[k, :rows, width:].astype(F32)
                value[at : at + half, :] = held[k, rows : rows + half, :own].astype(F32)
                value[at + half : at + rows, :] = held[k, rows : rows + half, width : width + own].astype(F32)
        for k in range(4):
            out[k * c : (k + 1) * c, :] = held[k, rows + half :, :].astype(F32)
        for i in range(2):
            core = scal[3] if i == 0 else 1 - scal[3]
            at = pl.multiple_of(core * rows, rows)
            cut = pair[i].astype(F32)
            left = pltpu.roll(cut[:, :width], own, 1)
            right = pltpu.roll(cut[:, width:], own, 1)
            extra[pl.ds(at, half), :] = left[:, :own]
            extra[pl.ds(pl.multiple_of(at + half, 8), half), :] = right[:, :own]

    outs = [((features, width), F32)] * 2 + [((features, own), F32), ((2 * rows, own), F32), ((width, features), F32)]
    scratch = [
        pltpu.VMEM((4, size, features), BF), pltpu.VMEM((2, half, features), BF),
        pltpu.SemaphoreType.DMA((4,)), pltpu.SemaphoreType.DMA((2,)),
    ]
    return call(body, outs, scalars, [], list(parts) + list(extras), scratch, us=3)


def swap(value, axis, bits=1):
    count = lax.axis_size(axis)
    return lax.ppermute(value, axis, [(i, i ^ bits) for i in range(count)])


def shift(value, steps):
    count = lax.axis_size("batch")
    first, last = max(0, -steps), min(count, count - steps)
    return lax.ppermute(value, "batch", [(i, i + steps) for i in range(first, last)])


def after(value, *earlier):
    return lax.optimization_barrier((value,) + earlier)[0]


def take(array, index, axis=0):
    return lax.dynamic_index_in_dim(array, index, axis, keepdims=False)


def paired(mine, other, side):
    return jnp.where(side == 0, mine, other), jnp.where(side == 0, other, mine)


class Reduction:
    def __init__(self, parts):
        self.core = lax.axis_index("batch") % 2
        self.section = lax.axis_index("section")
        self.parts = parts.reshape((2, 2) + parts.shape[1:])

    def over_cores(self):
        self.near = swap(take(self.parts, 1 - self.core), "batch")
        return self.near

    def prepare(self):
        mine = take(self.parts, self.core)
        other = 1 - self.section
        self.sent = (take(mine, other).astype(F32) + take(self.near, other).astype(F32)).astype(BF)
        self.kept = (take(mine, self.section).astype(F32) + take(self.near, self.section).astype(F32)).astype(BF)

    def over_sections(self):
        self.came = swap(self.sent, "section")

    def scatter(self):
        self.bits = list(range(1, lax.axis_size("batch").bit_length() - 1))
        index = lax.axis_index("batch")
        part = (self.kept.astype(F32) + self.came.astype(F32)).astype(BF)
        for bit in self.bits[:-1]:
            side = (index >> bit) & 1
            cut = part.reshape((2, part.shape[0] // 2) + part.shape[1:])
            if bit > 1:
                cut = lax.optimization_barrier(cut)
            got = swap(take(cut, 1 - side), "batch", 1 << bit)
            part = (take(cut, side), got)
            if bit != self.bits[-2]:
                part = (part[0].astype(F32) + part[1].astype(F32)).astype(BF)
        self.part = part
        return part

    def exchange(self):
        part = self.part
        self.part = (part[0].astype(F32) + part[1].astype(F32)).astype(BF)
        self.over = swap(self.part, "batch", 1 << self.bits[-1])

    def gather(self):
        part = (self.part.astype(F32) + self.over.astype(F32)).astype(BF)
        index = lax.axis_index("batch")
        for bit in reversed(self.bits[:-1]):
            got = swap(part, "batch", 1 << bit)
            self.pair = (part, got, (index >> bit) & 1)
            part = jnp.concatenate(paired(*self.pair), axis=0)
        return part

    def finish(self):
        self.quarter = jnp.concatenate(paired(*self.pair), axis=0)


def tie(value, *others):
    return lax.optimization_barrier((value,) + others)


def forward_layer(scalars, layer, table, w, x=None, ahead=None, carried=None, hooks=None):
    hooks = hooks or {}
    nothing = lambda value: value
    x, normed, q, kv = project(scalars, layer, w["qkv"], table, x=x, ahead=ahead, carried=carried)
    if "projected" in hooks:
        kv = hooks["projected"](kv, q)
    far = shift(kv, 2)
    near = swap(kv, "batch")
    out, amount, tops = attend_local(scalars, q, kv, near)
    far = hooks.get("arrived", nothing)(after(far, out))
    far = [far, swap(far, "batch")]
    att, lse, parts, came = [], [], [], []
    for c in range(CHUNKS):
        a, l, part = attend_far(scalars, layer, c, q[c], far, out, amount, tops, w["out"])
        att.append(a)
        lse.append(l)
        parts.append(part)
        came.append(swap(part, "tensor"))
    came[0] = hooks.get("far", lambda came, part: came)(came[0], parts[-1])
    hidden, mlp_in, active, slope, results = [], [], [], [], []
    for c in range(CHUNKS):
        h, m, a, s, part = feed_forward(scalars, layer, table, x[c], parts[c], came[c], w["up"], w["down"])
        hidden.append(h)
        mlp_in.append(m)
        active.append(a)
        slope.append(s)
        results.append((table, h, part))
    kept = dict(x=x, normed=normed, q=q, kv=kv, near=near, far=far, att=att, lse=lse, hidden=hidden,
                mlp_in=mlp_in, active=active, slope=slope)
    return results, kept


def backward_layer(scalars, layer, table, w, kept, dy, returned, steps):
    rows = CHUNKS * dy[0].shape[0]
    dy = steps("start", dy)
    d_up, parts, up_sums = [], [], []
    for c in range(CHUNKS):
        grad, part, sums = feed_back(scalars, layer, dy[c], kept["slope"][c], w["up"], w["down"])
        d_up.append(grad)
        up_sums.append(sums)
        parts.append((part, swap(part, "tensor")))
    wide = Reduction(wide_grads(scalars, kept["active"], dy, kept["mlp_in"], d_up))
    parts = steps("fed", parts, wide)
    dh, dh_low, d_att, delta, mid_sums = [], [], [], [], []
    for c in range(CHUNKS):
        r = middle_back(scalars, layer, table, kept["hidden"][c], *parts[c], dy[c], kept["att"][c], w["out"])
        for held, value in zip((dh, dh_low, d_att, delta, mid_sums), r):
            held.append(value)
    d_att = steps("mid", d_att, wide)
    dq, mine, others = attend_far_back(scalars, kept["q"], d_att, kept["lse"], delta, kept["far"])
    dq = steps("between", dq, wide)
    dq, crossing = attend_near_back(scalars, kept["q"], d_att, kept["lse"], delta, kept["near"], dq, others)
    came = swap(crossing, "batch")
    total, near = (mine.astype(F32) + came[:rows].astype(F32)).astype(BF), came[rows:]
    total, dq = steps("far", (total, dq), wide)
    home = shift(total, -2)
    dq0, dq1, dk0, dk1 = attend_own_back(scalars, kept["q"], d_att, kept["lse"], delta, kept["kv"], dq)
    dq, dkv = [dq0, dq1], [dk0, dk1]
    home, dq = steps("near", (home, dq), wide)
    dkv_low, parts, in_sums, back = [], [], [], []
    for c in range(CHUNKS):
        again = None if returned is None else returned[c]
        r = project_back(scalars, layer, c, dq[c], dkv[c], near, home, again, w["qkv"])
        dkv_low.append(r[0])
        parts.append((r[1], swap(r[1], "tensor")))
        in_sums.append(r[2])
        back.extend(r[3:])
    narrow = Reduction(narrow_grads(scalars, kept["normed"], dq, dkv_low, kept["att"], dh_low))
    parts = steps("proj", parts, wide, narrow)
    dx, dx_low, last_sums = [], [], []
    for c in range(CHUNKS):
        if c == 1:
            parts[1] = steps("last", parts[1], wide, narrow)
        r = last_back(scalars, table, kept["x"][c], *parts[c], dh[c])
        dx.append(r[0])
        dx_low.append(r[1])
        last_sums.append(r[2])
    up, mid, last, inn = [a + b for a, b in (up_sums, mid_sums, last_sums, in_sums)]
    blank = jnp.zeros((TABLE - BUP - 2, up.shape[1]), F32)
    small = jnp.concatenate(
        [last[0:1], mid[0:1], last[1:2], mid[1:2], mid[2:4], inn[0:2], up[0:2], blank], axis=0
    )
    return dx, dx_low, back, wide, narrow, small


def local(
    tokens, block_place, cotangent, norm_gains, norm_biases, query_key, query_bias, value_own, value_bias,
    value_extra, out_weight, out_bias, up_weight, up_bias, down_weight, down_bias,
):
    section = lax.axis_index("section")
    tensor = lax.axis_index("tensor")
    core = lax.axis_index("batch") % 2
    micros, _, half_rows, features = tokens.shape
    width = query_bias.shape[1]
    own_width = value_own.shape[2]
    inner = up_weight.shape[2]
    assert micros == 2 and lax.axis_size("section") == 2 and lax.axis_size("tensor") == 2
    assert 2 * own_width == width and 2 * width == features and inner == 2 * features

    place = take(block_place, section)[0]
    scalars = jnp.stack([place & 1, place >> 1, section, core]).astype(jnp.int32)

    my_tokens = take(tokens, section)[0]
    x = paired(my_tokens, swap(my_tokens, "tensor"), tensor)

    def row(*pieces):
        flat = jnp.concatenate([p.reshape(-1) for p in pieces])
        return jnp.pad(flat, (0, features - flat.shape[0]))[None]

    blank = jnp.zeros((width,), F32)
    own_table = jnp.concatenate(
        [norm_gains[0], norm_biases[0], out_bias, down_bias, row(query_bias[0]), row(blank, value_bias[0]),
         up_bias[0].reshape(2, features), jnp.zeros((TABLE - BUP - 2, features), F32)], axis=0
    )
    extra = jnp.where(section == 0, value_extra, jnp.zeros_like(value_extra))
    pieces = [query_key[0].reshape(features, 2 * width), value_own[0], extra]

    def half_of(weight):
        return take(weight.reshape((2, weight.shape[0] // 2) + weight.shape[1:]), core)

    qkv_half = jnp.concatenate([half_of(p) for p in pieces], axis=1)
    qkv = jnp.concatenate(pieces, axis=1)
    other_table = swap(own_table, "section")
    qkv_got = swap(qkv_half, "section")
    out_got = swap(half_of(out_weight[0]), "section")
    tables = paired(own_table, other_table, section)
    qkv_got, out_got, qkv, scalars, *rest = tie(qkv_got, out_got, qkv, scalars, *tables, *x)
    tables, x = rest[:2], rest[2:]
    qkv_other = swap(qkv_got, "batch")
    w = dict(qkv=(qkv, qkv_got, qkv_other))
    late = dict(
        up=swap(after(half_of(up_weight[0]), qkv_got), "section"),
        down=swap(after(half_of(down_weight[0]), qkv_got), "section"),
    )

    def on_projected(kv, q):
        mine, kv = tie(take(cotangent, section)[0], kv)
        late["dy"] = mine, swap(mine, "tensor")
        w["out"] = (out_weight[0], out_got, swap(after(out_got, kv), "batch"))
        return kv

    def on_arrived(far):
        mine, other = late["dy"]
        far, got, other = tie(far, late["up"], other)
        late["dy"] = paired(mine, other, tensor)
        w["up"] = (up_weight[0], got, swap(got, "batch"))
        return far

    def on_far(came, part):
        came, got = tie(came, late["down"], part)[:2]
        w["down"] = (down_weight[0], got, swap(got, "batch"))
        return came

    first, kept0 = forward_layer(
        scalars, 0, tables[0], w, x=x, hooks=dict(projected=on_projected, arrived=on_arrived, far=on_far)
    )
    first = [r + (swap(r[2], "tensor"),) for r in first]
    second, kept1 = forward_layer(scalars, 1, tables[1], w, ahead=first, carried=kept0["kv"])
    y0 = kept1["x"]

    def my_half(chunks):
        return jnp.where(tensor == 0, chunks[0], chunks[1])

    def by_section(mine0, mine1, kind):
        mine = jnp.where(section == 0, mine0, mine1)
        other = swap(jnp.where(section == 0, mine1, mine0).astype(kind), "section")
        return mine, other

    def steps1(number, values, wide=None, narrow=None):
        leaves, tree = jax.tree.flatten(values)
        if number == "fed":
            *leaves, wide.parts = tie(*leaves, wide.parts)
            wide.over_cores()
        if number == "mid":
            *leaves, wide.near = tie(*leaves, wide.near)
            wide.prepare()
            *leaves, wide.sent = tie(*leaves, wide.sent)
            wide.over_sections()
        if number == "near":
            *leaves, wide.came = tie(*leaves, wide.came)
            wide.scatter()
        if number == "proj":
            kept, got = wide.part
            *leaves, narrow.parts, got = tie(*leaves, narrow.parts, got)
            wide.part = kept, got
            narrow.over_cores()
        if number == "last":
            *leaves, narrow.near = tie(*leaves, narrow.near)
        return jax.tree.unflatten(tree, leaves)

    dx1, dx1_low, back, wide1, narrow1, small1 = backward_layer(scalars, 1, tables[1], w, kept1, late["dy"], None, steps1)

    def steps0(number, values, wide=None, narrow=None):
        leaves, tree = jax.tree.flatten(values)
        if number == "start":
            wide1.exchange()
            narrow1.prepare()
            *leaves, wide1.part, narrow1.sent = tie(*leaves, wide1.part, narrow1.sent)
            wide1.over = swap(wide1.part, "batch", 1 << wide1.bits[-1])
            narrow1.over_sections()
        if number == "fed":
            *leaves, wide.parts, narrow1.came, wide1.over = tie(*leaves, wide.parts, narrow1.came, wide1.over)
            wide.over_cores()
            narrow1.scatter()
            wide1.gather()
        if number == "mid":
            *leaves, wide.near = tie(*leaves, wide.near)
            wide.prepare()
            *leaves, wide.sent = tie(*leaves, wide.sent)
            wide.over_sections()
        if number == "between":
            mine, got, side = wide1.pair
            kept, came = narrow1.part
            *leaves, got, came = tie(*leaves, got, came)
            wide1.pair = mine, got, side
            narrow1.part = kept, came
        if number == "near":
            *leaves, wide.came = tie(*leaves, wide.came)
            wide.scatter()
        if number == "proj":
            kept, got = wide.part
            *leaves, narrow.parts, got = tie(*leaves, narrow.parts, got)
            wide.part = kept, got
            narrow.over_cores()
            wide.exchange()
        if number == "last":
            *leaves, narrow.near = tie(*leaves, narrow.near)
            narrow.prepare()
        return jax.tree.unflatten(tree, leaves)

    dx0, dx0_low, _, wide0, narrow0, small0 = backward_layer(scalars, 0, tables[0], w, kept0, dx1_low, back, steps0)
    sums = jnp.stack([small0, small1])
    y_parts = [r[2] for r in second]
    grads = [my_half(dx0), my_half(dx1)]
    sums, narrow0.sent, *y_parts = tie(sums, narrow0.sent, *y_parts)
    narrow0.over_sections()
    narrow1.exchange()
    y_came = [swap(y, "tensor") for y in y_parts]
    sums = sums + swap(sums, "batch")
    sums, narrow0.came, wide0.over = tie(sums, narrow0.came, wide0.over)
    narrow0.scatter()
    wide0.gather()
    mine, got, side = wide0.pair
    kept, came = narrow0.part
    mine_grads, other_grads = by_section(*grads, BF)
    table = take(sums, section) + swap(take(sums, 1 - section), "section")
    narrow1.gather()
    table, got, came, other_grads, *y_came = tie(table, got, came, other_grads, *y_came)
    wide0.pair = mine, got, side
    narrow0.part = kept, came
    narrow0.exchange()
    wide0.finish()
    wide1.finish()
    y1 = my_half(
        [(r[1] + r[0][BDOWN : BDOWN + 1] + r[2].astype(F32) + c.astype(F32)).astype(BF) for r, c in zip(second, y_came)]
    )
    mine_out, other_out = by_section(my_half(y0), y1, BF)
    for bit in range(1, lax.axis_size("batch").bit_length() - 1):
        table = table + swap(table, "batch", 1 << bit)
    wide_mine = jnp.where(section == 0, wide0.quarter, wide1.quarter)
    wide_other = swap(jnp.where(section == 0, wide1.quarter, wide0.quarter), "section")
    narrow0.over, table, other_out = tie(narrow0.over, table, other_out)
    narrow0.gather()
    narrow0.finish()
    narrow1.finish()
    outputs = jnp.stack(paired(mine_out, other_out, section))
    input_grads = jnp.stack(paired(mine_grads.astype(F32), other_grads.astype(F32), section))

    def gathered(first, second):
        mine = jnp.where(section == 0, first, second)
        other = swap(jnp.where(section == 0, second, first), "section")
        return mine, other, swap(mine, "batch"), swap(other, "batch")

    wide_all = (wide_mine, wide_other, swap(wide_mine, "batch"), swap(wide_other, "batch"))
    d_down, d_up = wide_unpack(scalars, wide_all, inner)
    rows = features // 4
    extra = narrow0.quarter[rows : rows + rows // 2]
    extras = (extra, swap(extra, "batch"))
    d_q, d_k, d_v, d_extra, d_out = narrow_unpack(
        scalars, gathered(narrow0.quarter, narrow1.quarter), extras, width
    )
    d_qk = jnp.stack([d_q, d_k], axis=1)
    return (
        outputs.reshape(1, micros, 1, half_rows, features),
        input_grads.reshape(1, micros, 1, half_rows, features),
        table[GAIN0 : GAIN1 + 1][None],
        table[BIAS0 : BIAS1 + 1][None],
        d_qk.reshape(1, features, 2, width),
        table[BQ : BQ + 1, :width],
        d_v[None],
        table[BKV : BKV + 1, width : width + own_width],
        d_extra,
        d_out[None],
        table[BO : BO + 1],
        d_up[None],
        table[BUP : BUP + 2].reshape(1, inner),
        d_down[None],
        table[BDOWN : BDOWN + 1],
    )


def solution(mesh):
    return jax.shard_map(
        local,
        mesh=mesh,
        in_specs=(
            P(None, "batch", "tensor", None),
            P(None, "batch"),
            P(None, "batch", "tensor", None),
            P("section", None, None),
            P("section", None, None),
            P("section", None, None, "tensor"),
            P("section", "tensor"),
            P("section", None, "tensor"),
            P("section", "tensor"),
            P(None, "tensor"),
            P("section", "tensor", None),
            P("section", None),
            P("section", None, "tensor"),
            P("section", "tensor"),
            P("section", "tensor", None),
            P("section", None),
        ),
        out_specs=(
            P("section", None, "batch", "tensor", None),
            P("section", None, "batch", "tensor", None),
            P("section", None, None),
            P("section", None, None),
            P("section", None, None, "tensor"),
            P("section", "tensor"),
            P("section", None, "tensor"),
            P("section", "tensor"),
            P("section", "tensor"),
            P("section", "tensor", None),
            P("section", None),
            P("section", None, "tensor"),
            P("section", "tensor"),
            P("section", "tensor", None),
            P("section", None),
        ),
        check_vma=False,
    )
```

```python
import jax
import jax.numpy as jnp
from jax import lax
from jax.experimental import pallas as pl
from jax.experimental.pallas import tpu as pltpu
from jax.sharding import PartitionSpec as P

F32 = jnp.float32
BF = jnp.bfloat16
LOW = -1e30
HEAD = 64
CHUNKS = 2

GAIN0, GAIN1, BIAS0, BIAS1, BO, BDOWN, BQ, BKV, BUP = range(9)
TABLE = 16

WHOLE = pl.BlockSpec(memory_space=pltpu.VMEM)
SCALARS = pl.BlockSpec(memory_space=pltpu.SMEM)
FAR_OFF = pl.BlockSpec(memory_space=pltpu.HBM)


def dot_nn(a, b):
    return lax.dot_general(a, b, (((1,), (0,)), ((), ())), preferred_element_type=F32)


def dot_nt(a, b):
    return lax.dot_general(a, b, (((1,), (1,)), ((), ())), preferred_element_type=F32)


def dot_tn(a, b):
    return lax.dot_general(a, b, (((0,), (0,)), ((), ())), preferred_element_type=F32)


class Late:
    def __init__(self, array):
        self.array = array


def in_hbm(array):
    return pltpu.with_memory_space_constraint(array, pltpu.HBM)


FLUSH = []


def flush(*refs):
    for ref in refs:
        for k, (held, copy, started) in enumerate(FLUSH[-1]):
            if held is ref and not started:
                copy.start()
                FLUSH[-1][k] = (held, copy, True)


LATER, RAW = 1, 2


def call(inner_body, outs, scalars, blocks, remote=(), scratch=(), us=1.0, limit=48):
    shapes = [pltpu.HBM(o[0], o[1]) if len(o) > 2 else jax.ShapeDtypeStruct(o[0], o[1]) for o in outs]
    kinds = [o[2] if len(o) > 2 else 0 for o in outs]
    late = [i for i, b in enumerate(blocks) if isinstance(b, Late)]
    blocks = [in_hbm(b.array) if isinstance(b, Late) else b for b in blocks]
    remote = [in_hbm(r) for r in remote]
    n_in, n_out = 1 + len(blocks) + len(remote), len(outs)
    later = [i for i, kind in enumerate(kinds) if kind == LATER]
    spare = [pltpu.VMEM(blocks[i].shape, blocks[i].dtype) for i in late]
    spare += [pltpu.VMEM(shapes[i].shape, shapes[i].dtype) for i in later]
    sems = [pltpu.SemaphoreType.DMA((max(len(late), 1),)), pltpu.SemaphoreType.DMA((max(len(later), 1),))]

    def body(*refs):
        refs = list(refs)
        first = n_in + n_out
        n_spare = len(spare)
        held, (sem, out_sem), own = refs[first : first + n_spare], refs[first + n_spare : first + n_spare + 2], refs[first + n_spare + 2 :]
        copies = [pltpu.make_async_copy(refs[1 + i], v, sem.at[k]) for k, (i, v) in enumerate(zip(late, held))]
        back = [
            pltpu.make_async_copy(v, refs[n_in + i], out_sem.at[k])
            for k, (i, v) in enumerate(zip(later, held[len(late) :]))
        ]
        for copy in copies:
            copy.start()
        for copy in copies:
            copy.wait()
        for i, v in zip(late, held):
            refs[1 + i] = v
        for i, v in zip(later, held[len(late) :]):
            refs[n_in + i] = v
        FLUSH.append([(held[len(late) + k], copy, False) for k, copy in enumerate(back)])
        inner_body(*refs[:first], *own)
        flush(*held[len(late) :])
        FLUSH.pop()
        for copy in back:
            copy.wait()

    return pl.pallas_call(
        body,
        out_shape=shapes,
        in_specs=[SCALARS] + [FAR_OFF if i in late else WHOLE for i in range(len(blocks))] + [FAR_OFF] * len(remote),
        out_specs=[FAR_OFF if kind else WHOLE for kind in kinds],
        scratch_shapes=spare + sems + list(scratch),
        compiler_params=pltpu.CompilerParams(vmem_limit_bytes=limit * 1024 * 1024),
        cost_estimate=pl.CostEstimate(flops=int(us * 1.2e8), bytes_accessed=int(us * 2e5), transcendentals=0),
    )(scalars, *blocks, *remote)


def fetch_start(scalars, layer, own, got, other, held, sem):
    half = held.shape[0] // 2

    @pl.when(scalars[2] == layer)
    def _():
        pltpu.make_async_copy(own, held, sem).start()

    @pl.when(scalars[2] != layer)
    def _():
        mine = pl.multiple_of(scalars[3] * half, half)
        rest = pl.multiple_of((1 - scalars[3]) * half, half)
        pltpu.make_async_copy(got, held.at[pl.ds(mine, half)], sem).start()
        pltpu.make_async_copy(other, held.at[pl.ds(rest, half)], sem).start()


def fetch_wait(own, held, sem):
    pltpu.make_async_copy(own, held, sem).wait()


def held_like(*weights):
    return [pltpu.VMEM(w[0].shape, BF) for w in weights] + [pltpu.SemaphoreType.DMA] * len(weights)


def norm_parts(v):
    centred = v - jnp.mean(v, axis=-1, keepdims=True)
    rate = lax.rsqrt(jnp.mean(centred * centred, axis=-1, keepdims=True) + 1e-05)
    return centred * rate, rate


def norm_grad(v, gain, grad):
    unit, rate = norm_parts(v)
    scaled = grad * gain
    inner = jnp.mean(scaled * unit, axis=-1, keepdims=True)
    result = rate * (scaled - jnp.mean(scaled, axis=-1, keepdims=True) - unit * inner)
    return result, jnp.sum(grad * unit, axis=0, keepdims=True), jnp.sum(grad, axis=0, keepdims=True)


def gelu_both(u):
    factor = 0.7978845608028654
    square = u * u
    t = jnp.tanh(factor * u * (1.0 + 0.044715 * square))
    half = 0.5 * (1.0 + t)
    slope = half + (0.5 * factor) * u * (1.0 - t * t) * (1.0 + (3 * 0.044715) * square)
    return u * half, slope


def project(scalars, layer, weights, table, x=None, ahead=None, carried=None):
    if ahead is None:
        rows, features = x[0].shape
        blocks = [table, *x]
    else:
        rows, features = ahead[0][1].shape
        blocks = [table, ahead[0][0], Late(carried)]
        for chunk in ahead:
            blocks.extend([Late(chunk[1]), *chunk[2:]])
    width = weights[0].shape[1] // 3

    def body(scal, tab, *refs):
        given = refs[: len(blocks) - 1]
        own, got, other = refs[len(blocks) - 1 : len(blocks) + 2]
        outs = refs[len(blocks) + 2 : -2]
        held, sem = refs[-2:]
        fetch_start(scal, layer, own, got, other, held, sem)
        for c in range(CHUNKS):
            at = slice(c * rows, (c + 1) * rows)
            if ahead is None:
                v = given[c][...].astype(F32)
            else:
                before, carry = given[:2]
                hid, mine, came = given[2 + 3 * c : 5 + 3 * c]
                y = hid[...] + before[BDOWN : BDOWN + 1] + mine[...].astype(F32) + came[...].astype(F32)
                low = y.astype(BF)
                outs[5 + c][...] = low
                v = low.astype(F32)
            unit, _ = norm_parts(v)
            normed = (unit * tab[GAIN0 : GAIN0 + 1] + tab[BIAS0 : BIAS0 + 1]).astype(BF)
            outs[c][...] = normed
            if c == 0:
                fetch_wait(own, held, sem)
            q = dot_nn(normed, held[:, :width]) + tab[BQ : BQ + 1, :width]
            outs[2 + c][...] = (q.astype(BF).astype(F32) * 0.125).astype(BF)
            kv = dot_nn(normed, held[:, width:]) + tab[BKV : BKV + 1]
            if ahead is not None:
                rolled = pltpu.roll(carry[at, :].astype(F32), width // 2, 1)
                lane = lax.broadcasted_iota(jnp.int32, kv.shape, 1)
                kv = jnp.where(lane >= width + width // 2, rolled, kv)
            outs[4][at, :] = kv.astype(BF)

    outs = [((rows, features), BF, LATER)] * 2 + [((rows, width), BF)] * 2 + [((2 * rows, 2 * width), BF)]
    if ahead is not None:
        outs += [((rows, features), BF, LATER)] * 2
    r = call(body, outs, scalars, blocks, weights, held_like(weights), us=2.5)
    return list(x) if ahead is None else r[5:], r[:2], r[2:4], r[4]


def low_lanes(shape):
    return lax.broadcasted_iota(jnp.int32, shape, 1) < HEAD


def head_of(pair, sub, fill):
    keep = low_lanes(pair.shape)
    return jnp.where(keep if sub == 0 else ~keep, pair, jnp.full_like(pair, fill))


def halves_of(ref, size):
    return tuple(ref.at[i * size : (i + 1) * size] for i in range(ref.shape[0] // size))


def spans(p, width):
    return slice(p * 128, (p + 1) * 128), slice(width + p * 128, width + (p + 1) * 128)


def scored(q, tiles, p, width, masks):
    ks, vs = spans(p, width)
    tops, outs = [], []
    for sub in range(2):
        scores = [dot_nt(q, head_of(t[:, ks], sub, 0)) for t in tiles]
        scores = [s if m is None else jnp.where(m, s, LOW) for s, m in zip(scores, masks)]
        top = scores[0].max(axis=1, keepdims=True)
        for s in scores[1:]:
            top = jnp.maximum(top, s.max(axis=1, keepdims=True))
        total = None
        for s, t in zip(scores, tiles):
            part = dot_nn(jnp.exp(s - top).astype(BF), head_of(t[:, vs], sub, 1))
            total = part if total is None else total + part
        tops.append(top)
        outs.append(total)
    low = low_lanes(outs[0].shape)
    value = jnp.where(low, outs[0], outs[1])
    amount = pltpu.roll(jnp.where(low, outs[1], outs[0]), HEAD, 1)
    return tops, value, amount


def attend_local(scalars, q, kv, near):
    size, width = q[0].shape
    rows = size * CHUNKS

    def body(scal, q0, q1, k_all, n_all, out, amount, tops):
        own = halves_of(k_all, size)
        row = lax.broadcasted_iota(jnp.int32, (size, size), 0)
        col = lax.broadcasted_iota(jnp.int32, (size, size), 1)
        causal = col <= row

        def run(extra):
            for c, q_ref in enumerate((q0, q1)):
                at = slice(c * size, (c + 1) * size)
                tiles = list(extra) + [own[i] for i in range(c + 1)]
                masks = [None] * (len(tiles) - 1) + [causal]
                for p in range(width // 128):
                    span = slice(p * 128, (p + 1) * 128)
                    top, value, total = scored(q_ref[:, span], tiles, p, width, masks)
                    out[at, span] = value
                    amount[at, span] = total
                    tops[at, 2 * p : 2 * p + 1] = top[0]
                    tops[at, 2 * p + 1 : 2 * p + 2] = top[1]

        @pl.when(scal[0] == 1)
        def _():
            run(halves_of(n_all, size))

        @pl.when(scal[0] == 0)
        def _():
            run(())

    outs = [((rows, width), F32), ((rows, width), F32), ((rows, 128), F32)]
    return call(body, outs, scalars, [*q, kv, near], us=5)


def attend_far(scalars, layer, c, q, far, out, amount, tops, weights):
    size, width = q.shape
    features = weights[0].shape[1]

    def body(scal, q_ref, fa, fb, out_ref, amount_ref, tops_ref, own, got, other, att, lse, part, stats, held, sem):
        fetch_start(scal, layer, own, got, other, held, sem)
        at = slice(c * size, (c + 1) * size)
        stats[...] = jnp.zeros_like(stats)

        def finish(p, value, total, top0, top1):
            span = slice(p * 128, (p + 1) * 128)
            att[:, span] = (value / total).astype(BF)
            logs = jnp.log(total)
            stats[:, 2 * p : 2 * p + 1] = top0 + logs[:, 0:1]
            stats[:, 2 * p + 1 : 2 * p + 2] = top1 + logs[:, HEAD : HEAD + 1]

        @pl.when(scal[1] == 0)
        def _():
            for p in range(width // 128):
                span = slice(p * 128, (p + 1) * 128)
                finish(p, out_ref[at, span], amount_ref[at, span], tops_ref[at, 2 * p : 2 * p + 1], tops_ref[at, 2 * p + 1 : 2 * p + 2])

        @pl.when(scal[1] == 1)
        def _():
            for p in range(width // 128):
                span = slice(p * 128, (p + 1) * 128)
                new, value, total = scored(q_ref[:, span], halves_of(fa, size) + halves_of(fb, size), p, width, [None] * 4)
                tops_all, olds, news = [], [], []
                for sub in range(2):
                    before = tops_ref[at, 2 * p + sub : 2 * p + sub + 1]
                    top = jnp.maximum(before, new[sub])
                    tops_all.append(top)
                    olds.append(jnp.exp(before - top))
                    news.append(jnp.exp(new[sub] - top))
                low = low_lanes(value.shape)
                keep = jnp.where(low, olds[0], olds[1])
                take = jnp.where(low, news[0], news[1])
                finish(p, out_ref[at, span] * keep + value * take, amount_ref[at, span] * keep + total * take, *tops_all)

        lse[...] = jnp.transpose(stats[...])[0:8, :]
        flush(att, lse)
        fetch_wait(own, held, sem)
        part[...] = dot_nn(att[...], held[...]).astype(BF)

    outs = [((size, width), BF, LATER), ((8, size), F32, LATER), ((size, features), BF)]
    scratch = [pltpu.VMEM((size, 128), F32)] + held_like(weights)
    return call(body, outs, scalars, [q, *far, out, amount, tops], weights, scratch, us=4.5)


def back_tile(p, width, q, do, lse, delta, kv, mask):
    ks, vs = spans(p, width)
    dq, dks, dvs = None, [], []
    for sub in range(2):
        h = 2 * p + sub
        key = head_of(kv[:, ks], sub, 0)
        scores = dot_nt(key, q)
        weight = jnp.exp(scores - lse[h : h + 1, :])
        if mask is not None:
            weight = jnp.where(mask, weight, 0.0)
        d_weight = dot_nt(head_of(kv[:, vs], sub, 0), do)
        d_score = (weight * (d_weight - delta[h : h + 1, :])).astype(BF)
        dvs.append(dot_nn(weight.astype(BF), do))
        dks.append(dot_nn(d_score, q))
        d = dot_tn(d_score, key)
        dq = d if dq is None else dq + d
    low = low_lanes(dks[0].shape)
    return dq, jnp.where(low, dks[0], dks[1]), jnp.where(low, dvs[0], dvs[1])


def staged(size, width):
    rows = size * CHUNKS
    return [pltpu.VMEM((rows, width), BF), pltpu.VMEM((rows, width), BF), pltpu.VMEM((8, rows), F32), pltpu.VMEM((8, rows), F32)]


def stage(size, given, held):
    for k, ref in enumerate(held):
        for c in range(CHUNKS):
            at = slice(c * size, (c + 1) * size)
            if k < 2:
                ref[at, :] = given[2 * k + c][...]
            else:
                ref[:, at] = given[2 * k + c][...]


def back_over(held, width, size, sources, dq_ref):
    q, do, lse, delta = held
    for p in range(width // 128):
        ks, vs = spans(p, width)
        total = dq_ref[:, ks]
        for source, ref, start in sources:
            for i in range(CHUNKS):
                at = slice(start + i * size, start + (i + 1) * size)
                tile = source.at[i * size : (i + 1) * size]
                dq, dk, dv = back_tile(p, width, q[:, ks], do[:, ks], lse, delta, tile, None)
                total = total + dq
                ref[at, ks] = dk.astype(BF)
                ref[at, vs] = dv.astype(BF)
        dq_ref[:, ks] = total


def attend_far_back(scalars, q, do, lse, delta, far):
    size, width = q[0].shape
    rows = size * CHUNKS

    def body(scal, q0, q1, o0, o1, l0, l1, d0, d1, fa, fb, dq_out, mine, others, *held):
        dq_out[...] = jnp.zeros_like(dq_out)

        @pl.when(scal[1] == 1)
        def _():
            stage(size, (q0, q1, o0, o1, l0, l1, d0, d1), held)
            back_over(held, width, size, [(fb, others, 0), (fa, mine, 0)], dq_out)

        @pl.when(scal[1] == 0)
        def _():
            mine[...] = jnp.zeros_like(mine)
            others[...] = jnp.zeros_like(others)

    outs = [((rows, width), F32), ((rows, 2 * width), BF), ((rows, 2 * width), BF)]
    blocks = [*map(Late, q), *do, *map(Late, lse), *delta, *map(Late, far)]
    return call(body, outs, scalars, blocks, (), staged(size, width), us=12)


def attend_near_back(scalars, q, do, lse, delta, near, dq_before):
    size, width = q[0].shape
    rows = size * CHUNKS

    def body(scal, q0, q1, o0, o1, l0, l1, d0, d1, n_all, before, dq_out, crossing, *held):
        dq_out[...] = before[...]

        @pl.when(scal[0] == 1)
        def _():
            stage(size, (q0, q1, o0, o1, l0, l1, d0, d1), held)
            back_over(held, width, size, [(n_all, crossing, 0)], dq_out)

        @pl.when(scal[0] == 0)
        def _():
            crossing[...] = jnp.zeros_like(crossing)

    outs = [((rows, width), F32), ((rows, 2 * width), BF)]
    blocks = [*map(Late, q), *do, *map(Late, lse), *delta, Late(near), dq_before]
    return call(body, outs, scalars, blocks, (), staged(size, width), us=0.2)


def attend_own_back(scalars, q, do, lse, delta, kv, dq_before):
    size, width = q[0].shape
    rows = size * CHUNKS

    def body(scal, q0, q1, o0, o1, l0, l1, d0, d1, k_all, before, dq0, dq1, dk0, dk1, *held):
        stage(size, (q0, q1, o0, o1, l0, l1, d0, d1), held)
        qs, dos, lses, deltas = held
        key = lax.broadcasted_iota(jnp.int32, (size, rows), 0)
        query = lax.broadcasted_iota(jnp.int32, (size, rows), 1)
        causal = key <= query
        for p in range(width // 128):
            ks, vs = spans(p, width)
            k0, k1 = halves_of(k_all, size)
            first, dk, dv = back_tile(p, width, qs[:, ks], dos[:, ks], lses, deltas, k0, causal)
            dk0[:, ks] = dk
            dk0[:, vs] = dv
            late = [ref.at[:, size:rows] for ref in (lses, deltas)]
            second, dk, dv = back_tile(p, width, qs[size:, ks], dos[size:, ks], *late, k1, causal[:, :size])
            dk1[:, ks] = dk
            dk1[:, vs] = dv
            dq0[:, ks] = ((before[:size, ks] + first[:size]) * 0.125).astype(BF)
            dq1[:, ks] = ((before[size:, ks] + first[size:] + second) * 0.125).astype(BF)

    outs = [((size, width), BF)] * 2 + [((size, 2 * width), F32)] * 2
    blocks = [*map(Late, q), *do, *map(Late, lse), *delta, Late(kv), dq_before]
    return call(body, outs, scalars, blocks, (), staged(size, width), us=0.2)


def feed_forward(scalars, layer, table, x, mine, came, up, down):
    rows, features = x.shape
    inner = up[0].shape[1]

    def body(scal, tab, x_ref, mine_ref, came_ref, u_own, u_got, u_other, d_own, d_got, d_other,
             hidden, mlp_in, active, slope, part, up_held, down_held, up_sem, down_sem):
        fetch_start(scal, layer, u_own, u_got, u_other, up_held, up_sem)
        fetch_start(scal, layer, d_own, d_got, d_other, down_held, down_sem)
        h = x_ref[...].astype(F32) + (mine_ref[...].astype(F32) + came_ref[...].astype(F32)) + tab[BO : BO + 1]
        hidden[...] = h
        unit, _ = norm_parts(h)
        low = (unit * tab[GAIN1 : GAIN1 + 1] + tab[BIAS1 : BIAS1 + 1]).astype(BF)
        mlp_in[...] = low
        flush(hidden, mlp_in)
        fetch_wait(u_own, up_held, up_sem)
        for j in range(inner // features):
            cols = slice(j * features, (j + 1) * features)
            value, grad = gelu_both(dot_nn(low, up_held[:, cols]) + tab[BUP + j : BUP + j + 1])
            active[:, cols] = value.astype(BF)
            slope[:, cols] = grad.astype(BF)
        flush(active, slope)
        fetch_wait(d_own, down_held, down_sem)
        part[...] = dot_nn(active[...], down_held[...]).astype(BF)

    outs = [((rows, features), F32, LATER), ((rows, features), BF, LATER), ((rows, inner), BF, LATER), ((rows, inner), BF, LATER), ((rows, features), BF)]
    return call(body, outs, scalars, [table, Late(x), mine, came], [*up, *down], held_like(up, down), us=4)


def feed_back(scalars, layer, dy, slope, up, down):
    rows, features = dy.shape
    inner = up[0].shape[1]

    def body(scal, dy_ref, slope_ref, u_own, u_got, u_other, d_own, d_got, d_other,
             d_up, part, sums, up_held, down_held, up_sem, down_sem):
        fetch_start(scal, layer, d_own, d_got, d_other, down_held, down_sem)
        fetch_start(scal, layer, u_own, u_got, u_other, up_held, up_sem)
        sums[...] = jnp.zeros_like(sums)
        fetch_wait(d_own, down_held, down_sem)
        for j in range(inner // features):
            cols = slice(j * features, (j + 1) * features)
            grad = (dot_nt(dy_ref[...], down_held[cols, :]) * slope_ref[:, cols].astype(F32)).astype(BF)
            d_up[:, cols] = grad
            sums[j : j + 1, :] = jnp.sum(grad.astype(F32), axis=0, keepdims=True)
        fetch_wait(u_own, up_held, up_sem)
        part[...] = dot_nt(d_up[...], up_held[...]).astype(BF)

    outs = [((rows, inner), BF), ((rows, features), BF), ((8, features), F32)]
    return call(body, outs, scalars, [dy, Late(slope)], [*up, *down], held_like(up, down), us=1.0)


def middle_back(scalars, layer, table, hidden, mine, came, dy, attended, weights):
    rows, features = hidden.shape
    width = attended.shape[1]

    def body(scal, tab, hid, mine_ref, came_ref, dy_ref, att, own, got, other, dh_ref, low_ref, da_ref, delta, sums, stats, held, sem):
        fetch_start(scal, layer, own, got, other, held, sem)
        grad = mine_ref[...].astype(F32) + came_ref[...].astype(F32)
        back, d_gain, d_bias = norm_grad(hid[...], tab[GAIN1 : GAIN1 + 1], grad)
        up = dy_ref[...].astype(F32)
        dh = up + back
        dh_ref[...] = dh
        low = dh.astype(BF)
        low_ref[...] = low
        flush(dh_ref, low_ref)
        sums[...] = jnp.zeros_like(sums)
        sums[0:1, :] = d_gain
        sums[1:2, :] = d_bias
        sums[2:3, :] = jnp.sum(dh, axis=0, keepdims=True)
        sums[3:4, :] = jnp.sum(up, axis=0, keepdims=True)
        stats[...] = jnp.zeros_like(stats)
        fetch_wait(own, held, sem)
        da = dot_nt(low, held[...]).astype(BF)
        da_ref[...] = da
        for p in range(width // 128):
            span = slice(p * 128, (p + 1) * 128)
            product = da[:, span].astype(F32) * att[:, span].astype(F32)
            first = low_lanes(product.shape)
            stats[:, 2 * p : 2 * p + 1] = jnp.sum(jnp.where(first, product, 0.0), axis=1, keepdims=True)
            stats[:, 2 * p + 1 : 2 * p + 2] = jnp.sum(jnp.where(first, 0.0, product), axis=1, keepdims=True)
        delta[...] = jnp.transpose(stats[...])[0:8, :]

    outs = [((rows, features), F32, LATER), ((rows, features), BF, LATER), ((rows, width), BF), ((8, rows), F32), ((8, features), F32)]
    scratch = [pltpu.VMEM((rows, 128), F32)] + held_like(weights)
    return call(body, outs, scalars, [table, Late(hidden), mine, came, dy, Late(attended)], weights, scratch, us=2.8)


def project_back(scalars, layer, c, dq, dkv, near, far, returned, weights):
    rows, width = dq.shape
    features = weights[0].shape[0]

    def body(scal, dq_ref, dkv_ref, near_ref, far_ref, *rest):
        back_ref = rest[0] if returned is not None else None
        own, got, other = rest[-9:-6] if returned is None else rest[-8:-5]
        outs = rest[-6:-2] if returned is None else rest[-5:-2]
        held, sem = rest[-2:]
        fetch_start(scal, layer, own, got, other, held, sem)
        at = slice(c * rows, (c + 1) * rows)
        total = dkv_ref[...] + near_ref[at, :].astype(F32) + far_ref[at, :].astype(F32)
        if returned is None:
            outs[3][...] = total
        else:
            rolled = pltpu.roll(back_ref[...], 2 * width - width // 2, 1)
            lane = lax.broadcasted_iota(jnp.int32, total.shape, 1)
            total = total + jnp.where((lane >= width) & (lane < width + width // 2), rolled, 0.0)
        low = total.astype(BF)
        outs[0][...] = low
        sums = outs[2]
        sums[...] = jnp.zeros_like(sums)
        sums[0:1, :width] = jnp.sum(dq_ref[...].astype(F32), axis=0, keepdims=True)
        sums[1:2, :] = jnp.sum(low.astype(F32), axis=0, keepdims=True)
        fetch_wait(own, held, sem)
        outs[1][...] = (dot_nt(dq_ref[...], held[:, :width]) + dot_nt(low, held[:, width:])).astype(BF)

    outs = [((rows, 2 * width), BF), ((rows, features), BF), ((8, features), F32)]
    blocks = [dq, dkv, near, far]
    if returned is None:
        outs.append(((rows, 2 * width), F32, LATER))
    else:
        blocks.append(Late(returned))
    return call(body, outs, scalars, blocks, weights, held_like(weights), us=2.7)


def last_back(scalars, table, x, mine, came, dh):
    rows, features = x.shape

    def body(scal, tab, x_ref, mine_ref, came_ref, dh_ref, dx_ref, low_ref, sums):
        grad = mine_ref[...].astype(F32) + came_ref[...].astype(F32)
        back, d_gain, d_bias = norm_grad(x_ref[...].astype(F32), tab[GAIN0 : GAIN0 + 1], grad)
        dx = dh_ref[...] + back
        dx_ref[...] = dx
        low_ref[...] = dx.astype(BF)
        sums[...] = jnp.zeros_like(sums)
        sums[0:1, :] = d_gain
        sums[1:2, :] = d_bias

    outs = [((rows, features), F32, LATER), ((rows, features), BF), ((8, features), F32)]
    return call(body, outs, scalars, [table, Late(x), mine, came, Late(dh)], us=0.5)


def both_chunks(left, left_span, right, right_span):
    total = None
    for a, b in zip(left, right):
        d = dot_tn(a[:, left_span], b[:, right_span])
        total = d if total is None else total + d
    return total


def hand_out(scal, packed, send, mine, sem):
    copies = [
        pltpu.make_async_copy(packed.at[pl.ds(2 * (1 - scal[3]), 2)], send, sem.at[0]),
        pltpu.make_async_copy(packed.at[pl.ds(2 * scal[3], 2)], mine, sem.at[1]),
    ]
    for copy in copies:
        copy.start()
    for copy in copies:
        copy.wait()


def wide_grads(scalars, active, dy, mlp_in, d_up):
    features = dy[0].shape[1]
    inner = active[0].shape[1]
    a, half = inner // 4, features // 2
    size = a + half

    def body(scal, a0, a1, y0, y1, m0, m1, u0, u1, send, mine, packed, sem):
        for k in range(4):
            span = slice(k * a, (k + 1) * a)
            packed[k, :a, :] = both_chunks((a0, a1), span, (y0, y1), slice(None)).astype(BF)
            for i in range(2):
                part = both_chunks((m0, m1), slice(i * half, (i + 1) * half), (u0, u1), span)
                packed[k, a:, i * a : (i + 1) * a] = part.astype(BF)
        hand_out(scal, packed, send, mine, sem)

    blocks = [*map(Late, active), *dy, *map(Late, mlp_in), *d_up]
    outs = [((2, size, features), BF, RAW)] * 2
    scratch = [pltpu.VMEM((4, size, features), BF), pltpu.SemaphoreType.DMA((2,))]
    return call(body, outs, scalars, blocks, (), scratch, us=3.7)


def narrow_grads(scalars, normed, dq, dkv, attended, dh_low):
    features = normed[0].shape[1]
    width = dq[0].shape[1]
    rows = features // 4
    half, c = rows // 2, width // 4
    size = rows + half + c

    def body(scal, n0, n1, q0, q1, k0, k1, t0, t1, h0, h1, send, mine, packed, sem):
        every = slice(None)
        for x in range(2):
            span = slice(2 * x * rows, 2 * (x + 1) * rows)
            first = both_chunks((n0, n1), span, (q0, q1), every).astype(BF)
            second = both_chunks((n0, n1), span, (k0, k1), every).astype(BF)
            for core in range(2):
                k, at = 2 * core + x, core * rows
                packed[k, :rows, :width] = first[at : at + rows, :]
                packed[k, :rows, width:] = second[at : at + rows, :width]
                packed[k, rows : rows + half, :width] = second[at : at + half, width:]
                packed[k, rows : rows + half, width:] = second[at + half : at + rows, width:]
        out = both_chunks((t0, t1), every, (h0, h1), every).astype(BF)
        for k in range(4):
            packed[k, rows + half :, :] = out[k * c : (k + 1) * c, :]
        hand_out(scal, packed, send, mine, sem)

    blocks = [*map(Late, normed), *dq, *dkv, *map(Late, attended), *map(Late, dh_low)]
    outs = [((2, size, features), BF, RAW)] * 2
    scratch = [pltpu.VMEM((4, size, features), BF), pltpu.SemaphoreType.DMA((2,))]
    return call(body, outs, scalars, blocks, (), scratch, us=2.1)


def collect(scal, parts, held, sem):
    copies = []
    for i, refs in enumerate(parts):
        core = scal[3] if i < 2 else 1 - scal[3]
        section = scal[2] if i % 2 == 0 else 1 - scal[2]
        size = held.shape[1] // len(refs)
        for j, ref in enumerate(refs):
            place = held.at[2 * core + section, j * size : (j + 1) * size]
            copies.append(pltpu.make_async_copy(ref, place, sem.at[len(copies)]))
    for copy in copies:
        copy.start()
    for copy in copies:
        copy.wait()


def wide_unpack(scalars, mine, mine2, other, other2, inner):
    size, features = mine.shape
    a, half = inner // 4, features // 2

    def body(scal, p0, p1a, p1b, p2, p3a, p3b, down, up, token, held, sem):
        collect(scal, ((p0,), (p1a, p1b), (p2,), (p3a, p3b)), held, sem)
        for k in range(4):
            down[k * a : (k + 1) * a, :] = held[k, :a, :].astype(F32)
            for i in range(2):
                up[i * half : (i + 1) * half, k * a : (k + 1) * a] = held[k, a:, i * a : (i + 1) * a].astype(F32)
        token[...] = jnp.zeros_like(token)

    outs = [((inner, features), F32), ((features, inner), F32), ((8, 128), F32)]
    scratch = [pltpu.VMEM((4, size, features), BF), pltpu.SemaphoreType.DMA((6,))]
    return call(body, outs, scalars, [], [mine, *other, mine2, *other2], scratch, us=5)


def narrow_unpack(scalars, parts, extras, width, token):
    size, features = parts[0].shape
    rows = features // 4
    half, c, own = rows // 2, width // 4, width // 2

    def body(scal, _, p0, p1, p2, p3, e0, e1, query, key, value, extra, out, held, pair, sem, pair_sem):
        last = [pltpu.make_async_copy(e, pair.at[i if i == 0 else 1], pair_sem.at[i]) for i, e in enumerate((e0, e1))]
        for copy in last:
            copy.start()
        collect(scal, ((p0,), (p1,), (p2,), (p3,)), held, sem)
        for copy in last:
            copy.wait()
        for x in range(2):
            for core in range(2):
                k, at = 2 * core + x, (2 * x + core) * rows
                query[at : at + rows, :] = held[k, :rows, :width].astype(F32)
                key[at : at + rows, :] = held[k, :rows, width:].astype(F32)
                value[at : at + half, :] = held[k, rows : rows + half, :own].astype(F32)
                value[at + half : at + rows, :] = held[k, rows : rows + half, width : width + own].astype(F32)
        for k in range(4):
            out[k * c : (k + 1) * c, :] = held[k, rows + half :, :].astype(F32)
        for i in range(2):
            core = scal[3] if i == 0 else 1 - scal[3]
            at = pl.multiple_of(core * rows, rows)
            cut = pair[i].astype(F32)
            left = pltpu.roll(cut[:, :width], own, 1)
            right = pltpu.roll(cut[:, width:], own, 1)
            extra[pl.ds(at, half), :] = left[:, :own]
            extra[pl.ds(pl.multiple_of(at + half, 8), half), :] = right[:, :own]

    outs = [((features, width), F32)] * 2 + [((features, own), F32), ((2 * rows, own), F32), ((width, features), F32)]
    scratch = [
        pltpu.VMEM((4, size, features), BF), pltpu.VMEM((2, half, features), BF),
        pltpu.SemaphoreType.DMA((4,)), pltpu.SemaphoreType.DMA((2,)),
    ]
    return call(body, outs, scalars, [token], list(parts) + list(extras), scratch, us=3)


def swap(value, axis, bits=1):
    count = lax.axis_size(axis)
    return lax.ppermute(value, axis, [(i, i ^ bits) for i in range(count)])


def shift(value, steps):
    count = lax.axis_size("batch")
    first, last = max(0, -steps), min(count, count - steps)
    return lax.ppermute(value, "batch", [(i, i + steps) for i in range(first, last)])


def after(value, *earlier):
    return lax.optimization_barrier((value,) + earlier)[0]


def take(array, index, axis=0):
    return lax.dynamic_index_in_dim(array, index, axis, keepdims=False)


def paired(mine, other, side):
    return jnp.where(side == 0, mine, other), jnp.where(side == 0, other, mine)


class Reduction:
    def __init__(self, grads, pieces):
        self.section = lax.axis_index("section")
        self.send, self.mine = grads
        self.pieces = pieces

    def over_cores(self):
        self.near = swap(self.send, "batch")

    def pair_sum(self, section, start, size):
        cut = [lax.dynamic_slice(a, (section, start, 0), (1, size, a.shape[2]))[0] for a in (self.mine, self.near)]
        return cut[0].astype(F32) + cut[1].astype(F32)

    def prepare(self):
        size = self.mine.shape[1] // self.pieces
        self.sent = [self.pair_sum(1 - self.section, i * size, size).astype(BF) for i in range(self.pieces)]

    def over_sections(self, i=0):
        if i == 0:
            self.came = []
        self.came.append(swap(self.sent[i], "section"))

    def scatter_send(self):
        index = lax.axis_index("batch")
        half = self.mine.shape[1] // 2
        came = self.came if self.pieces == 2 else [self.came[0][:half], self.came[0][half:]]
        cut = [(self.pair_sum(self.section, i * half, half) + came[i].astype(F32)).astype(BF) for i in range(2)]
        *first, near, far = chip_bits()
        for bit in first:
            keep, send = paired(*cut, (index >> bit) & 1)
            total = (keep.astype(F32) + swap(send, "batch", 1 << bit).astype(F32)).astype(BF)
            cut = jnp.split(total, 2, axis=0)
        self.keep, send = paired(*cut, (index >> near) & 1)
        return send

    def exchange_send(self, got):
        self.part = (self.keep.astype(F32) + got.astype(F32)).astype(BF)
        return self.part

    def gather_send(self, got):
        self.part = (self.part.astype(F32) + got.astype(F32)).astype(BF)
        return self.part

    def finish(self, got):
        index = lax.axis_index("batch")
        *first, near, far = chip_bits()
        part = jnp.concatenate(paired(self.part, got, (index >> near) & 1), axis=0)
        for bit in reversed(first):
            part = jnp.concatenate(paired(part, swap(part, "batch", 1 << bit), (index >> bit) & 1), axis=0)
        self.quarter = part


def chip_bits():
    return list(range(1, lax.axis_size("batch").bit_length() - 1))


def swap_all(values, place):
    sizes = [v.shape[0] for v in values]
    got = swap(jnp.concatenate(values, axis=0) if len(values) > 1 else values[0], "batch", 1 << chip_bits()[place])
    ends = [sum(sizes[: i + 1]) for i in range(len(sizes))]
    return [got[end - size : end] for size, end in zip(sizes, ends)]


def tie(value, *others):
    return lax.optimization_barrier((value,) + others)


def forward_layer(scalars, layer, table, w, x=None, ahead=None, carried=None, hooks=None):
    hooks = hooks or {}
    nothing = lambda value: value
    x, normed, q, kv = project(scalars, layer, w["qkv"], table, x=x, ahead=ahead, carried=carried)
    if "projected" in hooks:
        kv = hooks["projected"](kv, q)
    far = shift(kv, 2)
    near = swap(kv, "batch")
    out, amount, tops = attend_local(scalars, q, kv, near)
    far = hooks.get("arrived", nothing)(after(far, out))
    far = [far, swap(far, "batch")]
    att, lse, parts, came = [], [], [], []
    for c in range(CHUNKS):
        a, l, part = attend_far(scalars, layer, c, q[c], far, out, amount, tops, w["out"])
        att.append(a)
        lse.append(l)
        parts.append(part)
        came.append(swap(part, "tensor"))
    came = hooks.get("far", nothing)(came)
    hidden, mlp_in, active, slope, results = [], [], [], [], []
    for c in range(CHUNKS):
        h, m, a, s, part = feed_forward(scalars, layer, table, x[c], parts[c], came[c], w["up"], w["down"])
        hidden.append(h)
        mlp_in.append(m)
        active.append(a)
        slope.append(s)
        results.append((table, h, part))
    kept = dict(x=x, normed=normed, q=q, kv=kv, near=near, far=far, att=att, lse=lse, hidden=hidden,
                mlp_in=mlp_in, active=active, slope=slope)
    return results, kept


def backward_layer(scalars, layer, table, w, kept, dy, returned, steps):
    rows = CHUNKS * dy[0].shape[0]
    dy = list(steps("start", dy))
    d_up, parts, up_sums = [], [], []
    for c in range(CHUNKS):
        if c == 1:
            dy[1] = steps("half", after(dy[1], parts[0][0]))
        grad, part, sums = feed_back(scalars, layer, dy[c], kept["slope"][c], w["up"], w["down"])
        d_up.append(grad)
        up_sums.append(sums)
        parts.append((part, swap(part, "tensor")))
    wide = Reduction(wide_grads(scalars, kept["active"], dy, kept["mlp_in"], d_up), 2)
    parts = steps("fed", parts, wide)
    dh, dh_low, d_att, delta, mid_sums = [], [], [], [], []
    for c in range(CHUNKS):
        r = middle_back(scalars, layer, table, kept["hidden"][c], *parts[c], dy[c], kept["att"][c], w["out"])
        for held, value in zip((dh, dh_low, d_att, delta, mid_sums), r):
            held.append(value)
    d_att = steps("mid", d_att, wide)
    dq, mine, others = attend_far_back(scalars, kept["q"], d_att, kept["lse"], delta, kept["far"])
    total = (mine.astype(F32) + swap(others, "batch").astype(F32)).astype(BF)
    dq = steps("turn", after(dq, total), wide)
    home = shift(total, -2)
    dq, crossing = attend_near_back(scalars, kept["q"], d_att, kept["lse"], delta, kept["near"], dq)
    near = swap(crossing, "batch")
    dq = steps("between", dq, wide)
    dq0, dq1, dk0, dk1 = attend_own_back(scalars, kept["q"], d_att, kept["lse"], delta, kept["kv"], dq)
    dq, dkv = [dq0, dq1], [dk0, dk1]
    home, dq = steps("near", (home, dq), wide)
    dkv_low, parts, in_sums, back = [], [], [], []
    for c in range(CHUNKS):
        again = None if returned is None else returned[c]
        r = project_back(scalars, layer, c, dq[c], dkv[c], near, home, again, w["qkv"])
        dkv_low.append(r[0])
        parts.append((r[1], swap(r[1], "tensor")))
        in_sums.append(r[2])
        back.extend(r[3:])
    narrow = Reduction(narrow_grads(scalars, kept["normed"], dq, dkv_low, kept["att"], dh_low), 1)
    parts = steps("proj", parts, wide, narrow)
    parts = steps("last", parts, wide, narrow)
    dx, dx_low, last_sums = [], [], []
    for c in range(CHUNKS):
        r = last_back(scalars, table, kept["x"][c], *parts[c], dh[c])
        dx.append(r[0])
        dx_low.append(r[1])
        last_sums.append(r[2])
    up, mid, last, inn = [a + b for a, b in (up_sums, mid_sums, last_sums, in_sums)]
    blank = jnp.zeros((TABLE - BUP - 2, up.shape[1]), F32)
    small = jnp.concatenate(
        [last[0:1], mid[0:1], last[1:2], mid[1:2], mid[2:4], inn[0:2], up[0:2], blank], axis=0
    )
    return dx, dx_low, back, wide, narrow, small


def local(
    tokens, block_place, cotangent, norm_gains, norm_biases, query_key, query_bias, value_own, value_bias,
    value_extra, out_weight, out_bias, up_weight, up_bias, down_weight, down_bias,
):
    section = lax.axis_index("section")
    tensor = lax.axis_index("tensor")
    core = lax.axis_index("batch") % 2
    micros, _, half_rows, features = tokens.shape
    width = query_bias.shape[1]
    own_width = value_own.shape[2]
    inner = up_weight.shape[2]
    assert micros == 2 and lax.axis_size("section") == 2 and lax.axis_size("tensor") == 2
    assert 2 * own_width == width and 2 * width == features and inner == 2 * features

    place = take(block_place, section)[0]
    scalars = jnp.stack([place & 1, place >> 1, section, core]).astype(jnp.int32)

    my_tokens = take(tokens, section)[0]
    x = paired(my_tokens, swap(my_tokens, "tensor"), tensor)

    def row(*pieces):
        flat = jnp.concatenate([p.reshape(-1) for p in pieces])
        return jnp.pad(flat, (0, features - flat.shape[0]))[None]

    blank = jnp.zeros((width,), F32)
    own_table = jnp.concatenate(
        [norm_gains[0], norm_biases[0], out_bias, down_bias, row(query_bias[0]), row(blank, value_bias[0]),
         up_bias[0].reshape(2, features), jnp.zeros((TABLE - BUP - 2, features), F32)], axis=0
    )
    extra = jnp.where(section == 0, value_extra, jnp.zeros_like(value_extra))
    pieces = [query_key[0].reshape(features, 2 * width), value_own[0], extra]

    def half_of(weight):
        return take(weight.reshape((2, weight.shape[0] // 2) + weight.shape[1:]), core)

    qkv_half = jnp.concatenate([half_of(p) for p in pieces], axis=1)
    qkv = jnp.concatenate(pieces, axis=1)
    other_table = swap(own_table, "section")
    qkv_got = swap(qkv_half, "section")
    out_got = swap(half_of(out_weight[0]), "section")
    tables = paired(own_table, other_table, section)
    qkv_got, out_got, qkv, scalars, *rest = tie(qkv_got, out_got, qkv, scalars, *tables, *x)
    tables, x = rest[:2], rest[2:]
    qkv_other = swap(qkv_got, "batch")
    w = dict(qkv=(qkv, qkv_got, qkv_other))
    late = dict(
        up=swap(after(half_of(up_weight[0]), qkv_got), "section"),
        down=swap(after(half_of(down_weight[0]), qkv_got), "section"),
    )

    def on_projected(kv, q):
        mine, kv = tie(take(cotangent, section)[0], kv)
        late["dy"] = mine, swap(mine, "tensor")
        w["out"] = (out_weight[0], out_got, swap(after(out_got, kv), "batch"))
        return kv

    def on_arrived(far):
        mine, other = late["dy"]
        far, got, other = tie(far, late["up"], other)
        late["dy"] = paired(mine, other, tensor)
        w["up"] = (up_weight[0], got, swap(got, "batch"))
        return far

    def on_far(came):
        *came, got = tie(*came, late["down"])
        w["down"] = (down_weight[0], got, swap(got, "batch"))
        return came

    first, kept0 = forward_layer(
        scalars, 0, tables[0], w, x=x, hooks=dict(projected=on_projected, arrived=on_arrived, far=on_far)
    )
    first = [r + (swap(r[2], "tensor"),) for r in first]
    second, kept1 = forward_layer(scalars, 1, tables[1], w, ahead=first, carried=kept0["kv"])
    y0 = kept1["x"]

    def my_half(chunks):
        return jnp.where(tensor == 0, chunks[0], chunks[1])

    def by_section(mine0, mine1, kind):
        mine = jnp.where(section == 0, mine0, mine1)
        other = swap(jnp.where(section == 0, mine1, mine0).astype(kind), "section")
        return mine, other

    def steps1(number, values, wide=None, narrow=None):
        leaves, tree = jax.tree.flatten(values)
        if number == "fed":
            *leaves, wide.send = tie(*leaves, wide.send)
            wide.over_cores()
        if number == "mid":
            *leaves, wide.near = tie(*leaves, wide.near)
            wide.prepare()
            *leaves, wide.sent[0], wide.sent[1] = tie(*leaves, *wide.sent)
            wide.over_sections(0)
        if number == "between":
            *leaves, wide.came[0], wide.sent[1] = tie(*leaves, wide.came[0], wide.sent[1])
            wide.over_sections(1)
        if number == "near":
            *leaves, wide.came[1] = tie(*leaves, wide.came[1])
            late["a1"] = swap_all([wide.scatter_send()], -2)[0]
        if number == "proj":
            *leaves, narrow.send, got = tie(*leaves, narrow.send, late["a1"])
            narrow.over_cores()
            sent = wide.exchange_send(got)
            *leaves, sent = tie(*leaves, sent)
            late["b1"] = swap_all([sent], -1)[0]
        if number == "last":
            *leaves, narrow.near = tie(*leaves, narrow.near)
            narrow.prepare()
            *leaves, narrow.sent[0] = tie(*leaves, narrow.sent[0])
            narrow.over_sections()
        return jax.tree.unflatten(tree, leaves)

    dx1, dx1_low, back, wide1, narrow1, small1 = backward_layer(scalars, 1, tables[1], w, kept1, late["dy"], None, steps1)

    def steps0(number, values, wide=None, narrow=None):
        leaves, tree = jax.tree.flatten(values)
        if number == "half":
            *leaves, narrow1.came[0], got = tie(*leaves, narrow1.came[0], late["b1"])
            sent = [wide1.gather_send(got), narrow1.scatter_send()]
            *leaves, sent[0], sent[1] = tie(*leaves, *sent)
            late["c1"] = swap_all(sent, -2)
        if number == "fed":
            *leaves, wide.send, got, narrow_got = tie(*leaves, wide.send, *late["c1"])
            wide.over_cores()
            wide1.finish(got)
            sent = narrow1.exchange_send(narrow_got)
            *leaves, sent = tie(*leaves, sent)
            late["d1"] = swap_all([sent], -1)[0]
        if number == "mid":
            *leaves, wide.near, got = tie(*leaves, wide.near, late["d1"])
            wide.prepare()
            *leaves, wide.sent[0], wide.sent[1] = tie(*leaves, *wide.sent)
            wide.over_sections(0)
            late["e1"] = narrow1.gather_send(got)
        if number == "between":
            *leaves, wide.came[0], wide.sent[1] = tie(*leaves, wide.came[0], wide.sent[1])
            wide.over_sections(1)
        if number == "near":
            *leaves, wide.came[1] = tie(*leaves, wide.came[1])
            late["a0"] = swap_all([wide.scatter_send(), late["e1"]], -2)
        if number == "proj":
            *leaves, narrow.send, got, narrow_got = tie(*leaves, narrow.send, *late["a0"])
            narrow1.finish(narrow_got)
            narrow.over_cores()
            sent = wide.exchange_send(got)
            *leaves, sent = tie(*leaves, sent)
            late["b0"] = swap_all([sent], -1)[0]
            *leaves, narrow.near = tie(*leaves, narrow.near)
            narrow.prepare()
            *leaves, narrow.sent[0] = tie(*leaves, narrow.sent[0])
            narrow.over_sections()
            late["y1"] = [swap(after(r[2], leaves[0]), "tensor") for r in second]
        if number == "last":
            *leaves, narrow.came[0] = tie(*leaves, narrow.came[0])
        return jax.tree.unflatten(tree, leaves)

    dx0, dx0_low, _, wide0, narrow0, small0 = backward_layer(scalars, 0, tables[0], w, kept0, dx1_low, back, steps0)
    sums = jnp.stack([small0, small1])
    sums = sums + swap(sums, "batch")
    got, sums, *rest = tie(late["b0"], sums, *late["y1"], my_half(dx0), my_half(dx1))
    y_came, grads = rest[:2], rest[2:]
    sent = [narrow0.scatter_send(), wide0.gather_send(got)]
    sent[0], sent[1], sums, grads[0], grads[1] = tie(*sent, sums, *grads)
    late["c0"] = swap_all(sent, -2)
    table = take(sums, section) + swap(take(sums, 1 - section), "section")
    mine_grads, other_grads = by_section(*grads, BF)
    y1 = my_half(
        [(r[1] + r[0][BDOWN : BDOWN + 1] + r[2].astype(F32) + c.astype(F32)).astype(BF) for r, c in zip(second, y_came)]
    )
    mine_out, other_out = by_section(my_half(y0), y1, BF)

    narrow0_got, wide0_got, table, other_grads, other_out = tie(
        *late["c0"], table, other_grads, other_out
    )
    sent = narrow0.exchange_send(narrow0_got)
    wide0.finish(wide0_got)
    wide_mine = jnp.where(section == 0, wide0.quarter, wide1.quarter)
    wide_sent = jnp.split(jnp.where(section == 0, wide1.quarter, wide0.quarter), 2, axis=0)
    sent, wide_sent[0] = tie(sent, wide_sent[0])
    got = swap_all([sent], -1)[0]
    wide_other = [swap(wide_sent[0], "section")]
    for bit in chip_bits()[:-1]:
        table = table + swap(table, "batch", 1 << bit)

    got, table, wide_other[0], wide_sent[1] = tie(got, table, wide_other[0], wide_sent[1])
    sent = narrow0.gather_send(got)
    got = swap_all([sent], -2)[0]
    wide_mine2, wide_other2 = swap(wide_mine, "batch"), swap(wide_other[0], "batch")
    table = table + swap(table, "batch", 1 << chip_bits()[-1])
    wide_other.append(swap(wide_sent[1], "section"))

    got, wide_other[1], table = tie(got, wide_other[1], table)
    narrow0.finish(got)
    outputs = jnp.stack(paired(mine_out, other_out, section))
    input_grads = jnp.stack(paired(mine_grads.astype(F32), other_grads.astype(F32), section))

    def gathered(first, second):
        mine = jnp.where(section == 0, first, second)
        other = swap(jnp.where(section == 0, second, first), "section")
        mine2 = swap(mine, "batch")
        other, mine2 = tie(other, mine2, token)[:2]
        return mine, other, mine2, swap(other, "batch")

    d_down, d_up, token = wide_unpack(
        scalars, wide_mine, wide_mine2, wide_other, [wide_other2, swap(wide_other[1], "batch")], inner
    )
    rows = features // 4
    extra = narrow0.quarter[rows : rows + rows // 2]
    extras = (extra, swap(extra, "batch"))
    d_q, d_k, d_v, d_extra, d_out = narrow_unpack(
        scalars, gathered(narrow0.quarter, narrow1.quarter), extras, width, token
    )
    d_qk = jnp.stack([d_q, d_k], axis=1)
    return (
        outputs.reshape(1, micros, 1, half_rows, features),
        input_grads.reshape(1, micros, 1, half_rows, features),
        table[GAIN0 : GAIN1 + 1][None],
        table[BIAS0 : BIAS1 + 1][None],
        d_qk.reshape(1, features, 2, width),
        table[BQ : BQ + 1, :width],
        d_v[None],
        table[BKV : BKV + 1, width : width + own_width],
        d_extra,
        d_out[None],
        table[BO : BO + 1],
        d_up[None],
        table[BUP : BUP + 2].reshape(1, inner),
        d_down[None],
        table[BDOWN : BDOWN + 1],
    )


def solution(mesh):
    return jax.shard_map(
        local,
        mesh=mesh,
        in_specs=(
            P(None, "batch", "tensor", None),
            P(None, "batch"),
            P(None, "batch", "tensor", None),
            P("section", None, None),
            P("section", None, None),
            P("section", None, None, "tensor"),
            P("section", "tensor"),
            P("section", None, "tensor"),
            P("section", "tensor"),
            P(None, "tensor"),
            P("section", "tensor", None),
            P("section", None),
            P("section", None, "tensor"),
            P("section", "tensor"),
            P("section", "tensor", None),
            P("section", None),
        ),
        out_specs=(
            P("section", None, "batch", "tensor", None),
            P("section", None, "batch", "tensor", None),
            P("section", None, None),
            P("section", None, None),
            P("section", None, None, "tensor"),
            P("section", "tensor"),
            P("section", None, "tensor"),
            P("section", "tensor"),
            P("section", "tensor"),
            P("section", "tensor", None),
            P("section", None),
            P("section", None, "tensor"),
            P("section", "tensor"),
            P("section", "tensor", None),
            P("section", None),
        ),
        check_vma=False,
    )
```

```python
import jax
import jax.numpy as jnp
from jax import lax
from jax.experimental import pallas as pl
from jax.experimental.pallas import tpu as pltpu
from jax.sharding import PartitionSpec as P

F32 = jnp.float32
BF = jnp.bfloat16
LOW = -1e30
HEAD = 64
CHUNKS = 2

GAIN0, GAIN1, BIAS0, BIAS1, BO, BDOWN, BQ, BKV, BUP = range(9)
TABLE = 16

WHOLE = pl.BlockSpec(memory_space=pltpu.VMEM)
SCALARS = pl.BlockSpec(memory_space=pltpu.SMEM)
FAR_OFF = pl.BlockSpec(memory_space=pltpu.HBM)


def dot_nn(a, b):
    return lax.dot_general(a, b, (((1,), (0,)), ((), ())), preferred_element_type=F32)


def dot_nt(a, b):
    return lax.dot_general(a, b, (((1,), (1,)), ((), ())), preferred_element_type=F32)


def dot_tn(a, b):
    return lax.dot_general(a, b, (((0,), (0,)), ((), ())), preferred_element_type=F32)


class Late:
    def __init__(self, array):
        self.array = array


def in_hbm(array):
    return pltpu.with_memory_space_constraint(array, pltpu.HBM)


FLUSH = []


def flush(*refs):
    for ref in refs:
        for k, (held, copy, started) in enumerate(FLUSH[-1]):
            if held is ref and not started:
                copy.start()
                FLUSH[-1][k] = (held, copy, True)


LATER, RAW = 1, 2


def call(inner_body, outs, scalars, blocks, remote=(), scratch=(), us=1.0, limit=48):
    shapes = [pltpu.HBM(o[0], o[1]) if len(o) > 2 else jax.ShapeDtypeStruct(o[0], o[1]) for o in outs]
    kinds = [o[2] if len(o) > 2 else 0 for o in outs]
    late = [i for i, b in enumerate(blocks) if isinstance(b, Late)]
    blocks = [in_hbm(b.array) if isinstance(b, Late) else b for b in blocks]
    remote = [in_hbm(r) for r in remote]
    n_in, n_out = 1 + len(blocks) + len(remote), len(outs)
    later = [i for i, kind in enumerate(kinds) if kind == LATER]
    spare = [pltpu.VMEM(blocks[i].shape, blocks[i].dtype) for i in late]
    spare += [pltpu.VMEM(shapes[i].shape, shapes[i].dtype) for i in later]
    sems = [pltpu.SemaphoreType.DMA((max(len(late), 1),)), pltpu.SemaphoreType.DMA((max(len(later), 1),))]

    def body(*refs):
        refs = list(refs)
        first = n_in + n_out
        n_spare = len(spare)
        held, (sem, out_sem), own = refs[first : first + n_spare], refs[first + n_spare : first + n_spare + 2], refs[first + n_spare + 2 :]
        copies = [pltpu.make_async_copy(refs[1 + i], v, sem.at[k]) for k, (i, v) in enumerate(zip(late, held))]
        back = [
            pltpu.make_async_copy(v, refs[n_in + i], out_sem.at[k])
            for k, (i, v) in enumerate(zip(later, held[len(late) :]))
        ]
        for copy in copies:
            copy.start()
        for copy in copies:
            copy.wait()
        for i, v in zip(late, held):
            refs[1 + i] = v
        for i, v in zip(later, held[len(late) :]):
            refs[n_in + i] = v
        FLUSH.append([(held[len(late) + k], copy, False) for k, copy in enumerate(back)])
        inner_body(*refs[:first], *own)
        flush(*held[len(late) :])
        FLUSH.pop()
        for copy in back:
            copy.wait()

    return pl.pallas_call(
        body,
        out_shape=shapes,
        in_specs=[SCALARS] + [FAR_OFF if i in late else WHOLE for i in range(len(blocks))] + [FAR_OFF] * len(remote),
        out_specs=[FAR_OFF if kind else WHOLE for kind in kinds],
        scratch_shapes=spare + sems + list(scratch),
        compiler_params=pltpu.CompilerParams(vmem_limit_bytes=limit * 1024 * 1024),
        cost_estimate=pl.CostEstimate(flops=int(us * 1.2e8), bytes_accessed=int(us * 2e5), transcendentals=0),
    )(scalars, *blocks, *remote)


def fetch_start(scalars, layer, own, got, other, held, sem):
    half = held.shape[0] // 2

    @pl.when(scalars[2] == layer)
    def _():
        pltpu.make_async_copy(own, held, sem).start()

    @pl.when(scalars[2] != layer)
    def _():
        mine = pl.multiple_of(scalars[3] * half, half)
        rest = pl.multiple_of((1 - scalars[3]) * half, half)
        pltpu.make_async_copy(got, held.at[pl.ds(mine, half)], sem).start()
        pltpu.make_async_copy(other, held.at[pl.ds(rest, half)], sem).start()


def fetch_parts(scalars, layer, own, got, other, held, sem):
    half = held.shape[0] // 2

    @pl.when(scalars[2] == layer)
    def _():
        pltpu.make_async_copy(own, held, sem).start()

    @pl.when(scalars[2] != layer)
    def _():
        for side, refs in ((scalars[3], got), (1 - scalars[3], other)):
            at = pl.ds(pl.multiple_of(side * half, half), half)
            start = 0
            for ref in refs:
                end = start + ref.shape[1]
                pltpu.make_async_copy(ref, held.at[at, start:end], sem).start()
                start = end


def fetch_wait(own, held, sem):
    pltpu.make_async_copy(own, held, sem).wait()


def held_like(*weights):
    return [pltpu.VMEM(w[0].shape, BF) for w in weights] + [pltpu.SemaphoreType.DMA] * len(weights)


def norm_parts(v):
    centred = v - jnp.mean(v, axis=-1, keepdims=True)
    rate = lax.rsqrt(jnp.mean(centred * centred, axis=-1, keepdims=True) + 1e-05)
    return centred * rate, rate


def norm_grad(v, gain, grad):
    unit, rate = norm_parts(v)
    scaled = grad * gain
    inner = jnp.mean(scaled * unit, axis=-1, keepdims=True)
    result = rate * (scaled - jnp.mean(scaled, axis=-1, keepdims=True) - unit * inner)
    return result, jnp.sum(grad * unit, axis=0, keepdims=True), jnp.sum(grad, axis=0, keepdims=True)


def gelu_both(u):
    factor = 0.7978845608028654
    square = u * u
    t = jnp.tanh(factor * u * (1.0 + 0.044715 * square))
    half = 0.5 * (1.0 + t)
    slope = half + (0.5 * factor) * u * (1.0 - t * t) * (1.0 + (3 * 0.044715) * square)
    return u * half, slope


def project(scalars, layer, weights, table, x=None, ahead=None, carried=None):
    if ahead is None:
        rows, features = x[0].shape
        blocks = [table, *x]
    else:
        rows, features = ahead[0][1].shape
        blocks = [table, ahead[0][0], Late(carried)]
        for chunk in ahead:
            blocks.extend([Late(chunk[1]), *chunk[2:]])
    width = weights[0].shape[1] // 3

    def body(scal, tab, *refs):
        given = refs[: len(blocks) - 1]
        own, *parts = refs[len(blocks) - 1 : len(blocks) + 4]
        outs = refs[len(blocks) + 4 : -2]
        held, sem = refs[-2:]
        fetch_parts(scal, layer, own, parts[:2], parts[2:], held, sem)
        for c in range(CHUNKS):
            at = slice(c * rows, (c + 1) * rows)
            if ahead is None:
                v = given[c][...].astype(F32)
            else:
                before, carry = given[:2]
                hid, mine, came = given[2 + 3 * c : 5 + 3 * c]
                y = hid[...] + before[BDOWN : BDOWN + 1] + mine[...].astype(F32) + came[...].astype(F32)
                low = y.astype(BF)
                outs[5 + c][...] = low
                v = low.astype(F32)
            unit, _ = norm_parts(v)
            normed = (unit * tab[GAIN0 : GAIN0 + 1] + tab[BIAS0 : BIAS0 + 1]).astype(BF)
            outs[c][...] = normed
            if c == 0:
                fetch_wait(own, held, sem)
            q = dot_nn(normed, held[:, :width]) + tab[BQ : BQ + 1, :width]
            outs[2 + c][...] = (q.astype(BF).astype(F32) * 0.125).astype(BF)
            kv = dot_nn(normed, held[:, width:]) + tab[BKV : BKV + 1]
            if ahead is not None:
                rolled = pltpu.roll(carry[at, :].astype(F32), width // 2, 1)
                lane = lax.broadcasted_iota(jnp.int32, kv.shape, 1)
                kv = jnp.where(lane >= width + width // 2, rolled, kv)
            outs[4][at, :] = kv.astype(BF)

    outs = [((rows, features), BF, LATER)] * 2 + [((rows, width), BF)] * 2 + [((2 * rows, 2 * width), BF)]
    if ahead is not None:
        outs += [((rows, features), BF, LATER)] * 2
    r = call(body, outs, scalars, blocks, weights, held_like(weights), us=2.5)
    return list(x) if ahead is None else r[5:], r[:2], r[2:4], r[4]


def low_lanes(shape):
    return lax.broadcasted_iota(jnp.int32, shape, 1) < HEAD


def head_of(pair, sub, fill):
    keep = low_lanes(pair.shape)
    return jnp.where(keep if sub == 0 else ~keep, pair, jnp.full_like(pair, fill))


def halves_of(ref, size):
    return tuple(ref.at[i * size : (i + 1) * size] for i in range(ref.shape[0] // size))


def spans(p, width):
    return slice(p * 128, (p + 1) * 128), slice(width + p * 128, width + (p + 1) * 128)


def scored(q, tiles, p, width, masks):
    ks, vs = spans(p, width)
    tops, outs = [], []
    for sub in range(2):
        scores = [dot_nt(q, head_of(t[:, ks], sub, 0)) for t in tiles]
        scores = [s if m is None else jnp.where(m, s, LOW) for s, m in zip(scores, masks)]
        top = scores[0].max(axis=1, keepdims=True)
        for s in scores[1:]:
            top = jnp.maximum(top, s.max(axis=1, keepdims=True))
        total = None
        for s, t in zip(scores, tiles):
            part = dot_nn(jnp.exp(s - top).astype(BF), head_of(t[:, vs], sub, 1))
            total = part if total is None else total + part
        tops.append(top)
        outs.append(total)
    low = low_lanes(outs[0].shape)
    value = jnp.where(low, outs[0], outs[1])
    amount = pltpu.roll(jnp.where(low, outs[1], outs[0]), HEAD, 1)
    return tops, value, amount


def attend_local(scalars, q, kv, near):
    size, width = q[0].shape
    rows = size * CHUNKS

    def body(scal, q0, q1, k_all, n_all, out, amount, tops):
        own = halves_of(k_all, size)
        row = lax.broadcasted_iota(jnp.int32, (size, size), 0)
        col = lax.broadcasted_iota(jnp.int32, (size, size), 1)
        causal = col <= row

        def run(extra):
            for c, q_ref in enumerate((q0, q1)):
                at = slice(c * size, (c + 1) * size)
                tiles = list(extra) + [own[i] for i in range(c + 1)]
                masks = [None] * (len(tiles) - 1) + [causal]
                for p in range(width // 128):
                    span = slice(p * 128, (p + 1) * 128)
                    top, value, total = scored(q_ref[:, span], tiles, p, width, masks)
                    out[at, span] = value
                    amount[at, span] = total
                    tops[at, 2 * p : 2 * p + 1] = top[0]
                    tops[at, 2 * p + 1 : 2 * p + 2] = top[1]

        @pl.when(scal[0] == 1)
        def _():
            run(halves_of(n_all, size))

        @pl.when(scal[0] == 0)
        def _():
            run(())

    outs = [((rows, width), F32), ((rows, width), F32), ((rows, 128), F32)]
    return call(body, outs, scalars, [*q, kv, near], us=5)


def attend_far(scalars, layer, c, q, far, out, amount, tops, weights):
    size, width = q.shape
    features = weights[0].shape[1]

    def body(scal, q_ref, fa, fb, out_ref, amount_ref, tops_ref, own, got, other, att, lse, part, stats, held, sem):
        fetch_start(scal, layer, own, got, other, held, sem)
        at = slice(c * size, (c + 1) * size)
        stats[...] = jnp.zeros_like(stats)

        def finish(p, value, total, top0, top1):
            span = slice(p * 128, (p + 1) * 128)
            att[:, span] = (value / total).astype(BF)
            logs = jnp.log(total)
            stats[:, 2 * p : 2 * p + 1] = top0 + logs[:, 0:1]
            stats[:, 2 * p + 1 : 2 * p + 2] = top1 + logs[:, HEAD : HEAD + 1]

        @pl.when(scal[1] == 0)
        def _():
            for p in range(width // 128):
                span = slice(p * 128, (p + 1) * 128)
                finish(p, out_ref[at, span], amount_ref[at, span], tops_ref[at, 2 * p : 2 * p + 1], tops_ref[at, 2 * p + 1 : 2 * p + 2])

        @pl.when(scal[1] == 1)
        def _():
            for p in range(width // 128):
                span = slice(p * 128, (p + 1) * 128)
                new, value, total = scored(q_ref[:, span], halves_of(fa, size) + halves_of(fb, size), p, width, [None] * 4)
                tops_all, olds, news = [], [], []
                for sub in range(2):
                    before = tops_ref[at, 2 * p + sub : 2 * p + sub + 1]
                    top = jnp.maximum(before, new[sub])
                    tops_all.append(top)
                    olds.append(jnp.exp(before - top))
                    news.append(jnp.exp(new[sub] - top))
                low = low_lanes(value.shape)
                keep = jnp.where(low, olds[0], olds[1])
                take = jnp.where(low, news[0], news[1])
                finish(p, out_ref[at, span] * keep + value * take, amount_ref[at, span] * keep + total * take, *tops_all)

        lse[...] = jnp.transpose(stats[...])[0:8, :]
        flush(att, lse)
        fetch_wait(own, held, sem)
        part[...] = dot_nn(att[...], held[...]).astype(BF)

    outs = [((size, width), BF, LATER), ((8, size), F32, LATER), ((size, features), BF)]
    scratch = [pltpu.VMEM((size, 128), F32)] + held_like(weights)
    return call(body, outs, scalars, [q, *far, out, amount, tops], weights, scratch, us=4.5)


def back_tile(p, width, q, do, lse, delta, kv, mask):
    ks, vs = spans(p, width)
    dq, dks, dvs = None, [], []
    for sub in range(2):
        h = 2 * p + sub
        key = head_of(kv[:, ks], sub, 0)
        scores = dot_nt(key, q)
        weight = jnp.exp(scores - lse[h : h + 1, :])
        if mask is not None:
            weight = jnp.where(mask, weight, 0.0)
        d_weight = dot_nt(head_of(kv[:, vs], sub, 0), do)
        d_score = (weight * (d_weight - delta[h : h + 1, :])).astype(BF)
        dvs.append(dot_nn(weight.astype(BF), do))
        dks.append(dot_nn(d_score, q))
        d = dot_tn(d_score, key)
        dq = d if dq is None else dq + d
    low = low_lanes(dks[0].shape)
    return dq, jnp.where(low, dks[0], dks[1]), jnp.where(low, dvs[0], dvs[1])


def staged(size, width):
    rows = size * CHUNKS
    return [pltpu.VMEM((rows, width), BF), pltpu.VMEM((rows, width), BF), pltpu.VMEM((8, rows), F32), pltpu.VMEM((8, rows), F32)]


def stage(size, given, held):
    for k, ref in enumerate(held):
        for c in range(CHUNKS):
            at = slice(c * size, (c + 1) * size)
            if k < 2:
                ref[at, :] = given[2 * k + c][...]
            else:
                ref[:, at] = given[2 * k + c][...]


def back_over(held, width, size, sources, dq_ref):
    q, do, lse, delta = held
    for p in range(width // 128):
        ks, vs = spans(p, width)
        total = dq_ref[:, ks]
        for source, ref, start in sources:
            for i in range(CHUNKS):
                at = slice(start + i * size, start + (i + 1) * size)
                tile = source.at[i * size : (i + 1) * size]
                dq, dk, dv = back_tile(p, width, q[:, ks], do[:, ks], lse, delta, tile, None)
                total = total + dq
                ref[at, ks] = dk.astype(BF)
                ref[at, vs] = dv.astype(BF)
        dq_ref[:, ks] = total


def attend_far_back(scalars, q, do, lse, delta, far):
    size, width = q[0].shape
    rows = size * CHUNKS

    def body(scal, q0, q1, o0, o1, l0, l1, d0, d1, fa, fb, dq_out, mine, others, *held):
        dq_out[...] = jnp.zeros_like(dq_out)

        @pl.when(scal[1] == 1)
        def _():
            stage(size, (q0, q1, o0, o1, l0, l1, d0, d1), held)
            back_over(held, width, size, [(fb, others, 0), (fa, mine, 0)], dq_out)

        @pl.when(scal[1] == 0)
        def _():
            mine[...] = jnp.zeros_like(mine)
            others[...] = jnp.zeros_like(others)

    outs = [((rows, width), F32), ((rows, 2 * width), BF), ((rows, 2 * width), BF)]
    blocks = [*map(Late, q), *do, *map(Late, lse), *delta, *map(Late, far)]
    return call(body, outs, scalars, blocks, (), staged(size, width), us=12)


def attend_near_back(scalars, q, do, lse, delta, near, dq_before):
    size, width = q[0].shape
    rows = size * CHUNKS

    def body(scal, q0, q1, o0, o1, l0, l1, d0, d1, n_all, before, dq_out, crossing, *held):
        dq_out[...] = before[...]

        @pl.when(scal[0] == 1)
        def _():
            stage(size, (q0, q1, o0, o1, l0, l1, d0, d1), held)
            back_over(held, width, size, [(n_all, crossing, 0)], dq_out)

        @pl.when(scal[0] == 0)
        def _():
            crossing[...] = jnp.zeros_like(crossing)

    outs = [((rows, width), F32), ((rows, 2 * width), BF)]
    blocks = [*map(Late, q), *do, *map(Late, lse), *delta, Late(near), dq_before]
    return call(body, outs, scalars, blocks, (), staged(size, width), us=0.2)


def attend_own_back(scalars, q, do, lse, delta, kv, dq_before):
    size, width = q[0].shape
    rows = size * CHUNKS

    def body(scal, q0, q1, o0, o1, l0, l1, d0, d1, k_all, before, dq0, dq1, dk0, dk1, *held):
        stage(size, (q0, q1, o0, o1, l0, l1, d0, d1), held)
        qs, dos, lses, deltas = held
        key = lax.broadcasted_iota(jnp.int32, (size, rows), 0)
        query = lax.broadcasted_iota(jnp.int32, (size, rows), 1)
        causal = key <= query
        for p in range(width // 128):
            ks, vs = spans(p, width)
            k0, k1 = halves_of(k_all, size)
            first, dk, dv = back_tile(p, width, qs[:, ks], dos[:, ks], lses, deltas, k0, causal)
            dk0[:, ks] = dk
            dk0[:, vs] = dv
            late = [ref.at[:, size:rows] for ref in (lses, deltas)]
            second, dk, dv = back_tile(p, width, qs[size:, ks], dos[size:, ks], *late, k1, causal[:, :size])
            dk1[:, ks] = dk
            dk1[:, vs] = dv
            dq0[:, ks] = ((before[:size, ks] + first[:size]) * 0.125).astype(BF)
            dq1[:, ks] = ((before[size:, ks] + first[size:] + second) * 0.125).astype(BF)

    outs = [((size, width), BF)] * 2 + [((size, 2 * width), F32)] * 2
    blocks = [*map(Late, q), *do, *map(Late, lse), *delta, Late(kv), dq_before]
    return call(body, outs, scalars, blocks, (), staged(size, width), us=0.2)


def feed_forward(scalars, layer, table, x, mine, came, up, down):
    rows, features = x.shape
    inner = up[0].shape[1]

    def body(scal, tab, x_ref, mine_ref, came_ref, u_own, u_got, u_other, d_own, d_got, d_other,
             hidden, mlp_in, active, slope, part, up_held, down_held, up_sem, down_sem):
        fetch_start(scal, layer, u_own, u_got, u_other, up_held, up_sem)
        fetch_start(scal, layer, d_own, d_got, d_other, down_held, down_sem)
        h = x_ref[...].astype(F32) + (mine_ref[...].astype(F32) + came_ref[...].astype(F32)) + tab[BO : BO + 1]
        hidden[...] = h
        unit, _ = norm_parts(h)
        low = (unit * tab[GAIN1 : GAIN1 + 1] + tab[BIAS1 : BIAS1 + 1]).astype(BF)
        mlp_in[...] = low
        flush(hidden, mlp_in)
        fetch_wait(u_own, up_held, up_sem)
        for j in range(inner // features):
            cols = slice(j * features, (j + 1) * features)
            value, grad = gelu_both(dot_nn(low, up_held[:, cols]) + tab[BUP + j : BUP + j + 1])
            active[:, cols] = value.astype(BF)
            slope[:, cols] = grad.astype(BF)
        flush(active, slope)
        fetch_wait(d_own, down_held, down_sem)
        part[...] = dot_nn(active[...], down_held[...]).astype(BF)

    outs = [((rows, features), F32, LATER), ((rows, features), BF, LATER), ((rows, inner), BF, LATER), ((rows, inner), BF, LATER), ((rows, features), BF)]
    return call(body, outs, scalars, [table, Late(x), mine, came], [*up, *down], held_like(up, down), us=4)


def feed_back(scalars, layer, dy, slope, up, down):
    rows, features = dy.shape
    inner = up[0].shape[1]

    def body(scal, dy_ref, slope_ref, u_own, u_got, u_other, d_own, d_got, d_other,
             d_up, part, sums, up_held, down_held, up_sem, down_sem):
        fetch_start(scal, layer, d_own, d_got, d_other, down_held, down_sem)
        fetch_start(scal, layer, u_own, u_got, u_other, up_held, up_sem)
        sums[...] = jnp.zeros_like(sums)
        fetch_wait(d_own, down_held, down_sem)
        for j in range(inner // features):
            cols = slice(j * features, (j + 1) * features)
            grad = (dot_nt(dy_ref[...], down_held[cols, :]) * slope_ref[:, cols].astype(F32)).astype(BF)
            d_up[:, cols] = grad
            sums[j : j + 1, :] = jnp.sum(grad.astype(F32), axis=0, keepdims=True)
        fetch_wait(u_own, up_held, up_sem)
        part[...] = dot_nt(d_up[...], up_held[...]).astype(BF)

    outs = [((rows, inner), BF), ((rows, features), BF), ((8, features), F32)]
    return call(body, outs, scalars, [dy, Late(slope)], [*up, *down], held_like(up, down), us=1.0)


def middle_back(scalars, layer, table, hidden, parts, dy, attended, weights):
    rows, features = hidden[0].shape
    width = attended[0].shape[1]

    def body(scal, tab, *refs):
        given, (own, got, other) = refs[: 5 * CHUNKS], refs[5 * CHUNKS : 5 * CHUNKS + 3]
        outs = refs[5 * CHUNKS + 3 : 9 * CHUNKS + 4]
        stats, held, sem = refs[9 * CHUNKS + 4 :]
        fetch_start(scal, layer, own, got, other, held, sem)
        sums = outs[-1]
        sums[...] = jnp.zeros_like(sums)
        stats[...] = jnp.zeros_like(stats)
        lows = []
        for c in range(CHUNKS):
            hid, mine, came, dy_ref, att = given[5 * c : 5 * c + 5]
            dh_ref, low_ref, da_ref, delta = outs[4 * c : 4 * c + 4]
            grad = mine[...].astype(F32) + came[...].astype(F32)
            back, d_gain, d_bias = norm_grad(hid[...], tab[GAIN1 : GAIN1 + 1], grad)
            up = dy_ref[...].astype(F32)
            dh = up + back
            dh_ref[...] = dh
            low = dh.astype(BF)
            low_ref[...] = low
            flush(dh_ref, low_ref)
            added = (d_gain, d_bias, jnp.sum(dh, axis=0, keepdims=True), jnp.sum(up, axis=0, keepdims=True))
            for k, value in enumerate(added):
                sums[k : k + 1, :] += value
            lows.append(low)
        fetch_wait(own, held, sem)
        for c in range(CHUNKS):
            att = given[5 * c + 4]
            da_ref, delta = outs[4 * c + 2 : 4 * c + 4]
            da = dot_nt(lows[c], held[...]).astype(BF)
            da_ref[...] = da
            for p in range(width // 128):
                span = slice(p * 128, (p + 1) * 128)
                product = da[:, span].astype(F32) * att[:, span].astype(F32)
                first = low_lanes(product.shape)
                stats[:, 2 * p : 2 * p + 1] = jnp.sum(jnp.where(first, product, 0.0), axis=1, keepdims=True)
                stats[:, 2 * p + 1 : 2 * p + 2] = jnp.sum(jnp.where(first, 0.0, product), axis=1, keepdims=True)
            delta[...] = jnp.transpose(stats[...])[0:8, :]

    one = [((rows, features), F32, LATER), ((rows, features), BF, LATER), ((rows, width), BF), ((8, rows), F32)]
    scratch = [pltpu.VMEM((rows, 128), F32)] + held_like(weights)
    blocks = [table]
    for c in range(CHUNKS):
        blocks += [Late(hidden[c]), *parts[c], dy[c], Late(attended[c])]
    r = call(body, one * CHUNKS + [((8, features), F32)], scalars, blocks, weights, scratch, us=2.8)
    return [list(r[k : 4 * CHUNKS : 4]) for k in range(4)] + [r[-1]]


def project_back(scalars, layer, c, dq, dkv, near, far, returned, weights):
    rows, width = dq.shape
    features = weights[0].shape[0]

    def body(scal, dq_ref, dkv_ref, near_ref, far_ref, *rest):
        back_ref = rest[0] if returned is not None else None
        outs = rest[-6:-2] if returned is None else rest[-5:-2]
        own, *parts = rest[-11:-6] if returned is None else rest[-10:-5]
        held, sem = rest[-2:]
        fetch_parts(scal, layer, own, parts[:2], parts[2:], held, sem)
        at = slice(c * rows, (c + 1) * rows)
        total = dkv_ref[...] + near_ref[at, :].astype(F32) + far_ref[at, :].astype(F32)
        if returned is None:
            outs[3][...] = total
        else:
            rolled = pltpu.roll(back_ref[...], 2 * width - width // 2, 1)
            lane = lax.broadcasted_iota(jnp.int32, total.shape, 1)
            total = total + jnp.where((lane >= width) & (lane < width + width // 2), rolled, 0.0)
        low = total.astype(BF)
        outs[0][...] = low
        sums = outs[2]
        sums[...] = jnp.zeros_like(sums)
        sums[0:1, :width] = jnp.sum(dq_ref[...].astype(F32), axis=0, keepdims=True)
        sums[1:2, :] = jnp.sum(low.astype(F32), axis=0, keepdims=True)
        fetch_wait(own, held, sem)
        outs[1][...] = (dot_nt(dq_ref[...], held[:, :width]) + dot_nt(low, held[:, width:])).astype(BF)

    outs = [((rows, 2 * width), BF), ((rows, features), BF), ((8, features), F32)]
    blocks = [dq, dkv, near, far]
    if returned is None:
        outs.append(((rows, 2 * width), F32, LATER))
    else:
        blocks.append(Late(returned))
    return call(body, outs, scalars, blocks, weights, held_like(weights), us=2.7)


def last_back(scalars, table, x, parts, dh):
    rows, features = x[0].shape

    def body(scal, tab, *refs):
        given, outs = refs[: 4 * CHUNKS], refs[4 * CHUNKS :]
        sums = outs[-1]
        sums[...] = jnp.zeros_like(sums)
        for c in range(CHUNKS):
            x_ref, mine, came, dh_ref = given[4 * c : 4 * c + 4]
            dx_ref, low_ref = outs[2 * c : 2 * c + 2]
            grad = mine[...].astype(F32) + came[...].astype(F32)
            back, d_gain, d_bias = norm_grad(x_ref[...].astype(F32), tab[GAIN0 : GAIN0 + 1], grad)
            dx = dh_ref[...] + back
            dx_ref[...] = dx
            flush(dx_ref)
            low_ref[...] = dx.astype(BF)
            sums[0:1, :] += d_gain
            sums[1:2, :] += d_bias

    outs = [((rows, features), F32, LATER), ((rows, features), BF)] * CHUNKS + [((8, features), F32)]
    blocks = [table]
    for c in range(CHUNKS):
        blocks += [Late(x[c]), *parts[c], Late(dh[c])]
    r = call(body, outs, scalars, blocks, us=0.5)
    return list(r[0 : 2 * CHUNKS : 2]), list(r[1 : 2 * CHUNKS : 2]), r[-1]


def both_chunks(left, left_span, right, right_span):
    total = None
    for a, b in zip(left, right):
        d = dot_tn(a[:, left_span], b[:, right_span])
        total = d if total is None else total + d
    return total


def hand_out(scal, packed, send, mine, sem):
    copies = [
        pltpu.make_async_copy(packed.at[pl.ds(2 * (1 - scal[3]), 2)], send, sem.at[0]),
        pltpu.make_async_copy(packed.at[pl.ds(2 * scal[3], 2)], mine, sem.at[1]),
    ]
    for copy in copies:
        copy.start()
    for copy in copies:
        copy.wait()


def wide_grads(scalars, active, dy, mlp_in, d_up):
    features = dy[0].shape[1]
    inner = active[0].shape[1]
    a, half = inner // 4, features // 2
    size = a + half

    def body(scal, a0, a1, y0, y1, m0, m1, u0, u1, send, mine, packed, sem):
        for k in range(4):
            span = slice(k * a, (k + 1) * a)
            packed[k, :a, :] = both_chunks((a0, a1), span, (y0, y1), slice(None)).astype(BF)
            for i in range(2):
                part = both_chunks((m0, m1), slice(i * half, (i + 1) * half), (u0, u1), span)
                packed[k, a:, i * a : (i + 1) * a] = part.astype(BF)
        hand_out(scal, packed, send, mine, sem)

    blocks = [*map(Late, active), *dy, *map(Late, mlp_in), *d_up]
    outs = [((2, size, features), BF, RAW)] * 2
    scratch = [pltpu.VMEM((4, size, features), BF), pltpu.SemaphoreType.DMA((2,))]
    return call(body, outs, scalars, blocks, (), scratch, us=3.7)


def narrow_grads(scalars, normed, dq, dkv, attended, dh_low):
    features = normed[0].shape[1]
    width = dq[0].shape[1]
    rows = features // 4
    half, c = rows // 2, width // 4
    size = rows + half + c

    def body(scal, n0, n1, q0, q1, k0, k1, t0, t1, h0, h1, send, mine, packed, sem):
        every = slice(None)
        for x in range(2):
            span = slice(2 * x * rows, 2 * (x + 1) * rows)
            first = both_chunks((n0, n1), span, (q0, q1), every).astype(BF)
            second = both_chunks((n0, n1), span, (k0, k1), every).astype(BF)
            for core in range(2):
                k, at = 2 * core + x, core * rows
                packed[k, :rows, :width] = first[at : at + rows, :]
                packed[k, :rows, width:] = second[at : at + rows, :width]
                packed[k, rows : rows + half, :width] = second[at : at + half, width:]
                packed[k, rows : rows + half, width:] = second[at + half : at + rows, width:]
        out = both_chunks((t0, t1), every, (h0, h1), every).astype(BF)
        for k in range(4):
            packed[k, rows + half :, :] = out[k * c : (k + 1) * c, :]
        hand_out(scal, packed, send, mine, sem)

    blocks = [*map(Late, normed), *dq, *dkv, *map(Late, attended), *map(Late, dh_low)]
    outs = [((2, size, features), BF, RAW)] * 2
    scratch = [pltpu.VMEM((4, size, features), BF), pltpu.SemaphoreType.DMA((2,))]
    return call(body, outs, scalars, blocks, (), scratch, us=2.1)


def collect(scal, parts, held, sem):
    copies = []
    for i, refs in enumerate(parts):
        core = scal[3] if i < 2 else 1 - scal[3]
        section = scal[2] if i % 2 == 0 else 1 - scal[2]
        size = held.shape[1] // len(refs)
        for j, ref in enumerate(refs):
            place = held.at[2 * core + section, j * size : (j + 1) * size]
            copies.append(pltpu.make_async_copy(ref, place, sem.at[len(copies)]))
    for copy in copies:
        copy.start()
    for copy in copies:
        copy.wait()


def wide_unpack(scalars, mine, mine2, other, other2, inner):
    size, features = mine.shape
    a, half = inner // 4, features // 2

    def body(scal, p0, p1a, p1b, p2, p3a, p3b, down, up, token, held, sem):
        collect(scal, ((p0,), (p1a, p1b), (p2,), (p3a, p3b)), held, sem)
        for k in range(4):
            down[k * a : (k + 1) * a, :] = held[k, :a, :].astype(F32)
            for i in range(2):
                up[i * half : (i + 1) * half, k * a : (k + 1) * a] = held[k, a:, i * a : (i + 1) * a].astype(F32)
        token[...] = jnp.zeros_like(token)

    outs = [((inner, features), F32), ((features, inner), F32), ((8, 128), F32)]
    scratch = [pltpu.VMEM((4, size, features), BF), pltpu.SemaphoreType.DMA((6,))]
    return call(body, outs, scalars, [], [mine, *other, mine2, *other2], scratch, us=5)


def narrow_unpack(scalars, parts, extras, width, token):
    size, features = parts[0].shape
    rows = features // 4
    half, c, own = rows // 2, width // 4, width // 2

    def body(scal, _, p0, p1, p2, p3, e0, e1, pairs, value, extra, out, held, pair, sem, pair_sem):
        last = [pltpu.make_async_copy(e, pair.at[i if i == 0 else 1], pair_sem.at[i]) for i, e in enumerate((e0, e1))]
        for copy in last:
            copy.start()
        collect(scal, ((p0,), (p1,), (p2,), (p3,)), held, sem)
        for copy in last:
            copy.wait()
        for x in range(2):
            for core in range(2):
                k, at = 2 * core + x, (2 * x + core) * rows
                pairs[at : at + rows, 0, :] = held[k, :rows, :width].astype(F32)
                pairs[at : at + rows, 1, :] = held[k, :rows, width:].astype(F32)
                value[at : at + half, :] = held[k, rows : rows + half, :own].astype(F32)
                value[at + half : at + rows, :] = held[k, rows : rows + half, width : width + own].astype(F32)
        for k in range(4):
            out[k * c : (k + 1) * c, :] = held[k, rows + half :, :].astype(F32)
        for i in range(2):
            core = scal[3] if i == 0 else 1 - scal[3]
            at = pl.multiple_of(core * rows, rows)
            cut = pair[i].astype(F32)
            left = pltpu.roll(cut[:, :width], own, 1)
            right = pltpu.roll(cut[:, width:], own, 1)
            extra[pl.ds(at, half), :] = left[:, :own]
            extra[pl.ds(pl.multiple_of(at + half, 8), half), :] = right[:, :own]

    outs = [((features, 2, width), F32)] + [((features, own), F32), ((2 * rows, own), F32), ((width, features), F32)]
    scratch = [
        pltpu.VMEM((4, size, features), BF), pltpu.VMEM((2, half, features), BF),
        pltpu.SemaphoreType.DMA((4,)), pltpu.SemaphoreType.DMA((2,)),
    ]
    return call(body, outs, scalars, [token], list(parts) + list(extras), scratch, us=3)


def swap(value, axis, bits=1):
    count = lax.axis_size(axis)
    return lax.ppermute(value, axis, [(i, i ^ bits) for i in range(count)])


def shift(value, steps):
    count = lax.axis_size("batch")
    first, last = max(0, -steps), min(count, count - steps)
    return lax.ppermute(value, "batch", [(i, i + steps) for i in range(first, last)])


def after(value, *earlier):
    return lax.optimization_barrier((value,) + earlier)[0]


def take(array, index, axis=0):
    return lax.dynamic_index_in_dim(array, index, axis, keepdims=False)


def paired(mine, other, side):
    return jnp.where(side == 0, mine, other), jnp.where(side == 0, other, mine)


class Reduction:
    def __init__(self, grads, pieces):
        self.section = lax.axis_index("section")
        self.send, self.mine = grads
        self.pieces = pieces

    def over_cores(self):
        self.near = swap(self.send, "batch")

    def pair_sum(self, section, start, size):
        cut = [lax.dynamic_slice(a, (section, start, 0), (1, size, a.shape[2]))[0] for a in (self.mine, self.near)]
        return cut[0].astype(F32) + cut[1].astype(F32)

    def prepare(self):
        size = self.mine.shape[1] // self.pieces
        self.sent = [self.pair_sum(1 - self.section, i * size, size).astype(BF) for i in range(self.pieces)]

    def over_sections(self, i=0):
        if i == 0:
            self.came = []
        self.came.append(swap(self.sent[i], "section"))

    def scatter_send(self):
        index = lax.axis_index("batch")
        half = self.mine.shape[1] // 2
        came = self.came if self.pieces == 2 else [self.came[0][:half], self.came[0][half:]]
        cut = [(self.pair_sum(self.section, i * half, half) + came[i].astype(F32)).astype(BF) for i in range(2)]
        *first, near, far = chip_bits()
        for bit in first:
            keep, send = paired(*cut, (index >> bit) & 1)
            total = (keep.astype(F32) + swap(send, "batch", 1 << bit).astype(F32)).astype(BF)
            cut = jnp.split(total, 2, axis=0)
        self.keep, send = paired(*cut, (index >> near) & 1)
        return send

    def exchange_send(self, got):
        self.part = (self.keep.astype(F32) + got.astype(F32)).astype(BF)
        return self.part

    def gather_send(self, got):
        self.part = (self.part.astype(F32) + got.astype(F32)).astype(BF)
        return self.part

    def finish(self, got):
        index = lax.axis_index("batch")
        *first, near, far = chip_bits()
        part = jnp.concatenate(paired(self.part, got, (index >> near) & 1), axis=0)
        for bit in reversed(first):
            part = jnp.concatenate(paired(part, swap(part, "batch", 1 << bit), (index >> bit) & 1), axis=0)
        self.quarter = part


def chip_bits():
    return list(range(1, lax.axis_size("batch").bit_length() - 1))


def swap_all(values, place):
    sizes = [v.shape[0] for v in values]
    got = swap(jnp.concatenate(values, axis=0) if len(values) > 1 else values[0], "batch", 1 << chip_bits()[place])
    ends = [sum(sizes[: i + 1]) for i in range(len(sizes))]
    return [got[end - size : end] for size, end in zip(sizes, ends)]


def tie(value, *others):
    return lax.optimization_barrier((value,) + others)


def forward_layer(scalars, layer, table, w, x=None, ahead=None, carried=None, hooks=None):
    hooks = hooks or {}
    nothing = lambda value: value
    x, normed, q, kv = project(scalars, layer, w["qkv"], table, x=x, ahead=ahead, carried=carried)
    if "projected" in hooks:
        kv = hooks["projected"](kv, q)
    far = shift(kv, 2)
    near = swap(kv, "batch")
    out, amount, tops = attend_local(scalars, q, kv, near)
    far = hooks.get("arrived", nothing)(after(far, out))
    far = [far, swap(far, "batch")]
    att, lse, parts, came = [], [], [], []
    for c in range(CHUNKS):
        a, l, part = attend_far(scalars, layer, c, q[c], far, out, amount, tops, w["out"])
        att.append(a)
        lse.append(l)
        parts.append(part)
        came.append(swap(part, "tensor"))
    came = hooks.get("far", nothing)(came)
    hidden, mlp_in, active, slope, results = [], [], [], [], []
    for c in range(CHUNKS):
        h, m, a, s, part = feed_forward(scalars, layer, table, x[c], parts[c], came[c], w["up"], w["down"])
        hidden.append(h)
        mlp_in.append(m)
        active.append(a)
        slope.append(s)
        results.append((table, h, part))
    kept = dict(x=x, normed=normed, q=q, kv=kv, near=near, far=far, att=att, lse=lse, hidden=hidden,
                mlp_in=mlp_in, active=active, slope=slope)
    return results, kept


def backward_layer(scalars, layer, table, w, kept, dy, returned, steps):
    rows = CHUNKS * dy[0].shape[0]
    dy = list(steps("start", dy))
    d_up, parts, up_sums = [], [], []
    for c in range(CHUNKS):
        if c == 1:
            dy[1] = steps("half", after(dy[1], parts[0][0]))
        grad, part, sums = feed_back(scalars, layer, dy[c], kept["slope"][c], w["up"], w["down"])
        d_up.append(grad)
        up_sums.append(sums)
        parts.append((part, swap(part, "tensor")))
    wide = Reduction(wide_grads(scalars, kept["active"], dy, kept["mlp_in"], d_up), 2)
    parts = steps("fed", parts, wide)
    dh, dh_low, d_att, delta, mid = middle_back(
        scalars, layer, table, kept["hidden"], parts, dy, kept["att"], w["out"]
    )
    d_att = steps("mid", d_att, wide)
    dq, mine, others = attend_far_back(scalars, kept["q"], d_att, kept["lse"], delta, kept["far"])
    total = (mine.astype(F32) + swap(others, "batch").astype(F32)).astype(BF)
    dq = steps("turn", after(dq, total), wide)
    home = shift(total, -2)
    dq, crossing = attend_near_back(scalars, kept["q"], d_att, kept["lse"], delta, kept["near"], dq)
    near = swap(crossing, "batch")
    dq = steps("between", dq, wide)
    dq0, dq1, dk0, dk1 = attend_own_back(scalars, kept["q"], d_att, kept["lse"], delta, kept["kv"], dq)
    dq, dkv = [dq0, dq1], [dk0, dk1]
    home, dq = steps("near", (home, dq), wide)
    dkv_low, parts, in_sums, back = [], [], [], []
    for c in range(CHUNKS):
        again = None if returned is None else returned[c]
        r = project_back(scalars, layer, c, dq[c], dkv[c], near, home, again, w["qkv"])
        dkv_low.append(r[0])
        parts.append((r[1], swap(r[1], "tensor")))
        in_sums.append(r[2])
        back.extend(r[3:])
    narrow = Reduction(narrow_grads(scalars, kept["normed"], dq, dkv_low, kept["att"], dh_low), 1)
    parts = steps("proj", parts, wide, narrow)
    parts = steps("last", parts, wide, narrow)
    dx, dx_low, last = last_back(scalars, table, kept["x"], parts, dh)
    up, inn = [a + b for a, b in (up_sums, in_sums)]
    blank = jnp.zeros((TABLE - BUP - 2, up.shape[1]), F32)
    small = jnp.concatenate(
        [last[0:1], mid[0:1], last[1:2], mid[1:2], mid[2:4], inn[0:2], up[0:2], blank], axis=0
    )
    return dx, dx_low, back, wide, narrow, small


def local(
    tokens, block_place, cotangent, norm_gains, norm_biases, query_key, query_bias, value_own, value_bias,
    value_extra, out_weight, out_bias, up_weight, up_bias, down_weight, down_bias,
):
    section = lax.axis_index("section")
    tensor = lax.axis_index("tensor")
    core = lax.axis_index("batch") % 2
    micros, _, half_rows, features = tokens.shape
    width = query_bias.shape[1]
    own_width = value_own.shape[2]
    inner = up_weight.shape[2]
    assert micros == 2 and lax.axis_size("section") == 2 and lax.axis_size("tensor") == 2
    assert 2 * own_width == width and 2 * width == features and inner == 2 * features

    place = take(block_place, section)[0]
    scalars = jnp.stack([place & 1, place >> 1, section, core]).astype(jnp.int32)

    my_tokens = take(tokens, section)[0]
    x = paired(my_tokens, swap(my_tokens, "tensor"), tensor)

    def row(*pieces):
        flat = jnp.concatenate([p.reshape(-1) for p in pieces])
        return jnp.pad(flat, (0, features - flat.shape[0]))[None]

    blank = jnp.zeros((width,), F32)
    own_table = jnp.concatenate(
        [norm_gains[0], norm_biases[0], out_bias, down_bias, row(query_bias[0]), row(blank, value_bias[0]),
         up_bias[0].reshape(2, features), jnp.zeros((TABLE - BUP - 2, features), F32)], axis=0
    )
    def half_of(weight):
        return take(weight.reshape((2, weight.shape[0] // 2) + weight.shape[1:]), core)

    query_keys = query_key[0].reshape(features, 2 * width)
    extra = jnp.where(section == 0, value_extra, jnp.zeros_like(value_extra))
    halves = [half_of(query_keys), jnp.concatenate([half_of(value_own[0]), half_of(extra)], axis=1)]
    qkv = jnp.concatenate([query_keys, value_own[0], extra], axis=1)
    qkv_got = [swap(h, "section") for h in halves]
    other_table = swap(own_table, "section")
    out_got = swap(half_of(out_weight[0]), "section")
    up_got = swap(after(half_of(up_weight[0]), x[0]), "section")
    down_got = swap(after(half_of(down_weight[0]), x[0]), "section")
    tables = paired(own_table, other_table, section)
    qkv_got[0], qkv_got[1], out_got, qkv, scalars, *rest = tie(*qkv_got, out_got, qkv, scalars, *tables, *x)
    tables, x = rest[:2], rest[2:]
    w = dict(qkv=(qkv, *qkv_got, *[swap(g, "batch") for g in qkv_got]))
    late = dict(up=up_got, down=down_got)

    def on_projected(kv, q):
        mine, kv = tie(take(cotangent, section)[0], kv)
        late["dy"] = mine, swap(mine, "tensor")
        w["out"] = (out_weight[0], out_got, swap(after(out_got, kv), "batch"))
        return kv

    def on_arrived(far):
        mine, other = late["dy"]
        far, got, other = tie(far, late["up"], other)
        late["dy"] = paired(mine, other, tensor)
        w["up"] = (up_weight[0], got, swap(got, "batch"))
        return far

    def on_far(came):
        *came, got = tie(*came, late["down"])
        w["down"] = (down_weight[0], got, swap(got, "batch"))
        return came

    first, kept0 = forward_layer(
        scalars, 0, tables[0], w, x=x, hooks=dict(projected=on_projected, arrived=on_arrived, far=on_far)
    )
    first = [r + (swap(r[2], "tensor"),) for r in first]
    second, kept1 = forward_layer(scalars, 1, tables[1], w, ahead=first, carried=kept0["kv"])
    y0 = kept1["x"]

    def my_half(chunks):
        return jnp.where(tensor == 0, chunks[0], chunks[1])

    def by_section(mine0, mine1, kind):
        mine = jnp.where(section == 0, mine0, mine1)
        other = swap(jnp.where(section == 0, mine1, mine0).astype(kind), "section")
        return mine, other

    def steps1(number, values, wide=None, narrow=None):
        leaves, tree = jax.tree.flatten(values)
        if number == "fed":
            *leaves, wide.send = tie(*leaves, wide.send)
            wide.over_cores()
        if number == "mid":
            *leaves, wide.near = tie(*leaves, wide.near)
            wide.prepare()
            *leaves, wide.sent[0], wide.sent[1] = tie(*leaves, *wide.sent)
            wide.over_sections(0)
        if number == "between":
            *leaves, wide.came[0], wide.sent[1] = tie(*leaves, wide.came[0], wide.sent[1])
            wide.over_sections(1)
        if number == "near":
            *leaves, wide.came[1] = tie(*leaves, wide.came[1])
            late["a1"] = swap_all([wide.scatter_send()], -2)[0]
        if number == "proj":
            *leaves, narrow.send, got = tie(*leaves, narrow.send, late["a1"])
            narrow.over_cores()
            sent = wide.exchange_send(got)
            *leaves, sent = tie(*leaves, sent)
            late["b1"] = swap_all([sent], -1)[0]
        if number == "last":
            *leaves, narrow.near = tie(*leaves, narrow.near)
            narrow.prepare()
            *leaves, narrow.sent[0] = tie(*leaves, narrow.sent[0])
            narrow.over_sections()
        return jax.tree.unflatten(tree, leaves)

    dx1, dx1_low, back, wide1, narrow1, small1 = backward_layer(scalars, 1, tables[1], w, kept1, late["dy"], None, steps1)

    def steps0(number, values, wide=None, narrow=None):
        leaves, tree = jax.tree.flatten(values)
        if number == "half":
            *leaves, narrow1.came[0], got = tie(*leaves, narrow1.came[0], late["b1"])
            sent = [wide1.gather_send(got), narrow1.scatter_send()]
            *leaves, sent[0], sent[1] = tie(*leaves, *sent)
            late["c1"] = swap_all(sent, -2)
        if number == "fed":
            *leaves, wide.send, got, narrow_got = tie(*leaves, wide.send, *late["c1"])
            wide.over_cores()
            wide1.finish(got)
            sent = narrow1.exchange_send(narrow_got)
            *leaves, sent = tie(*leaves, sent)
            late["d1"] = swap_all([sent], -1)[0]
        if number == "mid":
            *leaves, wide.near, got = tie(*leaves, wide.near, late["d1"])
            wide.prepare()
            *leaves, wide.sent[0], wide.sent[1] = tie(*leaves, *wide.sent)
            wide.over_sections(0)
            late["e1"] = narrow1.gather_send(got)
        if number == "between":
            *leaves, wide.came[0], wide.sent[1] = tie(*leaves, wide.came[0], wide.sent[1])
            wide.over_sections(1)
        if number == "near":
            *leaves, wide.came[1] = tie(*leaves, wide.came[1])
            late["a0"] = swap_all([wide.scatter_send(), late["e1"]], -2)
        if number == "proj":
            *leaves, narrow.send, got, narrow_got = tie(*leaves, narrow.send, *late["a0"])
            narrow1.finish(narrow_got)
            narrow.over_cores()
            sent = wide.exchange_send(got)
            *leaves, sent = tie(*leaves, sent)
            late["b0"] = swap_all([sent], -1)[0]
            *leaves, narrow.near = tie(*leaves, narrow.near)
            narrow.prepare()
            *leaves, narrow.sent[0] = tie(*leaves, narrow.sent[0])
            narrow.over_sections()
            late["y1"] = [swap(after(r[2], leaves[0]), "tensor") for r in second]
        if number == "last":
            *leaves, narrow.came[0] = tie(*leaves, narrow.came[0])
        return jax.tree.unflatten(tree, leaves)

    dx0, dx0_low, _, wide0, narrow0, small0 = backward_layer(scalars, 0, tables[0], w, kept0, dx1_low, back, steps0)
    sums = jnp.stack([small0, small1])
    sums = sums + swap(sums, "batch")
    got, sums, *rest = tie(late["b0"], sums, *late["y1"], my_half(dx0), my_half(dx1))
    y_came, grads = rest[:2], rest[2:]
    sent = [narrow0.scatter_send(), wide0.gather_send(got)]
    sent[0], sent[1], sums, grads[0], grads[1] = tie(*sent, sums, *grads)
    late["c0"] = swap_all(sent, -2)
    table = take(sums, section) + swap(take(sums, 1 - section), "section")
    mine_grads, other_grads = by_section(*grads, BF)
    y1 = my_half(
        [(r[1] + r[0][BDOWN : BDOWN + 1] + r[2].astype(F32) + c.astype(F32)).astype(BF) for r, c in zip(second, y_came)]
    )
    mine_out, other_out = by_section(my_half(y0), y1, BF)

    narrow0_got, wide0_got, table, other_grads, other_out = tie(
        *late["c0"], table, other_grads, other_out
    )
    sent = narrow0.exchange_send(narrow0_got)
    wide0.finish(wide0_got)
    wide_mine = jnp.where(section == 0, wide0.quarter, wide1.quarter)
    wide_sent = jnp.split(jnp.where(section == 0, wide1.quarter, wide0.quarter), 2, axis=0)
    sent, wide_sent[0] = tie(sent, wide_sent[0])
    got = swap_all([sent], -1)[0]
    wide_other = [swap(wide_sent[0], "section")]
    for bit in chip_bits()[:-1]:
        table = table + swap(table, "batch", 1 << bit)

    got, table, wide_other[0], wide_sent[1] = tie(got, table, wide_other[0], wide_sent[1])
    sent = narrow0.gather_send(got)
    got = swap_all([sent], -2)[0]
    wide_mine2, wide_other2 = swap(wide_mine, "batch"), swap(wide_other[0], "batch")
    table = table + swap(table, "batch", 1 << chip_bits()[-1])
    wide_other.append(swap(wide_sent[1], "section"))

    got, wide_other[1], table = tie(got, wide_other[1], table)
    narrow0.finish(got)
    outputs = jnp.stack(paired(mine_out, other_out, section))
    input_grads = jnp.stack(paired(mine_grads.astype(F32), other_grads.astype(F32), section))

    def gathered(first, second):
        mine = jnp.where(section == 0, first, second)
        other = swap(jnp.where(section == 0, second, first), "section")
        mine2 = swap(mine, "batch")
        other, mine2 = tie(other, mine2, token)[:2]
        return mine, other, mine2, swap(other, "batch")

    d_down, d_up, token = wide_unpack(
        scalars, wide_mine, wide_mine2, wide_other, [wide_other2, swap(wide_other[1], "batch")], inner
    )
    rows = features // 4
    extra = narrow0.quarter[rows : rows + rows // 2]
    extras = (extra, swap(extra, "batch"))
    token, *extras = tie(token, *extras)
    d_qk, d_v, d_extra, d_out = narrow_unpack(
        scalars, gathered(narrow0.quarter, narrow1.quarter), extras, width, token
    )
    return (
        outputs.reshape(1, micros, 1, half_rows, features),
        input_grads.reshape(1, micros, 1, half_rows, features),
        table[GAIN0 : GAIN1 + 1][None],
        table[BIAS0 : BIAS1 + 1][None],
        d_qk.reshape(1, features, 2, width),
        table[BQ : BQ + 1, :width],
        d_v[None],
        table[BKV : BKV + 1, width : width + own_width],
        d_extra,
        d_out[None],
        table[BO : BO + 1],
        d_up[None],
        table[BUP : BUP + 2].reshape(1, inner),
        d_down[None],
        table[BDOWN : BDOWN + 1],
    )


def solution(mesh):
    return jax.shard_map(
        local,
        mesh=mesh,
        in_specs=(
            P(None, "batch", "tensor", None),
            P(None, "batch"),
            P(None, "batch", "tensor", None),
            P("section", None, None),
            P("section", None, None),
            P("section", None, None, "tensor"),
            P("section", "tensor"),
            P("section", None, "tensor"),
            P("section", "tensor"),
            P(None, "tensor"),
            P("section", "tensor", None),
            P("section", None),
            P("section", None, "tensor"),
            P("section", "tensor"),
            P("section", "tensor", None),
            P("section", None),
        ),
        out_specs=(
            P("section", None, "batch", "tensor", None),
            P("section", None, "batch", "tensor", None),
            P("section", None, None),
            P("section", None, None),
            P("section", None, None, "tensor"),
            P("section", "tensor"),
            P("section", None, "tensor"),
            P("section", "tensor"),
            P("section", "tensor"),
            P("section", "tensor", None),
            P("section", None),
            P("section", None, "tensor"),
            P("section", "tensor"),
            P("section", "tensor", None),
            P("section", None),
        ),
        check_vma=False,
    )
```

```python
import jax
import jax.numpy as jnp
from jax import lax
from jax.experimental import pallas as pl
from jax.experimental.pallas import tpu as pltpu
from jax.sharding import PartitionSpec as P

F32 = jnp.float32
BF = jnp.bfloat16
LOW = -1e30
HEAD = 64
CHUNKS = 2

GAIN0, GAIN1, BIAS0, BIAS1, BO, BDOWN, BQ, BKV, BUP = range(9)
TABLE = 16

WHOLE = pl.BlockSpec(memory_space=pltpu.VMEM)
SCALARS = pl.BlockSpec(memory_space=pltpu.SMEM)
FAR_OFF = pl.BlockSpec(memory_space=pltpu.HBM)


def dot_nn(a, b):
    return lax.dot_general(a, b, (((1,), (0,)), ((), ())), preferred_element_type=F32)


def dot_nt(a, b):
    return lax.dot_general(a, b, (((1,), (1,)), ((), ())), preferred_element_type=F32)


def dot_tn(a, b):
    return lax.dot_general(a, b, (((0,), (0,)), ((), ())), preferred_element_type=F32)


class Late:
    def __init__(self, array):
        self.array = array


def in_hbm(array):
    return pltpu.with_memory_space_constraint(array, pltpu.HBM)


FLUSH = []


def flush(*refs):
    for ref in refs:
        for k, (held, copy, started) in enumerate(FLUSH[-1]):
            if held is ref and not started:
                copy.start()
                FLUSH[-1][k] = (held, copy, True)


LATER, RAW = 1, 2


def call(inner_body, outs, scalars, blocks, remote=(), scratch=(), us=1.0, limit=48):
    shapes = [pltpu.HBM(o[0], o[1]) if len(o) > 2 else jax.ShapeDtypeStruct(o[0], o[1]) for o in outs]
    kinds = [o[2] if len(o) > 2 else 0 for o in outs]
    late = [i for i, b in enumerate(blocks) if isinstance(b, Late)]
    blocks = [in_hbm(b.array) if isinstance(b, Late) else b for b in blocks]
    remote = [in_hbm(r) for r in remote]
    n_in, n_out = 1 + len(blocks) + len(remote), len(outs)
    later = [i for i, kind in enumerate(kinds) if kind == LATER]
    spare = [pltpu.VMEM(blocks[i].shape, blocks[i].dtype) for i in late]
    spare += [pltpu.VMEM(shapes[i].shape, shapes[i].dtype) for i in later]
    sems = [pltpu.SemaphoreType.DMA((max(len(late), 1),)), pltpu.SemaphoreType.DMA((max(len(later), 1),))]

    def body(*refs):
        refs = list(refs)
        first = n_in + n_out
        n_spare = len(spare)
        held, (sem, out_sem), own = refs[first : first + n_spare], refs[first + n_spare : first + n_spare + 2], refs[first + n_spare + 2 :]
        copies = [pltpu.make_async_copy(refs[1 + i], v, sem.at[k]) for k, (i, v) in enumerate(zip(late, held))]
        back = [
            pltpu.make_async_copy(v, refs[n_in + i], out_sem.at[k])
            for k, (i, v) in enumerate(zip(later, held[len(late) :]))
        ]
        for copy in copies:
            copy.start()
        for copy in copies:
            copy.wait()
        for i, v in zip(late, held):
            refs[1 + i] = v
        for i, v in zip(later, held[len(late) :]):
            refs[n_in + i] = v
        FLUSH.append([(held[len(late) + k], copy, False) for k, copy in enumerate(back)])
        inner_body(*refs[:first], *own)
        flush(*held[len(late) :])
        FLUSH.pop()
        for copy in back:
            copy.wait()

    return pl.pallas_call(
        body,
        out_shape=shapes,
        in_specs=[SCALARS] + [FAR_OFF if i in late else WHOLE for i in range(len(blocks))] + [FAR_OFF] * len(remote),
        out_specs=[FAR_OFF if kind else WHOLE for kind in kinds],
        scratch_shapes=spare + sems + list(scratch),
        compiler_params=pltpu.CompilerParams(vmem_limit_bytes=limit * 1024 * 1024),
        cost_estimate=pl.CostEstimate(flops=int(us * 1.2e8), bytes_accessed=int(us * 2e5), transcendentals=0),
    )(scalars, *blocks, *remote)


def fetch_start(scalars, layer, own, got, other, held, sem):
    half = held.shape[0] // 2

    @pl.when(scalars[2] == layer)
    def _():
        pltpu.make_async_copy(own, held, sem).start()

    @pl.when(scalars[2] != layer)
    def _():
        mine = pl.multiple_of(scalars[3] * half, half)
        rest = pl.multiple_of((1 - scalars[3]) * half, half)
        pltpu.make_async_copy(got, held.at[pl.ds(mine, half)], sem).start()
        pltpu.make_async_copy(other, held.at[pl.ds(rest, half)], sem).start()


def fetch_parts(scalars, layer, own, got, other, held, sem):
    half = held.shape[0] // 2

    @pl.when(scalars[2] == layer)
    def _():
        pltpu.make_async_copy(own, held, sem).start()

    @pl.when(scalars[2] != layer)
    def _():
        for side, refs in ((scalars[3], got), (1 - scalars[3], other)):
            at = pl.ds(pl.multiple_of(side * half, half), half)
            start = 0
            for ref in refs:
                end = start + ref.shape[1]
                pltpu.make_async_copy(ref, held.at[at, start:end], sem).start()
                start = end


def fetch_wait(own, held, sem):
    pltpu.make_async_copy(own, held, sem).wait()


def held_like(*weights):
    return [pltpu.VMEM(w[0].shape, BF) for w in weights] + [pltpu.SemaphoreType.DMA] * len(weights)


def norm_parts(v):
    centred = v - jnp.mean(v, axis=-1, keepdims=True)
    rate = lax.rsqrt(jnp.mean(centred * centred, axis=-1, keepdims=True) + 1e-05)
    return centred * rate, rate


def norm_grad(v, gain, grad):
    unit, rate = norm_parts(v)
    scaled = grad * gain
    inner = jnp.mean(scaled * unit, axis=-1, keepdims=True)
    result = rate * (scaled - jnp.mean(scaled, axis=-1, keepdims=True) - unit * inner)
    return result, jnp.sum(grad * unit, axis=0, keepdims=True), jnp.sum(grad, axis=0, keepdims=True)


def gelu_both(u):
    factor = 0.7978845608028654
    square = u * u
    t = jnp.tanh(factor * u * (1.0 + 0.044715 * square))
    half = 0.5 * (1.0 + t)
    slope = half + (0.5 * factor) * u * (1.0 - t * t) * (1.0 + (3 * 0.044715) * square)
    return u * half, slope


def project(scalars, layer, weights, table, x=None, ahead=None, carried=None):
    if ahead is None:
        rows, features = x[0].shape
        blocks = [table, *x]
    else:
        rows, features = ahead[0][1].shape
        blocks = [table, ahead[0][0], Late(carried)]
        for chunk in ahead:
            blocks.extend([Late(chunk[1]), *chunk[2:]])
    width = weights[0].shape[1] // 3

    def body(scal, tab, *refs):
        given = refs[: len(blocks) - 1]
        own, *parts = refs[len(blocks) - 1 : len(blocks) + 4]
        outs = refs[len(blocks) + 4 : -2]
        held, sem = refs[-2:]
        fetch_parts(scal, layer, own, parts[:2], parts[2:], held, sem)
        for c in range(CHUNKS):
            at = slice(c * rows, (c + 1) * rows)
            if ahead is None:
                v = given[c][...].astype(F32)
            else:
                before, carry = given[:2]
                hid, mine, came = given[2 + 3 * c : 5 + 3 * c]
                y = hid[...] + before[BDOWN : BDOWN + 1] + mine[...].astype(F32) + came[...].astype(F32)
                low = y.astype(BF)
                outs[5 + c][...] = low
                v = low.astype(F32)
            unit, _ = norm_parts(v)
            normed = (unit * tab[GAIN0 : GAIN0 + 1] + tab[BIAS0 : BIAS0 + 1]).astype(BF)
            outs[c][...] = normed
            if c == 0:
                fetch_wait(own, held, sem)
            q = dot_nn(normed, held[:, :width]) + tab[BQ : BQ + 1, :width]
            outs[2 + c][...] = (q.astype(BF).astype(F32) * 0.125).astype(BF)
            kv = dot_nn(normed, held[:, width:]) + tab[BKV : BKV + 1]
            if ahead is not None:
                rolled = pltpu.roll(carry[at, :].astype(F32), width // 2, 1)
                lane = lax.broadcasted_iota(jnp.int32, kv.shape, 1)
                kv = jnp.where(lane >= width + width // 2, rolled, kv)
            outs[4][at, :] = kv.astype(BF)

    outs = [((rows, features), BF, LATER)] * 2 + [((rows, width), BF)] * 2 + [((2 * rows, 2 * width), BF)]
    if ahead is not None:
        outs += [((rows, features), BF, LATER)] * 2
    r = call(body, outs, scalars, blocks, weights, held_like(weights), us=2.5)
    return list(x) if ahead is None else r[5:], r[:2], r[2:4], r[4]


def low_lanes(shape):
    return lax.broadcasted_iota(jnp.int32, shape, 1) < HEAD


def head_of(pair, sub, fill):
    keep = low_lanes(pair.shape)
    return jnp.where(keep if sub == 0 else ~keep, pair, jnp.full_like(pair, fill))


def halves_of(ref, size):
    return tuple(ref.at[i * size : (i + 1) * size] for i in range(ref.shape[0] // size))


def spans(p, width):
    return slice(p * 128, (p + 1) * 128), slice(width + p * 128, width + (p + 1) * 128)


def scored(q, tiles, p, width, masks):
    ks, vs = spans(p, width)
    tops, outs = [], []
    for sub in range(2):
        scores = [dot_nt(q, head_of(t[:, ks], sub, 0)) for t in tiles]
        scores = [s if m is None else jnp.where(m, s, LOW) for s, m in zip(scores, masks)]
        top = scores[0].max(axis=1, keepdims=True)
        for s in scores[1:]:
            top = jnp.maximum(top, s.max(axis=1, keepdims=True))
        total = None
        for s, t in zip(scores, tiles):
            part = dot_nn(jnp.exp(s - top).astype(BF), head_of(t[:, vs], sub, 1))
            total = part if total is None else total + part
        tops.append(top)
        outs.append(total)
    low = low_lanes(outs[0].shape)
    value = jnp.where(low, outs[0], outs[1])
    amount = pltpu.roll(jnp.where(low, outs[1], outs[0]), HEAD, 1)
    return tops, value, amount


def attend_local(scalars, q, kv, near):
    size, width = q[0].shape
    rows = size * CHUNKS

    def body(scal, q0, q1, k_all, n_all, out, amount, tops):
        own = halves_of(k_all, size)
        row = lax.broadcasted_iota(jnp.int32, (size, size), 0)
        col = lax.broadcasted_iota(jnp.int32, (size, size), 1)
        causal = col <= row

        def run(extra):
            for c, q_ref in enumerate((q0, q1)):
                at = slice(c * size, (c + 1) * size)
                tiles = list(extra) + [own[i] for i in range(c + 1)]
                masks = [None] * (len(tiles) - 1) + [causal]
                for p in range(width // 128):
                    span = slice(p * 128, (p + 1) * 128)
                    top, value, total = scored(q_ref[:, span], tiles, p, width, masks)
                    out[at, span] = value
                    amount[at, span] = total
                    tops[at, 2 * p : 2 * p + 1] = top[0]
                    tops[at, 2 * p + 1 : 2 * p + 2] = top[1]

        @pl.when(scal[0] == 1)
        def _():
            run(halves_of(n_all, size))

        @pl.when(scal[0] == 0)
        def _():
            run(())

    outs = [((rows, width), F32), ((rows, width), F32), ((rows, 128), F32)]
    return call(body, outs, scalars, [*q, kv, near], us=5)


def attend_far(scalars, layer, c, q, far, out, amount, tops, weights):
    size, width = q.shape
    features = weights[0].shape[1]

    def body(scal, q_ref, fa, fb, out_ref, amount_ref, tops_ref, own, got, other, att, lse, part, stats, held, sem):
        fetch_start(scal, layer, own, got, other, held, sem)
        at = slice(c * size, (c + 1) * size)
        stats[...] = jnp.zeros_like(stats)

        def finish(p, value, total, top0, top1):
            span = slice(p * 128, (p + 1) * 128)
            att[:, span] = (value / total).astype(BF)
            logs = jnp.log(total)
            stats[:, 2 * p : 2 * p + 1] = top0 + logs[:, 0:1]
            stats[:, 2 * p + 1 : 2 * p + 2] = top1 + logs[:, HEAD : HEAD + 1]

        @pl.when(scal[1] == 0)
        def _():
            for p in range(width // 128):
                span = slice(p * 128, (p + 1) * 128)
                finish(p, out_ref[at, span], amount_ref[at, span], tops_ref[at, 2 * p : 2 * p + 1], tops_ref[at, 2 * p + 1 : 2 * p + 2])

        @pl.when(scal[1] == 1)
        def _():
            for p in range(width // 128):
                span = slice(p * 128, (p + 1) * 128)
                new, value, total = scored(q_ref[:, span], halves_of(fa, size) + halves_of(fb, size), p, width, [None] * 4)
                tops_all, olds, news = [], [], []
                for sub in range(2):
                    before = tops_ref[at, 2 * p + sub : 2 * p + sub + 1]
                    top = jnp.maximum(before, new[sub])
                    tops_all.append(top)
                    olds.append(jnp.exp(before - top))
                    news.append(jnp.exp(new[sub] - top))
                low = low_lanes(value.shape)
                keep = jnp.where(low, olds[0], olds[1])
                take = jnp.where(low, news[0], news[1])
                finish(p, out_ref[at, span] * keep + value * take, amount_ref[at, span] * keep + total * take, *tops_all)

        lse[...] = jnp.transpose(stats[...])[0:8, :]
        flush(att, lse)
        fetch_wait(own, held, sem)
        part[...] = dot_nn(att[...], held[...]).astype(BF)

    outs = [((size, width), BF, LATER), ((8, size), F32, LATER), ((size, features), BF)]
    scratch = [pltpu.VMEM((size, 128), F32)] + held_like(weights)
    return call(body, outs, scalars, [q, *far, out, amount, tops], weights, scratch, us=4.5)


def back_tile(p, width, q, do, lse, delta, kv, mask):
    ks, vs = spans(p, width)
    dq, dks, dvs = None, [], []
    for sub in range(2):
        h = 2 * p + sub
        key = head_of(kv[:, ks], sub, 0)
        scores = dot_nt(key, q)
        weight = jnp.exp(scores - lse[h : h + 1, :])
        if mask is not None:
            weight = jnp.where(mask, weight, 0.0)
        d_weight = dot_nt(head_of(kv[:, vs], sub, 0), do)
        d_score = (weight * (d_weight - delta[h : h + 1, :])).astype(BF)
        dvs.append(dot_nn(weight.astype(BF), do))
        dks.append(dot_nn(d_score, q))
        d = dot_tn(key, d_score)
        dq = d if dq is None else dq + d
    low = low_lanes(dks[0].shape)
    return dq, jnp.where(low, dks[0], dks[1]), jnp.where(low, dvs[0], dvs[1])


def staged(size, width):
    rows = size * CHUNKS
    return [pltpu.VMEM((rows, width), BF), pltpu.VMEM((rows, width), BF), pltpu.VMEM((8, rows), F32), pltpu.VMEM((8, rows), F32)]


def stage(size, given, held):
    for k, ref in enumerate(held):
        for c in range(CHUNKS):
            at = slice(c * size, (c + 1) * size)
            if k < 2:
                ref[at, :] = given[2 * k + c][...]
            else:
                ref[:, at] = given[2 * k + c][...]


def back_over(held, width, size, sources, dq_ref):
    q, do, lse, delta = held
    for p in range(width // 128):
        ks, vs = spans(p, width)
        total = None
        for source, ref, start in sources:
            for i in range(CHUNKS):
                at = slice(start + i * size, start + (i + 1) * size)
                tile = source.at[i * size : (i + 1) * size]
                dq, dk, dv = back_tile(p, width, q[:, ks], do[:, ks], lse, delta, tile, None)
                total = dq if total is None else total + dq
                ref[at, ks] = dk.astype(BF)
                ref[at, vs] = dv.astype(BF)
        dq_ref[:, ks] += jnp.transpose(total)


def attend_far_back(scalars, q, do, lse, delta, far):
    size, width = q[0].shape
    rows = size * CHUNKS

    def body(scal, q0, q1, o0, o1, l0, l1, d0, d1, fa, fb, dq_out, mine, others, *held):
        dq_out[...] = jnp.zeros_like(dq_out)

        @pl.when(scal[1] == 1)
        def _():
            stage(size, (q0, q1, o0, o1, l0, l1, d0, d1), held)
            back_over(held, width, size, [(fb, others, 0), (fa, mine, 0)], dq_out)

        @pl.when(scal[1] == 0)
        def _():
            mine[...] = jnp.zeros_like(mine)
            others[...] = jnp.zeros_like(others)

    outs = [((rows, width), F32), ((rows, 2 * width), BF), ((rows, 2 * width), BF)]
    blocks = [*map(Late, q), *do, *map(Late, lse), *delta, *map(Late, far)]
    return call(body, outs, scalars, blocks, (), staged(size, width), us=12)


def attend_near_back(scalars, q, do, lse, delta, near, dq_before):
    size, width = q[0].shape
    rows = size * CHUNKS

    def body(scal, q0, q1, o0, o1, l0, l1, d0, d1, n_all, before, dq_out, crossing, *held):
        dq_out[...] = before[...]

        @pl.when(scal[0] == 1)
        def _():
            stage(size, (q0, q1, o0, o1, l0, l1, d0, d1), held)
            back_over(held, width, size, [(n_all, crossing, 0)], dq_out)

        @pl.when(scal[0] == 0)
        def _():
            crossing[...] = jnp.zeros_like(crossing)

    outs = [((rows, width), F32), ((rows, 2 * width), BF)]
    blocks = [*map(Late, q), *do, *map(Late, lse), *delta, Late(near), dq_before]
    return call(body, outs, scalars, blocks, (), staged(size, width), us=0.2)


def attend_own_back(scalars, q, do, lse, delta, kv, dq_before):
    size, width = q[0].shape
    rows = size * CHUNKS

    def body(scal, q0, q1, o0, o1, l0, l1, d0, d1, k_all, before, dq0, dq1, dk0, dk1, *held):
        stage(size, (q0, q1, o0, o1, l0, l1, d0, d1), held)
        qs, dos, lses, deltas = held
        key = lax.broadcasted_iota(jnp.int32, (size, rows), 0)
        query = lax.broadcasted_iota(jnp.int32, (size, rows), 1)
        causal = key <= query
        for p in range(width // 128):
            ks, vs = spans(p, width)
            k0, k1 = halves_of(k_all, size)
            first, dk, dv = back_tile(p, width, qs[:, ks], dos[:, ks], lses, deltas, k0, causal)
            dk0[:, ks] = dk
            dk0[:, vs] = dv
            late = [ref.at[:, size:rows] for ref in (lses, deltas)]
            second, dk, dv = back_tile(p, width, qs[size:, ks], dos[size:, ks], *late, k1, causal[:, :size])
            dk1[:, ks] = dk
            dk1[:, vs] = dv
            first, second = jnp.transpose(first[:, :size]), jnp.transpose(first[:, size:] + second)
            dq0[:, ks] = ((before[:size, ks] + first) * 0.125).astype(BF)
            dq1[:, ks] = ((before[size:, ks] + second) * 0.125).astype(BF)

    outs = [((size, width), BF)] * 2 + [((size, 2 * width), F32)] * 2
    blocks = [*map(Late, q), *do, *map(Late, lse), *delta, Late(kv), dq_before]
    return call(body, outs, scalars, blocks, (), staged(size, width), us=0.2)


def feed_forward(scalars, layer, table, x, mine, came, up, down):
    rows, features = x.shape
    inner = up[0].shape[1]

    def body(scal, tab, x_ref, mine_ref, came_ref, u_own, u_got, u_other, d_own, d_got, d_other,
             hidden, mlp_in, active, slope, part, up_held, down_held, up_sem, down_sem):
        fetch_start(scal, layer, u_own, u_got, u_other, up_held, up_sem)
        fetch_start(scal, layer, d_own, d_got, d_other, down_held, down_sem)
        h = x_ref[...].astype(F32) + (mine_ref[...].astype(F32) + came_ref[...].astype(F32)) + tab[BO : BO + 1]
        hidden[...] = h
        unit, _ = norm_parts(h)
        low = (unit * tab[GAIN1 : GAIN1 + 1] + tab[BIAS1 : BIAS1 + 1]).astype(BF)
        mlp_in[...] = low
        flush(hidden, mlp_in)
        fetch_wait(u_own, up_held, up_sem)
        for j in range(inner // features):
            cols = slice(j * features, (j + 1) * features)
            value, grad = gelu_both(dot_nn(low, up_held[:, cols]) + tab[BUP + j : BUP + j + 1])
            active[:, cols] = value.astype(BF)
            slope[:, cols] = grad.astype(BF)
        flush(active, slope)
        fetch_wait(d_own, down_held, down_sem)
        part[...] = dot_nn(active[...], down_held[...]).astype(BF)

    outs = [((rows, features), F32, LATER), ((rows, features), BF, LATER), ((rows, inner), BF, LATER), ((rows, inner), BF, LATER), ((rows, features), BF)]
    return call(body, outs, scalars, [table, Late(x), mine, came], [*up, *down], held_like(up, down), us=4)


def feed_back(scalars, layer, dy, slope, up, down):
    rows, features = dy.shape
    inner = up[0].shape[1]

    def body(scal, dy_ref, slope_ref, u_own, u_got, u_other, d_own, d_got, d_other,
             d_up, part, sums, up_held, down_held, up_sem, down_sem):
        fetch_start(scal, layer, d_own, d_got, d_other, down_held, down_sem)
        fetch_start(scal, layer, u_own, u_got, u_other, up_held, up_sem)
        sums[...] = jnp.zeros_like(sums)
        fetch_wait(d_own, down_held, down_sem)
        for j in range(inner // features):
            cols = slice(j * features, (j + 1) * features)
            grad = (dot_nt(dy_ref[...], down_held[cols, :]) * slope_ref[:, cols].astype(F32)).astype(BF)
            d_up[:, cols] = grad
            sums[j : j + 1, :] = jnp.sum(grad.astype(F32), axis=0, keepdims=True)
        fetch_wait(u_own, up_held, up_sem)
        part[...] = dot_nt(d_up[...], up_held[...]).astype(BF)

    outs = [((rows, inner), BF), ((rows, features), BF), ((8, features), F32)]
    return call(body, outs, scalars, [dy, Late(slope)], [*up, *down], held_like(up, down), us=1.0)


def feed_both(scalars, layer, table, x, mine, came, dy, up, down):
    rows, features = x.shape
    inner = up[0].shape[1]

    def body(scal, tab, x_ref, mine_ref, came_ref, dy_ref, u_own, u_got, u_other, d_own, d_got, d_other,
             hidden, mlp_in, active, result, d_up, part, sums, up_held, down_held, up_sem, down_sem):
        fetch_start(scal, layer, u_own, u_got, u_other, up_held, up_sem)
        fetch_start(scal, layer, d_own, d_got, d_other, down_held, down_sem)
        h = x_ref[...].astype(F32) + (mine_ref[...].astype(F32) + came_ref[...].astype(F32)) + tab[BO : BO + 1]
        hidden[...] = h
        unit, _ = norm_parts(h)
        low = (unit * tab[GAIN1 : GAIN1 + 1] + tab[BIAS1 : BIAS1 + 1]).astype(BF)
        mlp_in[...] = low
        flush(hidden, mlp_in)
        sums[...] = jnp.zeros_like(sums)
        fetch_wait(u_own, up_held, up_sem)
        fetch_wait(d_own, down_held, down_sem)
        for j in range(inner // features):
            cols = slice(j * features, (j + 1) * features)
            value, slope = gelu_both(dot_nn(low, up_held[:, cols]) + tab[BUP + j : BUP + j + 1])
            active[:, cols] = value.astype(BF)
            grad = (dot_nt(dy_ref[...], down_held[cols, :]) * slope).astype(BF)
            d_up[:, cols] = grad
            sums[j : j + 1, :] = jnp.sum(grad.astype(F32), axis=0, keepdims=True)
        flush(active)
        part[...] = dot_nt(d_up[...], up_held[...]).astype(BF)
        result[...] = dot_nn(active[...], down_held[...]).astype(BF)

    outs = [
        ((rows, features), F32, LATER), ((rows, features), BF, LATER), ((rows, inner), BF, LATER), ((rows, features), BF, LATER),
        ((rows, inner), BF), ((rows, features), BF), ((8, features), F32),
    ]
    return call(body, outs, scalars, [table, Late(x), mine, came, dy], [*up, *down], held_like(up, down), us=1.0)


def middle_back(scalars, layer, table, hidden, parts, dy, attended, weights):
    rows, features = hidden[0].shape
    width = attended[0].shape[1]

    def body(scal, tab, *refs):
        given, (own, got, other) = refs[: 5 * CHUNKS], refs[5 * CHUNKS : 5 * CHUNKS + 3]
        outs = refs[5 * CHUNKS + 3 : 9 * CHUNKS + 4]
        stats, held, sem = refs[9 * CHUNKS + 4 :]
        fetch_start(scal, layer, own, got, other, held, sem)
        sums = outs[-1]
        sums[...] = jnp.zeros_like(sums)
        stats[...] = jnp.zeros_like(stats)
        lows = []
        for c in range(CHUNKS):
            hid, mine, came, dy_ref, att = given[5 * c : 5 * c + 5]
            dh_ref, low_ref, da_ref, delta = outs[4 * c : 4 * c + 4]
            grad = mine[...].astype(F32) + came[...].astype(F32)
            back, d_gain, d_bias = norm_grad(hid[...], tab[GAIN1 : GAIN1 + 1], grad)
            up = dy_ref[...].astype(F32)
            dh = up + back
            dh_ref[...] = dh
            low = dh.astype(BF)
            low_ref[...] = low
            flush(dh_ref, low_ref)
            added = (d_gain, d_bias, jnp.sum(dh, axis=0, keepdims=True), jnp.sum(up, axis=0, keepdims=True))
            for k, value in enumerate(added):
                sums[k : k + 1, :] += value
            lows.append(low)
        fetch_wait(own, held, sem)
        for c in range(CHUNKS):
            att = given[5 * c + 4]
            da_ref, delta = outs[4 * c + 2 : 4 * c + 4]
            da = dot_nt(lows[c], held[...]).astype(BF)
            da_ref[...] = da
            for p in range(width // 128):
                span = slice(p * 128, (p + 1) * 128)
                product = da[:, span].astype(F32) * att[:, span].astype(F32)
                first = low_lanes(product.shape)
                stats[:, 2 * p : 2 * p + 1] = jnp.sum(jnp.where(first, product, 0.0), axis=1, keepdims=True)
                stats[:, 2 * p + 1 : 2 * p + 2] = jnp.sum(jnp.where(first, 0.0, product), axis=1, keepdims=True)
            delta[...] = jnp.transpose(stats[...])[0:8, :]

    one = [((rows, features), F32, LATER), ((rows, features), BF, LATER), ((rows, width), BF), ((8, rows), F32)]
    scratch = [pltpu.VMEM((rows, 128), F32)] + held_like(weights)
    blocks = [table]
    for c in range(CHUNKS):
        blocks += [Late(hidden[c]), *parts[c], dy[c], Late(attended[c])]
    r = call(body, one * CHUNKS + [((8, features), F32)], scalars, blocks, weights, scratch, us=2.8)
    return [list(r[k : 4 * CHUNKS : 4]) for k in range(4)] + [r[-1]]


def project_back(scalars, layer, c, dq, dkv, near, far, returned, weights):
    rows, width = dq.shape
    features = weights[0].shape[0]

    def body(scal, dq_ref, dkv_ref, near_ref, far_ref, *rest):
        back_ref = rest[0] if returned is not None else None
        outs = rest[-6:-2] if returned is None else rest[-5:-2]
        own, *parts = rest[-11:-6] if returned is None else rest[-10:-5]
        held, sem = rest[-2:]
        fetch_parts(scal, layer, own, parts[:2], parts[2:], held, sem)
        at = slice(c * rows, (c + 1) * rows)
        total = dkv_ref[...] + near_ref[at, :].astype(F32) + far_ref[at, :].astype(F32)
        if returned is None:
            outs[3][...] = total
        else:
            rolled = pltpu.roll(back_ref[...], 2 * width - width // 2, 1)
            lane = lax.broadcasted_iota(jnp.int32, total.shape, 1)
            total = total + jnp.where((lane >= width) & (lane < width + width // 2), rolled, 0.0)
        low = total.astype(BF)
        outs[0][...] = low
        sums = outs[2]
        sums[...] = jnp.zeros_like(sums)
        sums[0:1, :width] = jnp.sum(dq_ref[...].astype(F32), axis=0, keepdims=True)
        sums[1:2, :] = jnp.sum(low.astype(F32), axis=0, keepdims=True)
        fetch_wait(own, held, sem)
        outs[1][...] = (dot_nt(dq_ref[...], held[:, :width]) + dot_nt(low, held[:, width:])).astype(BF)

    outs = [((rows, 2 * width), BF), ((rows, features), BF), ((8, features), F32)]
    blocks = [dq, dkv, near, far]
    if returned is None:
        outs.append(((rows, 2 * width), F32, LATER))
    else:
        blocks.append(Late(returned))
    return call(body, outs, scalars, blocks, weights, held_like(weights), us=2.7)


def last_back(scalars, table, x, parts, dh):
    rows, features = x[0].shape

    def body(scal, tab, *refs):
        given, outs = refs[: 4 * CHUNKS], refs[4 * CHUNKS :]
        sums = outs[-1]
        sums[...] = jnp.zeros_like(sums)
        for c in range(CHUNKS):
            x_ref, mine, came, dh_ref = given[4 * c : 4 * c + 4]
            dx_ref, low_ref = outs[2 * c : 2 * c + 2]
            grad = mine[...].astype(F32) + came[...].astype(F32)
            back, d_gain, d_bias = norm_grad(x_ref[...].astype(F32), tab[GAIN0 : GAIN0 + 1], grad)
            dx = dh_ref[...] + back
            dx_ref[...] = dx
            flush(dx_ref)
            low_ref[...] = dx.astype(BF)
            sums[0:1, :] += d_gain
            sums[1:2, :] += d_bias

    outs = [((rows, features), F32, LATER), ((rows, features), BF)] * CHUNKS + [((8, features), F32)]
    blocks = [table]
    for c in range(CHUNKS):
        blocks += [Late(x[c]), *parts[c], Late(dh[c])]
    r = call(body, outs, scalars, blocks, us=0.5)
    return list(r[0 : 2 * CHUNKS : 2]), list(r[1 : 2 * CHUNKS : 2]), r[-1]


def both_chunks(left, left_span, right, right_span):
    total = None
    for a, b in zip(left, right):
        d = dot_tn(a[:, left_span], b[:, right_span])
        total = d if total is None else total + d
    return total


def hand_out(scal, packed, send, mine, sem):
    copies = [
        pltpu.make_async_copy(packed.at[pl.ds(2 * (1 - scal[3]), 2)], send, sem.at[0]),
        pltpu.make_async_copy(packed.at[pl.ds(2 * scal[3], 2)], mine, sem.at[1]),
    ]
    for copy in copies:
        copy.start()
    for copy in copies:
        copy.wait()


def wide_grads(scalars, active, dy, mlp_in, d_up):
    features = dy[0].shape[1]
    inner = active[0].shape[1]
    a, half = inner // 4, features // 2
    size = a + half

    def body(scal, a0, a1, y0, y1, m0, m1, u0, u1, send, mine, packed, sem):
        for k in range(4):
            span = slice(k * a, (k + 1) * a)
            packed[k, :a, :] = both_chunks((a0, a1), span, (y0, y1), slice(None)).astype(BF)
            for i in range(2):
                part = both_chunks((m0, m1), slice(i * half, (i + 1) * half), (u0, u1), span)
                packed[k, a:, i * a : (i + 1) * a] = part.astype(BF)
        hand_out(scal, packed, send, mine, sem)

    blocks = [*map(Late, active), *dy, *map(Late, mlp_in), *d_up]
    outs = [((2, size, features), BF, RAW)] * 2
    scratch = [pltpu.VMEM((4, size, features), BF), pltpu.SemaphoreType.DMA((2,))]
    return call(body, outs, scalars, blocks, (), scratch, us=3.7)


def narrow_grads(scalars, normed, dq, dkv, attended, dh_low):
    features = normed[0].shape[1]
    width = dq[0].shape[1]
    rows = features // 4
    half, c = rows // 2, width // 4
    size = rows + half + c

    def body(scal, n0, n1, q0, q1, k0, k1, t0, t1, h0, h1, send, mine, packed, sem):
        every = slice(None)
        for x in range(2):
            span = slice(2 * x * rows, 2 * (x + 1) * rows)
            first = both_chunks((n0, n1), span, (q0, q1), every).astype(BF)
            second = both_chunks((n0, n1), span, (k0, k1), every).astype(BF)
            for core in range(2):
                k, at = 2 * core + x, core * rows
                packed[k, :rows, :width] = first[at : at + rows, :]
                packed[k, :rows, width:] = second[at : at + rows, :width]
                packed[k, rows : rows + half, :width] = second[at : at + half, width:]
                packed[k, rows : rows + half, width:] = second[at + half : at + rows, width:]
        out = both_chunks((t0, t1), every, (h0, h1), every).astype(BF)
        for k in range(4):
            packed[k, rows + half :, :] = out[k * c : (k + 1) * c, :]
        hand_out(scal, packed, send, mine, sem)

    blocks = [*map(Late, normed), *dq, *dkv, *map(Late, attended), *map(Late, dh_low)]
    outs = [((2, size, features), BF, RAW)] * 2
    scratch = [pltpu.VMEM((4, size, features), BF), pltpu.SemaphoreType.DMA((2,))]
    return call(body, outs, scalars, blocks, (), scratch, us=2.1)


def collect(scal, parts, held, sem):
    copies = []
    for i, refs in enumerate(parts):
        core = scal[3] if i < 2 else 1 - scal[3]
        section = scal[2] if i % 2 == 0 else 1 - scal[2]
        size = held.shape[1] // len(refs)
        for j, ref in enumerate(refs):
            place = held.at[2 * core + section, j * size : (j + 1) * size]
            copies.append(pltpu.make_async_copy(ref, place, sem.at[len(copies)]))
    for copy in copies:
        copy.start()
    for copy in copies:
        copy.wait()


def wide_unpack(scalars, mine, mine2, other, other2, inner):
    size, features = mine.shape
    a, half = inner // 4, features // 2

    def body(scal, p0, p1a, p1b, p2, p3a, p3b, down, up, token, held, sem):
        collect(scal, ((p0,), (p1a, p1b), (p2,), (p3a, p3b)), held, sem)
        for k in range(4):
            down[k * a : (k + 1) * a, :] = held[k, :a, :].astype(F32)
            for i in range(2):
                up[i * half : (i + 1) * half, k * a : (k + 1) * a] = held[k, a:, i * a : (i + 1) * a].astype(F32)
        token[...] = jnp.zeros_like(token)

    outs = [((inner, features), F32), ((features, inner), F32), ((8, 128), F32)]
    scratch = [pltpu.VMEM((4, size, features), BF), pltpu.SemaphoreType.DMA((6,))]
    return call(body, outs, scalars, [], [mine, *other, mine2, *other2], scratch, us=5)


def narrow_unpack(scalars, parts, extras, width, token):
    size, features = parts[0].shape
    rows = features // 4
    half, c, own = rows // 2, width // 4, width // 2

    def body(scal, _, p0, p1, p2, p3, e0, e1, pairs, value, extra, out, held, pair, sem, pair_sem):
        last = [pltpu.make_async_copy(e, pair.at[i if i == 0 else 1], pair_sem.at[i]) for i, e in enumerate((e0, e1))]
        for copy in last:
            copy.start()
        collect(scal, ((p0,), (p1,), (p2,), (p3,)), held, sem)
        for copy in last:
            copy.wait()
        for x in range(2):
            for core in range(2):
                k, at = 2 * core + x, (2 * x + core) * rows
                pairs[at : at + rows, 0, :] = held[k, :rows, :width].astype(F32)
                pairs[at : at + rows, 1, :] = held[k, :rows, width:].astype(F32)
                value[at : at + half, :] = held[k, rows : rows + half, :own].astype(F32)
                value[at + half : at + rows, :] = held[k, rows : rows + half, width : width + own].astype(F32)
        for k in range(4):
            out[k * c : (k + 1) * c, :] = held[k, rows + half :, :].astype(F32)
        for i in range(2):
            core = scal[3] if i == 0 else 1 - scal[3]
            at = pl.multiple_of(core * rows, rows)
            cut = pair[i].astype(F32)
            left = pltpu.roll(cut[:, :width], own, 1)
            right = pltpu.roll(cut[:, width:], own, 1)
            extra[pl.ds(at, half), :] = left[:, :own]
            extra[pl.ds(pl.multiple_of(at + half, 8), half), :] = right[:, :own]

    outs = [((features, 2, width), F32)] + [((features, own), F32), ((2 * rows, own), F32), ((width, features), F32)]
    scratch = [
        pltpu.VMEM((4, size, features), BF), pltpu.VMEM((2, half, features), BF),
        pltpu.SemaphoreType.DMA((4,)), pltpu.SemaphoreType.DMA((2,)),
    ]
    return call(body, outs, scalars, [token], list(parts) + list(extras), scratch, us=3)


def swap(value, axis, bits=1):
    count = lax.axis_size(axis)
    return lax.ppermute(value, axis, [(i, i ^ bits) for i in range(count)])


def shift(value, steps):
    count = lax.axis_size("batch")
    first, last = max(0, -steps), min(count, count - steps)
    return lax.ppermute(value, "batch", [(i, i + steps) for i in range(first, last)])


def after(value, *earlier):
    return lax.optimization_barrier((value,) + earlier)[0]


def take(array, index, axis=0):
    return lax.dynamic_index_in_dim(array, index, axis, keepdims=False)


def paired(mine, other, side):
    return jnp.where(side == 0, mine, other), jnp.where(side == 0, other, mine)


class Reduction:
    def __init__(self, grads, pieces):
        self.section = lax.axis_index("section")
        self.send, self.mine = grads
        self.pieces = pieces

    def over_cores(self):
        self.near = swap(self.send, "batch")

    def pair_sum(self, section, start, size):
        cut = [lax.dynamic_slice(a, (section, start, 0), (1, size, a.shape[2]))[0] for a in (self.mine, self.near)]
        return cut[0].astype(F32) + cut[1].astype(F32)

    def prepare(self):
        size = self.mine.shape[1] // self.pieces
        self.sent = [self.pair_sum(1 - self.section, i * size, size).astype(BF) for i in range(self.pieces)]

    def over_sections(self, i=0):
        if i == 0:
            self.came = []
        self.came.append(swap(self.sent[i], "section"))

    def scatter_send(self):
        index = lax.axis_index("batch")
        half = self.mine.shape[1] // 2
        came = self.came if self.pieces == 2 else [self.came[0][:half], self.came[0][half:]]
        cut = [(self.pair_sum(self.section, i * half, half) + came[i].astype(F32)).astype(BF) for i in range(2)]
        *first, near, far = chip_bits()
        for bit in first:
            keep, send = paired(*cut, (index >> bit) & 1)
            total = (keep.astype(F32) + swap(send, "batch", 1 << bit).astype(F32)).astype(BF)
            cut = jnp.split(total, 2, axis=0)
        self.keep, send = paired(*cut, (index >> near) & 1)
        return send

    def exchange_send(self, got):
        self.part = (self.keep.astype(F32) + got.astype(F32)).astype(BF)
        return self.part

    def gather_send(self, got):
        self.part = (self.part.astype(F32) + got.astype(F32)).astype(BF)
        return self.part

    def finish(self, got):
        index = lax.axis_index("batch")
        *first, near, far = chip_bits()
        part = jnp.concatenate(paired(self.part, got, (index >> near) & 1), axis=0)
        for bit in reversed(first):
            part = jnp.concatenate(paired(part, swap(part, "batch", 1 << bit), (index >> bit) & 1), axis=0)
        self.quarter = part


def chip_bits():
    return list(range(1, lax.axis_size("batch").bit_length() - 1))


def swap_all(values, place):
    sizes = [v.shape[0] for v in values]
    got = swap(jnp.concatenate(values, axis=0) if len(values) > 1 else values[0], "batch", 1 << chip_bits()[place])
    ends = [sum(sizes[: i + 1]) for i in range(len(sizes))]
    return [got[end - size : end] for size, end in zip(sizes, ends)]


def tie(value, *others):
    return lax.optimization_barrier((value,) + others)


def forward_layer(scalars, layer, table, w, x=None, ahead=None, carried=None, hooks=None):
    hooks = hooks or {}
    nothing = lambda value: value
    x, normed, q, kv = project(scalars, layer, w["qkv"], table, x=x, ahead=ahead, carried=carried)
    if "projected" in hooks:
        kv = hooks["projected"](kv, q)
    far = shift(kv, 2)
    near = swap(kv, "batch")
    out, amount, tops = attend_local(scalars, q, kv, near)
    far = hooks.get("arrived", nothing)(after(far, out))
    far = [far, swap(far, "batch")]
    att, lse, parts, came = [], [], [], []
    for c in range(CHUNKS):
        a, l, part = attend_far(scalars, layer, c, q[c], far, out, amount, tops, w["out"])
        att.append(a)
        lse.append(l)
        parts.append(part)
        came.append(swap(part, "tensor"))
    came = hooks.get("far", nothing)(came)
    hidden, mlp_in, active, slope, results = [], [], [], [], []
    for c in range(CHUNKS if layer == 0 else 0):
        h, m, a, s, part = feed_forward(scalars, layer, table, x[c], parts[c], came[c], w["up"], w["down"])
        hidden.append(h)
        mlp_in.append(m)
        active.append(a)
        slope.append(s)
        results.append((table, h, part))
    kept = dict(x=x, normed=normed, q=q, kv=kv, near=near, far=far, att=att, lse=lse, hidden=hidden,
                mlp_in=mlp_in, active=active, slope=slope, attention=(parts, came), results=results)
    return results, kept


def backward_layer(scalars, layer, table, w, kept, dy, returned, steps):
    rows = CHUNKS * dy[0].shape[0]
    dy = list(steps("start", dy))
    d_up, parts, up_sums = [], [], []
    for c in range(CHUNKS):
        if c == 1:
            dy[1] = steps("half", after(dy[1], parts[0][0]))
        if layer == 0:
            grad, part, sums = feed_back(scalars, layer, dy[c], kept["slope"][c], w["up"], w["down"])
        else:
            mine, came = [a[c] for a in kept["attention"]]
            h, m, a, y, grad, part, sums = feed_both(scalars, layer, table, kept["x"][c], mine, came, dy[c], w["up"], w["down"])
            kept["hidden"].append(h)
            kept["mlp_in"].append(m)
            kept["active"].append(a)
            kept["results"].append((table, h, y))
        d_up.append(grad)
        up_sums.append(sums)
        parts.append((part, swap(part, "tensor")))
    wide = Reduction(wide_grads(scalars, kept["active"], dy, kept["mlp_in"], d_up), 1)
    parts = steps("fed", parts, wide)
    dh, dh_low, d_att, delta, mid = middle_back(
        scalars, layer, table, kept["hidden"], parts, dy, kept["att"], w["out"]
    )
    d_att = steps("mid", d_att, wide)
    dq, mine, others = attend_far_back(scalars, kept["q"], d_att, kept["lse"], delta, kept["far"])
    total = (mine.astype(F32) + swap(others, "batch").astype(F32)).astype(BF)
    dq = steps("turn", after(dq, total), wide)
    home = shift(total, -2)
    dq, crossing = attend_near_back(scalars, kept["q"], d_att, kept["lse"], delta, kept["near"], dq)
    near = swap(crossing, "batch")
    dq = steps("between", dq, wide)
    dq0, dq1, dk0, dk1 = attend_own_back(scalars, kept["q"], d_att, kept["lse"], delta, kept["kv"], dq)
    dq, dkv = [dq0, dq1], [dk0, dk1]
    home, dq = steps("near", (home, dq), wide)
    dkv_low, parts, in_sums, back = [], [], [], []
    for c in range(CHUNKS):
        again = None if returned is None else returned[c]
        r = project_back(scalars, layer, c, dq[c], dkv[c], near, home, again, w["qkv"])
        dkv_low.append(r[0])
        parts.append((r[1], swap(r[1], "tensor")))
        in_sums.append(r[2])
        back.extend(r[3:])
    narrow = Reduction(narrow_grads(scalars, kept["normed"], dq, dkv_low, kept["att"], dh_low), 1)
    parts = steps("proj", parts, wide, narrow)
    parts = steps("last", parts, wide, narrow)
    dx, dx_low, last = last_back(scalars, table, kept["x"], parts, dh)
    up, inn = [a + b for a, b in (up_sums, in_sums)]
    blank = jnp.zeros((TABLE - BUP - 2, up.shape[1]), F32)
    small = jnp.concatenate(
        [last[0:1], mid[0:1], last[1:2], mid[1:2], mid[2:4], inn[0:2], up[0:2], blank], axis=0
    )
    return dx, dx_low, back, wide, narrow, small


def local(
    tokens, block_place, cotangent, norm_gains, norm_biases, query_key, query_bias, value_own, value_bias,
    value_extra, out_weight, out_bias, up_weight, up_bias, down_weight, down_bias,
):
    section = lax.axis_index("section")
    tensor = lax.axis_index("tensor")
    core = lax.axis_index("batch") % 2
    micros, _, half_rows, features = tokens.shape
    width = query_bias.shape[1]
    own_width = value_own.shape[2]
    inner = up_weight.shape[2]
    assert micros == 2 and lax.axis_size("section") == 2 and lax.axis_size("tensor") == 2
    assert 2 * own_width == width and 2 * width == features and inner == 2 * features

    place = take(block_place, section)[0]
    scalars = jnp.stack([place & 1, place >> 1, section, core]).astype(jnp.int32)

    my_tokens = take(tokens, section)[0]
    x = paired(my_tokens, swap(my_tokens, "tensor"), tensor)

    def row(*pieces):
        flat = jnp.concatenate([p.reshape(-1) for p in pieces])
        return jnp.pad(flat, (0, features - flat.shape[0]))[None]

    blank = jnp.zeros((width,), F32)
    own_table = jnp.concatenate(
        [norm_gains[0], norm_biases[0], out_bias, down_bias, row(query_bias[0]), row(blank, value_bias[0]),
         up_bias[0].reshape(2, features), jnp.zeros((TABLE - BUP - 2, features), F32)], axis=0
    )
    def half_of(weight):
        return take(weight.reshape((2, weight.shape[0] // 2) + weight.shape[1:]), core)

    query_keys = query_key[0].reshape(features, 2 * width)
    extra = jnp.where(section == 0, value_extra, jnp.zeros_like(value_extra))
    halves = [half_of(query_keys), jnp.concatenate([half_of(value_own[0]), half_of(extra)], axis=1)]
    qkv = jnp.concatenate([query_keys, value_own[0], extra], axis=1)
    qkv_got = [swap(h, "section") for h in halves]
    other_table = swap(own_table, "section")
    out_got = swap(half_of(out_weight[0]), "section")
    up_got = swap(after(half_of(up_weight[0]), x[0]), "section")
    down_got = swap(after(half_of(down_weight[0]), x[0]), "section")
    tables = paired(own_table, other_table, section)
    qkv_got[0], qkv_got[1], out_got, qkv, scalars, *rest = tie(*qkv_got, out_got, qkv, scalars, *tables, *x)
    tables, x = rest[:2], rest[2:]
    w = dict(qkv=(qkv, *qkv_got, *[swap(g, "batch") for g in qkv_got]))
    late = dict(up=up_got, down=down_got)

    def on_projected(kv, q):
        mine, kv = tie(take(cotangent, section)[0], kv)
        late["dy"] = mine, swap(mine, "tensor")
        w["out"] = (out_weight[0], out_got, swap(after(out_got, kv), "batch"))
        return kv

    def on_arrived(far):
        mine, other = late["dy"]
        far, got, other = tie(far, late["up"], other)
        late["dy"] = paired(mine, other, tensor)
        w["up"] = (up_weight[0], got, swap(got, "batch"))
        return far

    def on_far(came):
        *came, got = tie(*came, late["down"])
        w["down"] = (down_weight[0], got, swap(got, "batch"))
        return came

    first, kept0 = forward_layer(
        scalars, 0, tables[0], w, x=x, hooks=dict(projected=on_projected, arrived=on_arrived, far=on_far)
    )
    first = [r + (swap(r[2], "tensor"),) for r in first]
    _, kept1 = forward_layer(scalars, 1, tables[1], w, ahead=first, carried=kept0["kv"])
    y0 = kept1["x"]

    def my_half(chunks):
        return jnp.where(tensor == 0, chunks[0], chunks[1])

    def by_section(mine0, mine1, kind):
        mine = jnp.where(section == 0, mine0, mine1)
        other = swap(jnp.where(section == 0, mine1, mine0).astype(kind), "section")
        return mine, other

    def steps1(number, values, wide=None, narrow=None):
        leaves, tree = jax.tree.flatten(values)
        if number == "fed":
            *leaves, wide.send = tie(*leaves, wide.send)
            wide.over_cores()
        if number == "mid":
            *leaves, wide.near = tie(*leaves, wide.near)
            wide.prepare()
            *leaves, wide.sent[0] = tie(*leaves, *wide.sent)
            wide.over_sections(0)
        if number == "near":
            *leaves, wide.came[0] = tie(*leaves, wide.came[0])
            late["a1"] = swap_all([wide.scatter_send()], -2)[0]
        if number == "proj":
            *leaves, narrow.send, got = tie(*leaves, narrow.send, late["a1"])
            narrow.over_cores()
            sent = wide.exchange_send(got)
            *leaves, sent = tie(*leaves, sent)
            late["b1"] = swap_all([sent], -1)[0]
        if number == "last":
            *leaves, narrow.near = tie(*leaves, narrow.near)
            narrow.prepare()
            *leaves, narrow.sent[0] = tie(*leaves, narrow.sent[0])
            narrow.over_sections()
        return jax.tree.unflatten(tree, leaves)

    dx1, dx1_low, back, wide1, narrow1, small1 = backward_layer(scalars, 1, tables[1], w, kept1, late["dy"], None, steps1)

    def steps0(number, values, wide=None, narrow=None):
        leaves, tree = jax.tree.flatten(values)
        if number == "half":
            *leaves, narrow1.came[0], got = tie(*leaves, narrow1.came[0], late["b1"])
            sent = [wide1.gather_send(got), narrow1.scatter_send()]
            *leaves, sent[0], sent[1] = tie(*leaves, *sent)
            late["c1"] = swap_all(sent, -2)
        if number == "fed":
            *leaves, wide.send, got, narrow_got = tie(*leaves, wide.send, *late["c1"])
            wide.over_cores()
            wide1.finish(got)
            sent = narrow1.exchange_send(narrow_got)
            *leaves, sent = tie(*leaves, sent)
            late["d1"] = swap_all([sent], -1)[0]
        if number == "mid":
            *leaves, wide.near, got = tie(*leaves, wide.near, late["d1"])
            wide.prepare()
            *leaves, wide.sent[0] = tie(*leaves, *wide.sent)
            wide.over_sections(0)
            late["e1"] = narrow1.gather_send(got)
        if number == "near":
            *leaves, wide.came[0] = tie(*leaves, wide.came[0])
            late["a0"] = swap_all([wide.scatter_send(), late["e1"]], -2)
        if number == "proj":
            *leaves, narrow.send, got, narrow_got = tie(*leaves, narrow.send, *late["a0"])
            narrow1.finish(narrow_got)
            narrow.over_cores()
            sent = wide.exchange_send(got)
            *leaves, sent = tie(*leaves, sent)
            late["b0"] = swap_all([sent], -1)[0]
            *leaves, narrow.near = tie(*leaves, narrow.near)
            narrow.prepare()
            *leaves, narrow.sent[0] = tie(*leaves, narrow.sent[0])
            narrow.over_sections()
            late["y1"] = [swap(after(r[2], leaves[0]), "tensor") for r in kept1["results"]]
        if number == "last":
            *leaves, narrow.came[0] = tie(*leaves, narrow.came[0])
        return jax.tree.unflatten(tree, leaves)

    dx0, dx0_low, _, wide0, narrow0, small0 = backward_layer(scalars, 0, tables[0], w, kept0, dx1_low, back, steps0)
    sums = jnp.stack([small0, small1])
    sums = sums + swap(sums, "batch")
    got, sums, *rest = tie(late["b0"], sums, *late["y1"], my_half(dx0), my_half(dx1))
    y_came, grads = rest[:2], rest[2:]
    sent = [narrow0.scatter_send(), wide0.gather_send(got)]
    sent[0], sent[1], sums, grads[0], grads[1] = tie(*sent, sums, *grads)
    late["c0"] = swap_all(sent, -2)
    table = take(sums, section) + swap(take(sums, 1 - section), "section")
    mine_grads, other_grads = by_section(*grads, BF)
    y1 = my_half(
        [(r[1] + r[0][BDOWN : BDOWN + 1] + r[2].astype(F32) + c.astype(F32)).astype(BF) for r, c in zip(kept1["results"], y_came)]
    )
    mine_out, other_out = by_section(my_half(y0), y1, BF)

    narrow0_got, wide0_got, table, other_grads, other_out = tie(
        *late["c0"], table, other_grads, other_out
    )
    sent = narrow0.exchange_send(narrow0_got)
    wide0.finish(wide0_got)
    wide_mine = jnp.where(section == 0, wide0.quarter, wide1.quarter)
    wide_sent = jnp.split(jnp.where(section == 0, wide1.quarter, wide0.quarter), 2, axis=0)
    sent, wide_sent[0] = tie(sent, wide_sent[0])
    got = swap_all([sent], -1)[0]
    wide_other = [swap(wide_sent[0], "section")]
    for bit in chip_bits()[:-1]:
        table = table + swap(table, "batch", 1 << bit)

    got, table, wide_other[0], wide_sent[1] = tie(got, table, wide_other[0], wide_sent[1])
    sent = narrow0.gather_send(got)
    got = swap_all([sent], -2)[0]
    wide_mine2, wide_other2 = swap(wide_mine, "batch"), swap(wide_other[0], "batch")
    table = table + swap(table, "batch", 1 << chip_bits()[-1])
    wide_other.append(swap(wide_sent[1], "section"))

    got, wide_other[1], table = tie(got, wide_other[1], table)
    narrow0.finish(got)
    outputs = jnp.stack(paired(mine_out, other_out, section))
    input_grads = jnp.stack(paired(mine_grads.astype(F32), other_grads.astype(F32), section))

    def gathered(first, second):
        mine = jnp.where(section == 0, first, second)
        other = swap(jnp.where(section == 0, second, first), "section")
        mine2 = swap(mine, "batch")
        other, mine2 = tie(other, mine2, token)[:2]
        return mine, other, mine2, swap(other, "batch")

    d_down, d_up, token = wide_unpack(
        scalars, wide_mine, wide_mine2, wide_other, [wide_other2, swap(wide_other[1], "batch")], inner
    )
    rows = features // 4
    extra = narrow0.quarter[rows : rows + rows // 2]
    extras = (extra, swap(extra, "batch"))
    token, *extras = tie(token, *extras)
    d_qk, d_v, d_extra, d_out = narrow_unpack(
        scalars, gathered(narrow0.quarter, narrow1.quarter), extras, width, token
    )
    return (
        outputs.reshape(1, micros, 1, half_rows, features),
        input_grads.reshape(1, micros, 1, half_rows, features),
        table[GAIN0 : GAIN1 + 1][None],
        table[BIAS0 : BIAS1 + 1][None],
        d_qk.reshape(1, features, 2, width),
        table[BQ : BQ + 1, :width],
        d_v[None],
        table[BKV : BKV + 1, width : width + own_width],
        d_extra,
        d_out[None],
        table[BO : BO + 1],
        d_up[None],
        table[BUP : BUP + 2].reshape(1, inner),
        d_down[None],
        table[BDOWN : BDOWN + 1],
    )


def solution(mesh):
    return jax.shard_map(
        local,
        mesh=mesh,
        in_specs=(
            P(None, "batch", "tensor", None),
            P(None, "batch"),
            P(None, "batch", "tensor", None),
            P("section", None, None),
            P("section", None, None),
            P("section", None, None, "tensor"),
            P("section", "tensor"),
            P("section", None, "tensor"),
            P("section", "tensor"),
            P(None, "tensor"),
            P("section", "tensor", None),
            P("section", None),
            P("section", None, "tensor"),
            P("section", "tensor"),
            P("section", "tensor", None),
            P("section", None),
        ),
        out_specs=(
            P("section", None, "batch", "tensor", None),
            P("section", None, "batch", "tensor", None),
            P("section", None, None),
            P("section", None, None),
            P("section", None, None, "tensor"),
            P("section", "tensor"),
            P("section", None, "tensor"),
            P("section", "tensor"),
            P("section", "tensor"),
            P("section", "tensor", None),
            P("section", None),
            P("section", None, "tensor"),
            P("section", "tensor"),
            P("section", "tensor", None),
            P("section", None),
        ),
        check_vma=False,
    )
```

```python
import jax
import jax.numpy as jnp
from jax import lax
from jax.experimental import pallas as pl
from jax.experimental.pallas import tpu as pltpu
from jax.sharding import PartitionSpec as P

F32 = jnp.float32
BF = jnp.bfloat16
LOW = -1e30
HEAD = 64
CHUNKS = 2

GAIN0, GAIN1, BIAS0, BIAS1, BO, BDOWN, BQ, BKV, BUP = range(9)
TABLE = 16

WHOLE = pl.BlockSpec(memory_space=pltpu.VMEM)
SCALARS = pl.BlockSpec(memory_space=pltpu.SMEM)
FAR_OFF = pl.BlockSpec(memory_space=pltpu.HBM)


def dot_nn(a, b):
    return lax.dot_general(a, b, (((1,), (0,)), ((), ())), preferred_element_type=F32)


def dot_nt(a, b):
    return lax.dot_general(a, b, (((1,), (1,)), ((), ())), preferred_element_type=F32)


def dot_tn(a, b):
    return lax.dot_general(a, b, (((0,), (0,)), ((), ())), preferred_element_type=F32)


class Late:
    def __init__(self, array):
        self.array = array


def in_hbm(array):
    return pltpu.with_memory_space_constraint(array, pltpu.HBM)


FLUSH = []


def flush(*refs):
    for ref in refs:
        for k, (held, copy, started) in enumerate(FLUSH[-1]):
            if held is ref and not started:
                copy.start()
                FLUSH[-1][k] = (held, copy, True)


LATER, RAW = 1, 2


def call(inner_body, outs, scalars, blocks, remote=(), scratch=(), us=1.0, limit=48):
    shapes = [pltpu.HBM(o[0], o[1]) if len(o) > 2 else jax.ShapeDtypeStruct(o[0], o[1]) for o in outs]
    kinds = [o[2] if len(o) > 2 else 0 for o in outs]
    late = [i for i, b in enumerate(blocks) if isinstance(b, Late)]
    blocks = [in_hbm(b.array) if isinstance(b, Late) else b for b in blocks]
    remote = [in_hbm(r) for r in remote]
    n_in, n_out = 1 + len(blocks) + len(remote), len(outs)
    later = [i for i, kind in enumerate(kinds) if kind == LATER]
    spare = [pltpu.VMEM(blocks[i].shape, blocks[i].dtype) for i in late]
    spare += [pltpu.VMEM(shapes[i].shape, shapes[i].dtype) for i in later]
    sems = [pltpu.SemaphoreType.DMA((max(len(late), 1),)), pltpu.SemaphoreType.DMA((max(len(later), 1),))]

    def body(*refs):
        refs = list(refs)
        first = n_in + n_out
        n_spare = len(spare)
        held, (sem, out_sem), own = refs[first : first + n_spare], refs[first + n_spare : first + n_spare + 2], refs[first + n_spare + 2 :]
        copies = [pltpu.make_async_copy(refs[1 + i], v, sem.at[k]) for k, (i, v) in enumerate(zip(late, held))]
        back = [
            pltpu.make_async_copy(v, refs[n_in + i], out_sem.at[k])
            for k, (i, v) in enumerate(zip(later, held[len(late) :]))
        ]
        for copy in copies:
            copy.start()
        for copy in copies:
            copy.wait()
        for i, v in zip(late, held):
            refs[1 + i] = v
        for i, v in zip(later, held[len(late) :]):
            refs[n_in + i] = v
        FLUSH.append([(held[len(late) + k], copy, False) for k, copy in enumerate(back)])
        inner_body(*refs[:first], *own)
        flush(*held[len(late) :])
        FLUSH.pop()
        for copy in back:
            copy.wait()

    return pl.pallas_call(
        body,
        out_shape=shapes,
        in_specs=[SCALARS] + [FAR_OFF if i in late else WHOLE for i in range(len(blocks))] + [FAR_OFF] * len(remote),
        out_specs=[FAR_OFF if kind else WHOLE for kind in kinds],
        scratch_shapes=spare + sems + list(scratch),
        compiler_params=pltpu.CompilerParams(vmem_limit_bytes=limit * 1024 * 1024),
        cost_estimate=pl.CostEstimate(flops=int(us * 1.2e8), bytes_accessed=int(us * 2e5), transcendentals=0),
    )(scalars, *blocks, *remote)


def fetch_start(scalars, layer, own, got, other, held, sem):
    half = held.shape[0] // 2

    @pl.when(scalars[2] == layer)
    def _():
        pltpu.make_async_copy(own, held, sem).start()

    @pl.when(scalars[2] != layer)
    def _():
        mine = pl.multiple_of(scalars[3] * half, half)
        rest = pl.multiple_of((1 - scalars[3]) * half, half)
        pltpu.make_async_copy(got, held.at[pl.ds(mine, half)], sem).start()
        pltpu.make_async_copy(other, held.at[pl.ds(rest, half)], sem).start()


def fetch_parts(scalars, layer, own, got, other, held, sem):
    half = held.shape[0] // 2

    @pl.when(scalars[2] == layer)
    def _():
        pltpu.make_async_copy(own, held, sem).start()

    @pl.when(scalars[2] != layer)
    def _():
        for side, refs in ((scalars[3], got), (1 - scalars[3], other)):
            at = pl.ds(pl.multiple_of(side * half, half), half)
            start = 0
            for ref in refs:
                end = start + ref.shape[1]
                pltpu.make_async_copy(ref, held.at[at, start:end], sem).start()
                start = end


def fetch_wait(own, held, sem):
    pltpu.make_async_copy(own, held, sem).wait()


def held_like(*weights):
    return [pltpu.VMEM(w[0].shape, BF) for w in weights] + [pltpu.SemaphoreType.DMA] * len(weights)


def norm_parts(v):
    centred = v - jnp.mean(v, axis=-1, keepdims=True)
    rate = lax.rsqrt(jnp.mean(centred * centred, axis=-1, keepdims=True) + 1e-05)
    return centred * rate, rate


def norm_grad(v, gain, grad):
    unit, rate = norm_parts(v)
    scaled = grad * gain
    inner = jnp.mean(scaled * unit, axis=-1, keepdims=True)
    result = rate * (scaled - jnp.mean(scaled, axis=-1, keepdims=True) - unit * inner)
    return result, jnp.sum(grad * unit, axis=0, keepdims=True), jnp.sum(grad, axis=0, keepdims=True)


def gelu_both(u):
    factor = 0.7978845608028654
    square = u * u
    t = jnp.tanh(factor * u * (1.0 + 0.044715 * square))
    half = 0.5 * (1.0 + t)
    slope = half + (0.5 * factor) * u * (1.0 - t * t) * (1.0 + (3 * 0.044715) * square)
    return u * half, slope


def project(scalars, layer, weights, table, x=None, ahead=None, carried=None):
    if ahead is None:
        rows, features = x[0].shape
        blocks = [table, *x]
    else:
        rows, features = ahead[0][1].shape
        blocks = [table, ahead[0][0], Late(carried)]
        for chunk in ahead:
            blocks.extend([Late(chunk[1]), *chunk[2:]])
    width = weights[0].shape[1] // 3

    def body(scal, tab, *refs):
        given = refs[: len(blocks) - 1]
        own, *parts = refs[len(blocks) - 1 : len(blocks) + 4]
        outs = refs[len(blocks) + 4 : -2]
        held, sem = refs[-2:]
        fetch_parts(scal, layer, own, parts[:2], parts[2:], held, sem)
        for c in range(CHUNKS):
            at = slice(c * rows, (c + 1) * rows)
            if ahead is None:
                v = given[c][...].astype(F32)
            else:
                before, carry = given[:2]
                hid, mine, came = given[2 + 3 * c : 5 + 3 * c]
                y = hid[...] + before[BDOWN : BDOWN + 1] + mine[...].astype(F32) + came[...].astype(F32)
                low = y.astype(BF)
                outs[5 + c][...] = low
                v = low.astype(F32)
            unit, _ = norm_parts(v)
            normed = (unit * tab[GAIN0 : GAIN0 + 1] + tab[BIAS0 : BIAS0 + 1]).astype(BF)
            outs[c][...] = normed
            if c == 0:
                fetch_wait(own, held, sem)
            q = dot_nn(normed, held[:, :width]) + tab[BQ : BQ + 1, :width]
            outs[2 + c][...] = (q.astype(BF).astype(F32) * 0.125).astype(BF)
            kv = dot_nn(normed, held[:, width:]) + tab[BKV : BKV + 1]
            if ahead is not None:
                rolled = pltpu.roll(carry[at, :].astype(F32), width // 2, 1)
                lane = lax.broadcasted_iota(jnp.int32, kv.shape, 1)
                kv = jnp.where(lane >= width + width // 2, rolled, kv)
            outs[4][at, :] = kv.astype(BF)

    outs = [((rows, features), BF, LATER)] * 2 + [((rows, width), BF)] * 2 + [((2 * rows, 2 * width), BF)]
    if ahead is not None:
        outs += [((rows, features), BF, LATER)] * 2
    r = call(body, outs, scalars, blocks, weights, held_like(weights), us=2.5)
    return list(x) if ahead is None else r[5:], r[:2], r[2:4], r[4]


def low_lanes(shape):
    return lax.broadcasted_iota(jnp.int32, shape, 1) < HEAD


def head_of(pair, sub, fill):
    keep = low_lanes(pair.shape)
    return jnp.where(keep if sub == 0 else ~keep, pair, jnp.full_like(pair, fill))


def halves_of(ref, size):
    return tuple(ref.at[i * size : (i + 1) * size] for i in range(ref.shape[0] // size))


def spans(p, width):
    return slice(p * 128, (p + 1) * 128), slice(width + p * 128, width + (p + 1) * 128)


def scored(q, tiles, p, width, masks):
    ks, vs = spans(p, width)
    tops, outs = [], []
    for sub in range(2):
        scores = [dot_nt(q, head_of(t[:, ks], sub, 0)) for t in tiles]
        scores = [s if m is None else jnp.where(m, s, LOW) for s, m in zip(scores, masks)]
        top = scores[0].max(axis=1, keepdims=True)
        for s in scores[1:]:
            top = jnp.maximum(top, s.max(axis=1, keepdims=True))
        total = None
        for s, t in zip(scores, tiles):
            part = dot_nn(jnp.exp(s - top).astype(BF), head_of(t[:, vs], sub, 1))
            total = part if total is None else total + part
        tops.append(top)
        outs.append(total)
    low = low_lanes(outs[0].shape)
    value = jnp.where(low, outs[0], outs[1])
    amount = pltpu.roll(jnp.where(low, outs[1], outs[0]), HEAD, 1)
    return tops, value, amount


def attend_local(scalars, q, kv, near):
    size, width = q[0].shape
    rows = size * CHUNKS

    def body(scal, q0, q1, k_all, n_all, out, amount, tops):
        own = halves_of(k_all, size)
        row = lax.broadcasted_iota(jnp.int32, (size, size), 0)
        col = lax.broadcasted_iota(jnp.int32, (size, size), 1)
        causal = col <= row

        def run(extra):
            for c, q_ref in enumerate((q0, q1)):
                at = slice(c * size, (c + 1) * size)
                tiles = list(extra) + [own[i] for i in range(c + 1)]
                masks = [None] * (len(tiles) - 1) + [causal]
                for p in range(width // 128):
                    span = slice(p * 128, (p + 1) * 128)
                    top, value, total = scored(q_ref[:, span], tiles, p, width, masks)
                    out[at, span] = value
                    amount[at, span] = total
                    tops[at, 2 * p : 2 * p + 1] = top[0]
                    tops[at, 2 * p + 1 : 2 * p + 2] = top[1]

        @pl.when(scal[0] == 1)
        def _():
            run(halves_of(n_all, size))

        @pl.when(scal[0] == 0)
        def _():
            run(())

    outs = [((rows, width), F32), ((rows, width), F32), ((rows, 128), F32)]
    return call(body, outs, scalars, [*q, kv, near], us=5)


def attend_far(scalars, layer, c, q, far, out, amount, tops, weights):
    size, width = q.shape
    features = weights[0].shape[1]

    def body(scal, q_ref, fa, fb, out_ref, amount_ref, tops_ref, own, got, other, att, lse, part, stats, held, sem):
        fetch_start(scal, layer, own, got, other, held, sem)
        at = slice(c * size, (c + 1) * size)
        stats[...] = jnp.zeros_like(stats)

        def finish(p, value, total, top0, top1):
            span = slice(p * 128, (p + 1) * 128)
            att[:, span] = (value / total).astype(BF)
            logs = jnp.log(total)
            stats[:, 2 * p : 2 * p + 1] = top0 + logs[:, 0:1]
            stats[:, 2 * p + 1 : 2 * p + 2] = top1 + logs[:, HEAD : HEAD + 1]

        @pl.when(scal[1] == 0)
        def _():
            for p in range(width // 128):
                span = slice(p * 128, (p + 1) * 128)
                finish(p, out_ref[at, span], amount_ref[at, span], tops_ref[at, 2 * p : 2 * p + 1], tops_ref[at, 2 * p + 1 : 2 * p + 2])

        @pl.when(scal[1] == 1)
        def _():
            for p in range(width // 128):
                span = slice(p * 128, (p + 1) * 128)
                new, value, total = scored(q_ref[:, span], halves_of(fa, size) + halves_of(fb, size), p, width, [None] * 4)
                tops_all, olds, news = [], [], []
                for sub in range(2):
                    before = tops_ref[at, 2 * p + sub : 2 * p + sub + 1]
                    top = jnp.maximum(before, new[sub])
                    tops_all.append(top)
                    olds.append(jnp.exp(before - top))
                    news.append(jnp.exp(new[sub] - top))
                low = low_lanes(value.shape)
                keep = jnp.where(low, olds[0], olds[1])
                take = jnp.where(low, news[0], news[1])
                finish(p, out_ref[at, span] * keep + value * take, amount_ref[at, span] * keep + total * take, *tops_all)

        lse[...] = jnp.transpose(stats[...])[0:8, :]
        flush(att, lse)
        fetch_wait(own, held, sem)
        part[...] = dot_nn(att[...], held[...]).astype(BF)

    outs = [((size, width), BF, LATER), ((8, size), F32, LATER), ((size, features), BF)]
    scratch = [pltpu.VMEM((size, 128), F32)] + held_like(weights)
    return call(body, outs, scalars, [q, *far, out, amount, tops], weights, scratch, us=4.5)


def back_tile(p, width, q, do, lse, delta, kv, mask):
    ks, vs = spans(p, width)
    dq, dks, dvs = None, [], []
    for sub in range(2):
        h = 2 * p + sub
        key = head_of(kv[:, ks], sub, 0)
        scores = dot_nt(key, q)
        weight = jnp.exp(scores - lse[h : h + 1, :])
        if mask is not None:
            weight = jnp.where(mask, weight, 0.0)
        d_weight = dot_nt(head_of(kv[:, vs], sub, 0), do)
        d_score = (weight * (d_weight - delta[h : h + 1, :])).astype(BF)
        dvs.append(dot_nn(weight.astype(BF), do))
        dks.append(dot_nn(d_score, q))
        d = dot_tn(key, d_score)
        dq = d if dq is None else dq + d
    low = low_lanes(dks[0].shape)
    return dq, jnp.where(low, dks[0], dks[1]), jnp.where(low, dvs[0], dvs[1])


def staged(size, width):
    rows = size * CHUNKS
    return [pltpu.VMEM((rows, width), BF), pltpu.VMEM((rows, width), BF), pltpu.VMEM((8, rows), F32), pltpu.VMEM((8, rows), F32)]


def stage(size, given, held):
    for k, ref in enumerate(held):
        for c in range(CHUNKS):
            at = slice(c * size, (c + 1) * size)
            if k < 2:
                ref[at, :] = given[2 * k + c][...]
            else:
                ref[:, at] = given[2 * k + c][...]


def back_over(held, width, size, sources, dq_ref):
    q, do, lse, delta = held
    for p in range(width // 128):
        ks, vs = spans(p, width)
        total = None
        for source, ref, start in sources:
            for i in range(CHUNKS):
                at = slice(start + i * size, start + (i + 1) * size)
                tile = source.at[i * size : (i + 1) * size]
                dq, dk, dv = back_tile(p, width, q[:, ks], do[:, ks], lse, delta, tile, None)
                total = dq if total is None else total + dq
                ref[at, ks] = dk.astype(BF)
                ref[at, vs] = dv.astype(BF)
        dq_ref[:, ks] += jnp.transpose(total)


def attend_far_back(scalars, q, do, lse, delta, far):
    size, width = q[0].shape
    rows = size * CHUNKS

    def body(scal, q0, q1, o0, o1, l0, l1, d0, d1, fa, fb, dq_out, mine, others, *held):
        dq_out[...] = jnp.zeros_like(dq_out)

        @pl.when(scal[1] == 1)
        def _():
            stage(size, (q0, q1, o0, o1, l0, l1, d0, d1), held)
            back_over(held, width, size, [(fb, others, 0), (fa, mine, 0)], dq_out)

        @pl.when(scal[1] == 0)
        def _():
            mine[...] = jnp.zeros_like(mine)
            others[...] = jnp.zeros_like(others)

    outs = [((rows, width), F32), ((rows, 2 * width), BF), ((rows, 2 * width), BF)]
    blocks = [*map(Late, q), *do, *map(Late, lse), *delta, *map(Late, far)]
    return call(body, outs, scalars, blocks, (), staged(size, width), us=12)


def attend_near_back(scalars, q, do, lse, delta, near, dq_before):
    size, width = q[0].shape
    rows = size * CHUNKS

    def body(scal, q0, q1, o0, o1, l0, l1, d0, d1, n_all, before, dq_out, crossing, *held):
        dq_out[...] = before[...]

        @pl.when(scal[0] == 1)
        def _():
            stage(size, (q0, q1, o0, o1, l0, l1, d0, d1), held)
            back_over(held, width, size, [(n_all, crossing, 0)], dq_out)

        @pl.when(scal[0] == 0)
        def _():
            crossing[...] = jnp.zeros_like(crossing)

    outs = [((rows, width), F32), ((rows, 2 * width), BF)]
    blocks = [*map(Late, q), *do, *map(Late, lse), *delta, Late(near), dq_before]
    return call(body, outs, scalars, blocks, (), staged(size, width), us=0.2)


def attend_own_back(scalars, q, do, lse, delta, kv, dq_before):
    size, width = q[0].shape
    rows = size * CHUNKS

    def body(scal, q0, q1, o0, o1, l0, l1, d0, d1, k_all, before, dq0, dq1, dk0, dk1, *held):
        stage(size, (q0, q1, o0, o1, l0, l1, d0, d1), held)
        qs, dos, lses, deltas = held
        key = lax.broadcasted_iota(jnp.int32, (size, rows), 0)
        query = lax.broadcasted_iota(jnp.int32, (size, rows), 1)
        causal = key <= query
        for p in range(width // 128):
            ks, vs = spans(p, width)
            k0, k1 = halves_of(k_all, size)
            first, dk, dv = back_tile(p, width, qs[:, ks], dos[:, ks], lses, deltas, k0, causal)
            dk0[:, ks] = dk
            dk0[:, vs] = dv
            late = [ref.at[:, size:rows] for ref in (lses, deltas)]
            second, dk, dv = back_tile(p, width, qs[size:, ks], dos[size:, ks], *late, k1, causal[:, :size])
            dk1[:, ks] = dk
            dk1[:, vs] = dv
            first, second = jnp.transpose(first[:, :size]), jnp.transpose(first[:, size:] + second)
            dq0[:, ks] = ((before[:size, ks] + first) * 0.125).astype(BF)
            dq1[:, ks] = ((before[size:, ks] + second) * 0.125).astype(BF)

    outs = [((size, width), BF)] * 2 + [((size, 2 * width), F32)] * 2
    blocks = [*map(Late, q), *do, *map(Late, lse), *delta, Late(kv), dq_before]
    return call(body, outs, scalars, blocks, (), staged(size, width), us=0.2)


def feed_forward(scalars, layer, table, x, mine, came, up, down):
    rows, features = x.shape
    inner = up[0].shape[1]

    def body(scal, tab, x_ref, mine_ref, came_ref, u_own, u_got, u_other, d_own, d_got, d_other,
             hidden, mlp_in, active, slope, part, up_held, down_held, up_sem, down_sem):
        fetch_start(scal, layer, u_own, u_got, u_other, up_held, up_sem)
        fetch_start(scal, layer, d_own, d_got, d_other, down_held, down_sem)
        h = x_ref[...].astype(F32) + (mine_ref[...].astype(F32) + came_ref[...].astype(F32)) + tab[BO : BO + 1]
        hidden[...] = h
        unit, _ = norm_parts(h)
        low = (unit * tab[GAIN1 : GAIN1 + 1] + tab[BIAS1 : BIAS1 + 1]).astype(BF)
        mlp_in[...] = low
        flush(hidden, mlp_in)
        fetch_wait(u_own, up_held, up_sem)
        for j in range(inner // features):
            cols = slice(j * features, (j + 1) * features)
            value, grad = gelu_both(dot_nn(low, up_held[:, cols]) + tab[BUP + j : BUP + j + 1])
            active[:, cols] = value.astype(BF)
            slope[:, cols] = grad.astype(BF)
        flush(active, slope)
        fetch_wait(d_own, down_held, down_sem)
        part[...] = dot_nn(active[...], down_held[...]).astype(BF)

    outs = [((rows, features), F32, LATER), ((rows, features), BF, LATER), ((rows, inner), BF, LATER), ((rows, inner), BF, LATER), ((rows, features), BF)]
    return call(body, outs, scalars, [table, Late(x), mine, came], [*up, *down], held_like(up, down), us=4)


def feed_back(scalars, layer, dy, slope, up, down):
    rows, features = dy.shape
    inner = up[0].shape[1]

    def body(scal, dy_ref, slope_ref, u_own, u_got, u_other, d_own, d_got, d_other,
             d_up, part, sums, up_held, down_held, up_sem, down_sem):
        fetch_start(scal, layer, d_own, d_got, d_other, down_held, down_sem)
        fetch_start(scal, layer, u_own, u_got, u_other, up_held, up_sem)
        sums[...] = jnp.zeros_like(sums)
        fetch_wait(d_own, down_held, down_sem)
        for j in range(inner // features):
            cols = slice(j * features, (j + 1) * features)
            grad = (dot_nt(dy_ref[...], down_held[cols, :]) * slope_ref[:, cols].astype(F32)).astype(BF)
            d_up[:, cols] = grad
            sums[j : j + 1, :] = jnp.sum(grad.astype(F32), axis=0, keepdims=True)
        fetch_wait(u_own, up_held, up_sem)
        part[...] = dot_nt(d_up[...], up_held[...]).astype(BF)

    outs = [((rows, inner), BF), ((rows, features), BF), ((8, features), F32)]
    return call(body, outs, scalars, [dy, Late(slope)], [*up, *down], held_like(up, down), us=1.0)


def feed_both(scalars, layer, table, x, mine, came, dy, up, down):
    rows, features = x.shape
    inner = up[0].shape[1]

    def body(scal, tab, x_ref, mine_ref, came_ref, dy_ref, u_own, u_got, u_other, d_own, d_got, d_other,
             hidden, mlp_in, active, result, d_up, part, sums, up_held, down_held, up_sem, down_sem):
        fetch_start(scal, layer, u_own, u_got, u_other, up_held, up_sem)
        fetch_start(scal, layer, d_own, d_got, d_other, down_held, down_sem)
        h = x_ref[...].astype(F32) + (mine_ref[...].astype(F32) + came_ref[...].astype(F32)) + tab[BO : BO + 1]
        hidden[...] = h
        unit, _ = norm_parts(h)
        low = (unit * tab[GAIN1 : GAIN1 + 1] + tab[BIAS1 : BIAS1 + 1]).astype(BF)
        mlp_in[...] = low
        flush(hidden, mlp_in)
        sums[...] = jnp.zeros_like(sums)
        fetch_wait(u_own, up_held, up_sem)
        fetch_wait(d_own, down_held, down_sem)
        for j in range(inner // features):
            cols = slice(j * features, (j + 1) * features)
            value, slope = gelu_both(dot_nn(low, up_held[:, cols]) + tab[BUP + j : BUP + j + 1])
            active[:, cols] = value.astype(BF)
            grad = (dot_nt(dy_ref[...], down_held[cols, :]) * slope).astype(BF)
            d_up[:, cols] = grad
            sums[j : j + 1, :] = jnp.sum(grad.astype(F32), axis=0, keepdims=True)
        flush(active)
        part[...] = dot_nt(d_up[...], up_held[...]).astype(BF)
        result[...] = dot_nn(active[...], down_held[...]).astype(BF)

    outs = [
        ((rows, features), F32, LATER), ((rows, features), BF, LATER), ((rows, inner), BF, LATER), ((rows, features), BF, LATER),
        ((rows, inner), BF), ((rows, features), BF), ((8, features), F32),
    ]
    return call(body, outs, scalars, [table, Late(x), mine, came, dy], [*up, *down], held_like(up, down), us=1.0)


def middle_back(scalars, layer, table, hidden, parts, dy, attended, weights):
    rows, features = hidden[0].shape
    width = attended[0].shape[1]

    def body(scal, tab, *refs):
        given, (own, got, other) = refs[: 5 * CHUNKS], refs[5 * CHUNKS : 5 * CHUNKS + 3]
        outs = refs[5 * CHUNKS + 3 : 9 * CHUNKS + 4]
        stats, held, sem = refs[9 * CHUNKS + 4 :]
        fetch_start(scal, layer, own, got, other, held, sem)
        sums = outs[-1]
        sums[...] = jnp.zeros_like(sums)
        stats[...] = jnp.zeros_like(stats)
        lows = []
        for c in range(CHUNKS):
            hid, mine, came, dy_ref, att = given[5 * c : 5 * c + 5]
            dh_ref, low_ref, da_ref, delta = outs[4 * c : 4 * c + 4]
            grad = mine[...].astype(F32) + came[...].astype(F32)
            back, d_gain, d_bias = norm_grad(hid[...], tab[GAIN1 : GAIN1 + 1], grad)
            up = dy_ref[...].astype(F32)
            dh = up + back
            dh_ref[...] = dh
            low = dh.astype(BF)
            low_ref[...] = low
            flush(dh_ref, low_ref)
            added = (d_gain, d_bias, jnp.sum(dh, axis=0, keepdims=True), jnp.sum(up, axis=0, keepdims=True))
            for k, value in enumerate(added):
                sums[k : k + 1, :] += value
            lows.append(low)
        fetch_wait(own, held, sem)
        for c in range(CHUNKS):
            att = given[5 * c + 4]
            da_ref, delta = outs[4 * c + 2 : 4 * c + 4]
            da = dot_nt(lows[c], held[...]).astype(BF)
            da_ref[...] = da
            for p in range(width // 128):
                span = slice(p * 128, (p + 1) * 128)
                product = da[:, span].astype(F32) * att[:, span].astype(F32)
                first = low_lanes(product.shape)
                stats[:, 2 * p : 2 * p + 1] = jnp.sum(jnp.where(first, product, 0.0), axis=1, keepdims=True)
                stats[:, 2 * p + 1 : 2 * p + 2] = jnp.sum(jnp.where(first, 0.0, product), axis=1, keepdims=True)
            delta[...] = jnp.transpose(stats[...])[0:8, :]

    one = [((rows, features), F32, LATER), ((rows, features), BF, LATER), ((rows, width), BF), ((8, rows), F32)]
    scratch = [pltpu.VMEM((rows, 128), F32)] + held_like(weights)
    blocks = [table]
    for c in range(CHUNKS):
        blocks += [Late(hidden[c]), *parts[c], dy[c], Late(attended[c])]
    r = call(body, one * CHUNKS + [((8, features), F32)], scalars, blocks, weights, scratch, us=2.8)
    return [list(r[k : 4 * CHUNKS : 4]) for k in range(4)] + [r[-1]]


def project_back(scalars, layer, c, dq, dkv, near, far, returned, weights):
    rows, width = dq.shape
    features = weights[0].shape[0]

    def body(scal, dq_ref, dkv_ref, near_ref, far_ref, *rest):
        back_ref = rest[0] if returned is not None else None
        outs = rest[-6:-2] if returned is None else rest[-5:-2]
        own, *parts = rest[-11:-6] if returned is None else rest[-10:-5]
        held, sem = rest[-2:]
        fetch_parts(scal, layer, own, parts[:2], parts[2:], held, sem)
        at = slice(c * rows, (c + 1) * rows)
        total = dkv_ref[...] + near_ref[at, :].astype(F32) + far_ref[at, :].astype(F32)
        if returned is None:
            outs[3][...] = total
        else:
            rolled = pltpu.roll(back_ref[...], 2 * width - width // 2, 1)
            lane = lax.broadcasted_iota(jnp.int32, total.shape, 1)
            total = total + jnp.where((lane >= width) & (lane < width + width // 2), rolled, 0.0)
        low = total.astype(BF)
        outs[0][...] = low
        sums = outs[2]
        sums[...] = jnp.zeros_like(sums)
        sums[0:1, :width] = jnp.sum(dq_ref[...].astype(F32), axis=0, keepdims=True)
        sums[1:2, :] = jnp.sum(low.astype(F32), axis=0, keepdims=True)
        fetch_wait(own, held, sem)
        outs[1][...] = (dot_nt(dq_ref[...], held[:, :width]) + dot_nt(low, held[:, width:])).astype(BF)

    outs = [((rows, 2 * width), BF), ((rows, features), BF), ((8, features), F32)]
    blocks = [dq, dkv, near, far]
    if returned is None:
        outs.append(((rows, 2 * width), F32, LATER))
    else:
        blocks.append(Late(returned))
    return call(body, outs, scalars, blocks, weights, held_like(weights), us=2.7)


def last_back(scalars, table, x, parts, dh):
    rows, features = x[0].shape

    def body(scal, tab, *refs):
        given, outs = refs[: 4 * CHUNKS], refs[4 * CHUNKS :]
        sums = outs[-1]
        sums[...] = jnp.zeros_like(sums)
        for c in range(CHUNKS):
            x_ref, mine, came, dh_ref = given[4 * c : 4 * c + 4]
            dx_ref, low_ref = outs[2 * c : 2 * c + 2]
            grad = mine[...].astype(F32) + came[...].astype(F32)
            back, d_gain, d_bias = norm_grad(x_ref[...].astype(F32), tab[GAIN0 : GAIN0 + 1], grad)
            dx = dh_ref[...] + back
            dx_ref[...] = dx
            flush(dx_ref)
            low_ref[...] = dx.astype(BF)
            sums[0:1, :] += d_gain
            sums[1:2, :] += d_bias

    outs = [((rows, features), F32, LATER), ((rows, features), BF)] * CHUNKS + [((8, features), F32)]
    blocks = [table]
    for c in range(CHUNKS):
        blocks += [Late(x[c]), *parts[c], Late(dh[c])]
    r = call(body, outs, scalars, blocks, us=0.5)
    return list(r[0 : 2 * CHUNKS : 2]), list(r[1 : 2 * CHUNKS : 2]), r[-1]


def both_chunks(left, left_span, right, right_span):
    total = None
    for a, b in zip(left, right):
        d = dot_tn(a[:, left_span], b[:, right_span])
        total = d if total is None else total + d
    return total


def hand_out(scal, packed, send, mine, sem):
    copies = [
        pltpu.make_async_copy(packed.at[pl.ds(2 * (1 - scal[3]), 2)], send, sem.at[0]),
        pltpu.make_async_copy(packed.at[pl.ds(2 * scal[3], 2)], mine, sem.at[1]),
    ]
    for copy in copies:
        copy.start()
    for copy in copies:
        copy.wait()


def wide_grads(scalars, active, dy, mlp_in, d_up):
    features = dy[0].shape[1]
    inner = active[0].shape[1]
    a, half = inner // 4, features // 2
    size = a + half

    def body(scal, a0, a1, y0, y1, m0, m1, u0, u1, send, mine, packed, sem):
        for k in range(4):
            span = slice(k * a, (k + 1) * a)
            packed[k, :a, :] = both_chunks((a0, a1), span, (y0, y1), slice(None)).astype(BF)
            for i in range(2):
                part = both_chunks((m0, m1), slice(i * half, (i + 1) * half), (u0, u1), span)
                packed[k, a:, i * a : (i + 1) * a] = part.astype(BF)
        hand_out(scal, packed, send, mine, sem)

    blocks = [*map(Late, active), *dy, *map(Late, mlp_in), *d_up]
    outs = [((2, size, features), BF, RAW)] * 2
    scratch = [pltpu.VMEM((4, size, features), BF), pltpu.SemaphoreType.DMA((2,))]
    return call(body, outs, scalars, blocks, (), scratch, us=3.7)


def narrow_grads(scalars, normed, dq, dkv, attended, dh_low):
    features = normed[0].shape[1]
    width = dq[0].shape[1]
    rows = features // 4
    half, c = rows // 2, width // 4
    size = rows + half + c

    def body(scal, n0, n1, q0, q1, k0, k1, t0, t1, h0, h1, send, mine, packed, sem):
        every = slice(None)
        for x in range(2):
            span = slice(2 * x * rows, 2 * (x + 1) * rows)
            first = both_chunks((n0, n1), span, (q0, q1), every).astype(BF)
            second = both_chunks((n0, n1), span, (k0, k1), every).astype(BF)
            for core in range(2):
                k, at = 2 * core + x, core * rows
                packed[k, :rows, :width] = first[at : at + rows, :]
                packed[k, :rows, width:] = second[at : at + rows, :width]
                packed[k, rows : rows + half, :width] = second[at : at + half, width:]
                packed[k, rows : rows + half, width:] = second[at + half : at + rows, width:]
        out = both_chunks((t0, t1), every, (h0, h1), every).astype(BF)
        for k in range(4):
            packed[k, rows + half :, :] = out[k * c : (k + 1) * c, :]
        hand_out(scal, packed, send, mine, sem)

    blocks = [*map(Late, normed), *dq, *dkv, *map(Late, attended), *map(Late, dh_low)]
    outs = [((2, size, features), BF, RAW)] * 2
    scratch = [pltpu.VMEM((4, size, features), BF), pltpu.SemaphoreType.DMA((2,))]
    return call(body, outs, scalars, blocks, (), scratch, us=2.1)


def collect(scal, parts, held, sem):
    copies = []
    for i, refs in enumerate(parts):
        core = scal[3] if i < 2 else 1 - scal[3]
        section = scal[2] if i % 2 == 0 else 1 - scal[2]
        size = held.shape[1] // len(refs)
        for j, ref in enumerate(refs):
            place = held.at[2 * core + section, j * size : (j + 1) * size]
            copies.append(pltpu.make_async_copy(ref, place, sem.at[len(copies)]))
    for copy in copies:
        copy.start()
    for copy in copies:
        copy.wait()


def wide_unpack(scalars, mine, mine2, other, other2, inner):
    size, features = mine.shape
    a, half = inner // 4, features // 2

    def body(scal, p0, p1a, p1b, p2, p3a, p3b, down, up, token, held, sem):
        collect(scal, ((p0,), (p1a, p1b), (p2,), (p3a, p3b)), held, sem)
        for k in range(4):
            down[k * a : (k + 1) * a, :] = held[k, :a, :].astype(F32)
            for i in range(2):
                up[i * half : (i + 1) * half, k * a : (k + 1) * a] = held[k, a:, i * a : (i + 1) * a].astype(F32)
        token[...] = jnp.zeros_like(token)

    outs = [((inner, features), F32), ((features, inner), F32), ((8, 128), F32)]
    scratch = [pltpu.VMEM((4, size, features), BF), pltpu.SemaphoreType.DMA((6,))]
    return call(body, outs, scalars, [], [mine, *other, mine2, *other2], scratch, us=5)


def narrow_unpack(scalars, parts, extras, width, token):
    size, features = parts[0].shape
    rows = features // 4
    half, c, own = rows // 2, width // 4, width // 2

    def body(scal, _, p0, p1, p2, p3, e0, e1, pairs, value, extra, out, held, pair, sem, pair_sem):
        last = [pltpu.make_async_copy(e, pair.at[i if i == 0 else 1], pair_sem.at[i]) for i, e in enumerate((e0, e1))]
        for copy in last:
            copy.start()
        collect(scal, ((p0,), (p1,), (p2,), (p3,)), held, sem)
        for copy in last:
            copy.wait()
        for x in range(2):
            for core in range(2):
                k, at = 2 * core + x, (2 * x + core) * rows
                pairs[at : at + rows, 0, :] = held[k, :rows, :width].astype(F32)
                pairs[at : at + rows, 1, :] = held[k, :rows, width:].astype(F32)
                value[at : at + half, :] = held[k, rows : rows + half, :own].astype(F32)
                value[at + half : at + rows, :] = held[k, rows : rows + half, width : width + own].astype(F32)
        for k in range(4):
            out[k * c : (k + 1) * c, :] = held[k, rows + half :, :].astype(F32)
        for i in range(2):
            core = scal[3] if i == 0 else 1 - scal[3]
            at = pl.multiple_of(core * rows, rows)
            cut = pair[i].astype(F32)
            left = pltpu.roll(cut[:, :width], own, 1)
            right = pltpu.roll(cut[:, width:], own, 1)
            extra[pl.ds(at, half), :] = left[:, :own]
            extra[pl.ds(pl.multiple_of(at + half, 8), half), :] = right[:, :own]

    outs = [((features, 2, width), F32)] + [((features, own), F32), ((2 * rows, own), F32), ((width, features), F32)]
    scratch = [
        pltpu.VMEM((4, size, features), BF), pltpu.VMEM((2, half, features), BF),
        pltpu.SemaphoreType.DMA((4,)), pltpu.SemaphoreType.DMA((2,)),
    ]
    return call(body, outs, scalars, [token], list(parts) + list(extras), scratch, us=3)


def swap(value, axis, bits=1):
    count = lax.axis_size(axis)
    return lax.ppermute(value, axis, [(i, i ^ bits) for i in range(count)])


def shift(value, steps):
    count = lax.axis_size("batch")
    first, last = max(0, -steps), min(count, count - steps)
    return lax.ppermute(value, "batch", [(i, i + steps) for i in range(first, last)])


def after(value, *earlier):
    return lax.optimization_barrier((value,) + earlier)[0]


def take(array, index, axis=0):
    return lax.dynamic_index_in_dim(array, index, axis, keepdims=False)


def paired(mine, other, side):
    return jnp.where(side == 0, mine, other), jnp.where(side == 0, other, mine)


class Reduction:
    def __init__(self, grads, pieces):
        self.section = lax.axis_index("section")
        self.send, self.mine = grads
        self.pieces = pieces

    def over_cores(self):
        self.near = swap(self.send, "batch")

    def pair_sum(self, section, start, size):
        cut = [lax.dynamic_slice(a, (section, start, 0), (1, size, a.shape[2]))[0] for a in (self.mine, self.near)]
        return cut[0].astype(F32) + cut[1].astype(F32)

    def prepare(self):
        size = self.mine.shape[1] // self.pieces
        self.sent = [self.pair_sum(1 - self.section, i * size, size).astype(BF) for i in range(self.pieces)]

    def over_sections(self, i=0):
        if i == 0:
            self.came = []
        self.came.append(swap(self.sent[i], "section"))

    def scatter_send(self):
        index = lax.axis_index("batch")
        half = self.mine.shape[1] // 2
        came = self.came if self.pieces == 2 else [self.came[0][:half], self.came[0][half:]]
        cut = [(self.pair_sum(self.section, i * half, half) + came[i].astype(F32)).astype(BF) for i in range(2)]
        *first, near, far = chip_bits()
        for bit in first:
            keep, send = paired(*cut, (index >> bit) & 1)
            total = (keep.astype(F32) + swap(send, "batch", 1 << bit).astype(F32)).astype(BF)
            cut = jnp.split(total, 2, axis=0)
        self.keep, send = paired(*cut, (index >> near) & 1)
        return send

    def exchange_send(self, got):
        self.part = (self.keep.astype(F32) + got.astype(F32)).astype(BF)
        return self.part

    def gather_send(self, got):
        self.part = (self.part.astype(F32) + got.astype(F32)).astype(BF)
        return self.part

    def finish(self, got):
        index = lax.axis_index("batch")
        *first, near, far = chip_bits()
        part = jnp.concatenate(paired(self.part, got, (index >> near) & 1), axis=0)
        for bit in reversed(first):
            part = jnp.concatenate(paired(part, swap(part, "batch", 1 << bit), (index >> bit) & 1), axis=0)
        self.quarter = part


def chip_bits():
    return list(range(1, lax.axis_size("batch").bit_length() - 1))


def swap_all(values, place):
    sizes = [v.shape[0] for v in values]
    got = swap(jnp.concatenate(values, axis=0) if len(values) > 1 else values[0], "batch", 1 << chip_bits()[place])
    ends = [sum(sizes[: i + 1]) for i in range(len(sizes))]
    return [got[end - size : end] for size, end in zip(sizes, ends)]


def tie(value, *others):
    return lax.optimization_barrier((value,) + others)


def forward_layer(scalars, layer, table, w, x=None, ahead=None, carried=None, hooks=None):
    hooks = hooks or {}
    nothing = lambda value: value
    x, normed, q, kv = project(scalars, layer, w["qkv"], table, x=x, ahead=ahead, carried=carried)
    if "projected" in hooks:
        kv = hooks["projected"](kv, q)
    far = shift(kv, 2)
    near = swap(kv, "batch")
    out, amount, tops = attend_local(scalars, q, kv, near)
    far = hooks.get("arrived", nothing)(after(far, out))
    far = [far, swap(far, "batch")]
    att, lse, parts, came = [], [], [], []
    for c in range(CHUNKS):
        a, l, part = attend_far(scalars, layer, c, q[c], far, out, amount, tops, w["out"])
        att.append(a)
        lse.append(l)
        parts.append(part)
        came.append(swap(part, "tensor"))
    came = hooks.get("far", nothing)(came)
    hidden, mlp_in, active, slope, results = [], [], [], [], []
    for c in range(CHUNKS if layer == 0 else 0):
        h, m, a, s, part = feed_forward(scalars, layer, table, x[c], parts[c], came[c], w["up"], w["down"])
        hidden.append(h)
        mlp_in.append(m)
        active.append(a)
        slope.append(s)
        results.append((table, h, part))
    kept = dict(x=x, normed=normed, q=q, kv=kv, near=near, far=far, att=att, lse=lse, hidden=hidden,
                mlp_in=mlp_in, active=active, slope=slope, attention=(parts, came), results=results)
    return results, kept


def backward_layer(scalars, layer, table, w, kept, dy, returned, steps):
    rows = CHUNKS * dy[0].shape[0]
    dy = list(steps("start", dy))
    d_up, parts, up_sums = [], [], []
    for c in range(CHUNKS):
        if c == 1:
            dy[1] = steps("half", after(dy[1], parts[0][0]))
        if layer == 0:
            grad, part, sums = feed_back(scalars, layer, dy[c], kept["slope"][c], w["up"], w["down"])
        else:
            mine, came = [a[c] for a in kept["attention"]]
            h, m, a, y, grad, part, sums = feed_both(scalars, layer, table, kept["x"][c], mine, came, dy[c], w["up"], w["down"])
            kept["hidden"].append(h)
            kept["mlp_in"].append(m)
            kept["active"].append(a)
            kept["results"].append((table, h, y))
        d_up.append(grad)
        up_sums.append(sums)
        parts.append((part, swap(part, "tensor")))
    wide = Reduction(wide_grads(scalars, kept["active"], dy, kept["mlp_in"], d_up), 1)
    parts = steps("fed", parts, wide)
    dh, dh_low, d_att, delta, mid = middle_back(
        scalars, layer, table, kept["hidden"], parts, dy, kept["att"], w["out"]
    )
    d_att = steps("mid", d_att, wide)
    dq, mine, others = attend_far_back(scalars, kept["q"], d_att, kept["lse"], delta, kept["far"])
    total = (mine.astype(F32) + swap(others, "batch").astype(F32)).astype(BF)
    dq = steps("turn", after(dq, total), wide)
    home = shift(total, -2)
    dq, crossing = attend_near_back(scalars, kept["q"], d_att, kept["lse"], delta, kept["near"], dq)
    near = swap(crossing, "batch")
    dq = steps("between", dq, wide)
    dq0, dq1, dk0, dk1 = attend_own_back(scalars, kept["q"], d_att, kept["lse"], delta, kept["kv"], dq)
    dq, dkv = [dq0, dq1], [dk0, dk1]
    home, dq = steps("near", (home, dq), wide)
    dkv_low, parts, in_sums, back = [], [], [], []
    for c in range(CHUNKS):
        again = None if returned is None else returned[c]
        r = project_back(scalars, layer, c, dq[c], dkv[c], near, home, again, w["qkv"])
        dkv_low.append(r[0])
        parts.append((r[1], swap(r[1], "tensor")))
        in_sums.append(r[2])
        back.extend(r[3:])
    narrow = Reduction(narrow_grads(scalars, kept["normed"], dq, dkv_low, kept["att"], dh_low), 1)
    parts = steps("proj", parts, wide, narrow)
    parts = steps("last", parts, wide, narrow)
    dx, dx_low, last = last_back(scalars, table, kept["x"], parts, dh)
    up, inn = [a + b for a, b in (up_sums, in_sums)]
    blank = jnp.zeros((TABLE - BUP - 2, up.shape[1]), F32)
    small = jnp.concatenate(
        [last[0:1], mid[0:1], last[1:2], mid[1:2], mid[2:4], inn[0:2], up[0:2], blank], axis=0
    )
    return dx, dx_low, back, wide, narrow, small


def local(
    tokens, block_place, cotangent, norm_gains, norm_biases, query_key, query_bias, value_own, value_bias,
    value_extra, out_weight, out_bias, up_weight, up_bias, down_weight, down_bias,
):
    section = lax.axis_index("section")
    tensor = lax.axis_index("tensor")
    core = lax.axis_index("batch") % 2
    micros, _, half_rows, features = tokens.shape
    width = query_bias.shape[1]
    own_width = value_own.shape[2]
    inner = up_weight.shape[2]
    assert micros == 2 and lax.axis_size("section") == 2 and lax.axis_size("tensor") == 2
    assert 2 * own_width == width and 2 * width == features and inner == 2 * features

    place = take(block_place, section)[0]
    scalars = jnp.stack([place & 1, place >> 1, section, core]).astype(jnp.int32)

    my_tokens = take(tokens, section)[0]
    x = paired(my_tokens, swap(my_tokens, "tensor"), tensor)

    def row(*pieces):
        flat = jnp.concatenate([p.reshape(-1) for p in pieces])
        return jnp.pad(flat, (0, features - flat.shape[0]))[None]

    blank = jnp.zeros((width,), F32)
    own_table = jnp.concatenate(
        [norm_gains[0], norm_biases[0], out_bias, down_bias, row(query_bias[0]), row(blank, value_bias[0]),
         up_bias[0].reshape(2, features), jnp.zeros((TABLE - BUP - 2, features), F32)], axis=0
    )
    def half_of(weight):
        return take(weight.reshape((2, weight.shape[0] // 2) + weight.shape[1:]), core)

    query_keys = query_key[0].reshape(features, 2 * width)
    extra = jnp.where(section == 0, value_extra, jnp.zeros_like(value_extra))
    halves = [half_of(query_keys), half_of(value_own[0])]
    other_extra = half_of(jnp.where(section == 1, value_extra, jnp.zeros_like(value_extra)))
    qkv = jnp.concatenate([query_keys, value_own[0], extra], axis=1)
    qkv_got = [swap(h, "section") for h in halves]
    qkv_got[1] = jnp.concatenate([qkv_got[1], other_extra], axis=1)
    other_table = swap(own_table, "section")
    out_got = swap(half_of(out_weight[0]), "section")
    up_got = swap(after(half_of(up_weight[0]), x[0]), "section")
    down_got = swap(after(half_of(down_weight[0]), x[0]), "section")
    tables = paired(own_table, other_table, section)
    qkv_got[0], qkv_got[1], out_got, qkv, scalars, *rest = tie(*qkv_got, out_got, qkv, scalars, *tables, *x)
    tables, x = rest[:2], rest[2:]
    w = dict(qkv=(qkv, *qkv_got, *[swap(g, "batch") for g in qkv_got]))
    late = dict(up=up_got, down=down_got)

    def on_projected(kv, q):
        mine, kv = tie(take(cotangent, section)[0], kv)
        late["dy"] = mine, swap(mine, "tensor")
        w["out"] = (out_weight[0], out_got, swap(after(out_got, kv), "batch"))
        return kv

    def on_arrived(far):
        mine, other = late["dy"]
        far, got, other = tie(far, late["up"], other)
        late["dy"] = paired(mine, other, tensor)
        w["up"] = (up_weight[0], got, swap(got, "batch"))
        return far

    def on_far(came):
        *came, got = tie(*came, late["down"])
        w["down"] = (down_weight[0], got, swap(got, "batch"))
        return came

    first, kept0 = forward_layer(
        scalars, 0, tables[0], w, x=x, hooks=dict(projected=on_projected, arrived=on_arrived, far=on_far)
    )
    first = [r + (swap(r[2], "tensor"),) for r in first]
    _, kept1 = forward_layer(scalars, 1, tables[1], w, ahead=first, carried=kept0["kv"])
    y0 = kept1["x"]

    def my_half(chunks):
        return jnp.where(tensor == 0, chunks[0], chunks[1])

    def by_section(mine0, mine1, kind):
        mine = jnp.where(section == 0, mine0, mine1)
        other = swap(jnp.where(section == 0, mine1, mine0).astype(kind), "section")
        return mine, other

    def steps1(number, values, wide=None, narrow=None):
        leaves, tree = jax.tree.flatten(values)
        if number == "fed":
            *leaves, wide.send = tie(*leaves, wide.send)
            wide.over_cores()
        if number == "mid":
            *leaves, wide.near = tie(*leaves, wide.near)
            wide.prepare()
            *leaves, wide.sent[0] = tie(*leaves, *wide.sent)
            wide.over_sections(0)
        if number == "near":
            *leaves, wide.came[0] = tie(*leaves, wide.came[0])
            late["a1"] = swap_all([wide.scatter_send()], -2)[0]
        if number == "proj":
            *leaves, narrow.send, got = tie(*leaves, narrow.send, late["a1"])
            narrow.over_cores()
            sent = wide.exchange_send(got)
            *leaves, sent = tie(*leaves, sent)
            late["b1"] = swap_all([sent], -1)[0]
        if number == "last":
            *leaves, narrow.near = tie(*leaves, narrow.near)
            narrow.prepare()
            *leaves, narrow.sent[0] = tie(*leaves, narrow.sent[0])
            narrow.over_sections()
        return jax.tree.unflatten(tree, leaves)

    dx1, dx1_low, back, wide1, narrow1, small1 = backward_layer(scalars, 1, tables[1], w, kept1, late["dy"], None, steps1)

    def steps0(number, values, wide=None, narrow=None):
        leaves, tree = jax.tree.flatten(values)
        if number == "half":
            *leaves, narrow1.came[0], got = tie(*leaves, narrow1.came[0], late["b1"])
            sent = [wide1.gather_send(got), narrow1.scatter_send()]
            *leaves, sent[0], sent[1] = tie(*leaves, *sent)
            late["c1"] = swap_all(sent, -2)
        if number == "fed":
            *leaves, wide.send, got, narrow_got = tie(*leaves, wide.send, *late["c1"])
            wide.over_cores()
            wide1.finish(got)
            sent = narrow1.exchange_send(narrow_got)
            *leaves, sent = tie(*leaves, sent)
            late["d1"] = swap_all([sent], -1)[0]
        if number == "mid":
            *leaves, wide.near, got = tie(*leaves, wide.near, late["d1"])
            wide.prepare()
            *leaves, wide.sent[0] = tie(*leaves, *wide.sent)
            wide.over_sections(0)
            late["e1"] = narrow1.gather_send(got)
        if number == "near":
            *leaves, wide.came[0] = tie(*leaves, wide.came[0])
            late["a0"] = swap_all([wide.scatter_send(), late["e1"]], -2)
        if number == "proj":
            *leaves, narrow.send, got, narrow_got = tie(*leaves, narrow.send, *late["a0"])
            narrow1.finish(narrow_got)
            narrow.over_cores()
            sent = wide.exchange_send(got)
            *leaves, sent = tie(*leaves, sent)
            late["b0"] = swap_all([sent], -1)[0]
            *leaves, narrow.near = tie(*leaves, narrow.near)
            narrow.prepare()
            *leaves, narrow.sent[0] = tie(*leaves, narrow.sent[0])
            narrow.over_sections()
            late["y1"] = [swap(after(r[2], leaves[0]), "tensor") for r in kept1["results"]]
        if number == "last":
            *leaves, narrow.came[0] = tie(*leaves, narrow.came[0])
        return jax.tree.unflatten(tree, leaves)

    dx0, dx0_low, _, wide0, narrow0, small0 = backward_layer(scalars, 0, tables[0], w, kept0, dx1_low, back, steps0)
    sums = jnp.stack([small0, small1])
    sums = sums + swap(sums, "batch")
    got, sums, *rest = tie(late["b0"], sums, *late["y1"], my_half(dx0), my_half(dx1))
    y_came, grads = rest[:2], rest[2:]
    sent = [narrow0.scatter_send(), wide0.gather_send(got)]
    sent[0], sent[1], sums, grads[0], grads[1] = tie(*sent, sums, *grads)
    late["c0"] = swap_all(sent, -2)
    table = take(sums, section) + swap(take(sums, 1 - section), "section")
    mine_grads, other_grads = by_section(*grads, BF)
    y1 = my_half(
        [(r[1] + r[0][BDOWN : BDOWN + 1] + r[2].astype(F32) + c.astype(F32)).astype(BF) for r, c in zip(kept1["results"], y_came)]
    )
    mine_out, other_out = by_section(my_half(y0), y1, BF)

    narrow0_got, wide0_got, table, other_grads, other_out = tie(
        *late["c0"], table, other_grads, other_out
    )
    sent = narrow0.exchange_send(narrow0_got)
    wide0.finish(wide0_got)
    wide_mine = jnp.where(section == 0, wide0.quarter, wide1.quarter)
    wide_sent = jnp.split(jnp.where(section == 0, wide1.quarter, wide0.quarter), 2, axis=0)
    sent, wide_sent[0] = tie(sent, wide_sent[0])
    got = swap_all([sent], -1)[0]
    wide_other = [swap(wide_sent[0], "section")]
    for bit in chip_bits()[:-1]:
        table = table + swap(table, "batch", 1 << bit)

    got, table, wide_other[0], wide_sent[1] = tie(got, table, wide_other[0], wide_sent[1])
    sent = narrow0.gather_send(got)
    got = swap_all([sent], -2)[0]
    wide_mine2, wide_other2 = swap(wide_mine, "batch"), swap(wide_other[0], "batch")
    table = table + swap(table, "batch", 1 << chip_bits()[-1])
    wide_other.append(swap(wide_sent[1], "section"))

    got, wide_other[1], table = tie(got, wide_other[1], table)
    narrow0.finish(got)
    outputs = jnp.stack(paired(mine_out, other_out, section))
    input_grads = jnp.stack(paired(mine_grads.astype(F32), other_grads.astype(F32), section))

    def gathered(first, second):
        mine = jnp.where(section == 0, first, second)
        other = swap(jnp.where(section == 0, second, first), "section")
        mine2 = swap(mine, "batch")
        other, mine2 = tie(other, mine2, token)[:2]
        return mine, other, mine2, swap(other, "batch")

    d_down, d_up, token = wide_unpack(
        scalars, wide_mine, wide_mine2, wide_other, [wide_other2, swap(wide_other[1], "batch")], inner
    )
    rows = features // 4
    extra = narrow0.quarter[rows : rows + rows // 2]
    extras = (extra, swap(extra, "batch"))
    token, *extras = tie(token, *extras)
    d_qk, d_v, d_extra, d_out = narrow_unpack(
        scalars, gathered(narrow0.quarter, narrow1.quarter), extras, width, token
    )
    return (
        outputs.reshape(1, micros, 1, half_rows, features),
        input_grads.reshape(1, micros, 1, half_rows, features),
        table[GAIN0 : GAIN1 + 1][None],
        table[BIAS0 : BIAS1 + 1][None],
        d_qk.reshape(1, features, 2, width),
        table[BQ : BQ + 1, :width],
        d_v[None],
        table[BKV : BKV + 1, width : width + own_width],
        d_extra,
        d_out[None],
        table[BO : BO + 1],
        d_up[None],
        table[BUP : BUP + 2].reshape(1, inner),
        d_down[None],
        table[BDOWN : BDOWN + 1],
    )


def solution(mesh):
    return jax.shard_map(
        local,
        mesh=mesh,
        in_specs=(
            P(None, "batch", "tensor", None),
            P(None, "batch"),
            P(None, "batch", "tensor", None),
            P("section", None, None),
            P("section", None, None),
            P("section", None, None, "tensor"),
            P("section", "tensor"),
            P("section", None, "tensor"),
            P("section", "tensor"),
            P(None, "tensor"),
            P("section", "tensor", None),
            P("section", None),
            P("section", None, "tensor"),
            P("section", "tensor"),
            P("section", "tensor", None),
            P("section", None),
        ),
        out_specs=(
            P("section", None, "batch", "tensor", None),
            P("section", None, "batch", "tensor", None),
            P("section", None, None),
            P("section", None, None),
            P("section", None, None, "tensor"),
            P("section", "tensor"),
            P("section", None, "tensor"),
            P("section", "tensor"),
            P("section", "tensor"),
            P("section", "tensor", None),
            P("section", None),
            P("section", None, "tensor"),
            P("section", "tensor"),
            P("section", "tensor", None),
            P("section", None),
        ),
        check_vma=False,
    )
```
